128 devices in a mesh: seq: 32 (over x, z, core), val: 4 (over y).
Axes of the slice: x: 4, y: 4, z: 4, core: 2. Of those that a mesh axis runs over, the one named last changes fastest.
Arguments:
- tokens: bfloat16 [12288, 4096], P('seq', 'val'), may hold values from -6 to 6
- w_query: bfloat16 [4096, 2048], P(None, 'val'), may hold values from -0.09375 to 0.09375
- w_key: bfloat16 [4096, 2048], P(None, 'val'), may hold values from -0.09375 to 0.09375
- w_value: bfloat16 [4096, 8, 512], P(None, None, 'val'), may hold values from -0.09375 to 0.09375
- w_gate: bfloat16 [4096, 2, 8], replicated, may hold values from -0.09375 to 0.09375
- gate_bias: float32 [2, 8], replicated, as said below
- norm_gain: float32 [8, 512], P(None, 'val'), may hold values from 0.1 to 1.9
- w_out: bfloat16 [8, 512, 4096], P(None, 'val'), may hold values from -0.09375 to 0.09375
Outputs:
- layer_out: bfloat16 [12288, 4096], P('seq', 'val')
The draws below stay inside these ranges and needn't reach their ends.
Inputs may be any that keep to these rules, and one draw needn't show every extreme that they name: `gate_bias`: row 0 holds input gate biases; row 1 holds forget gate biases, all positive.
All inputs are finite; a program needn't handle non-finite values.
Results may differ from the reference program's by a relative error of at most 0.015.
Values may be sent and summed in bfloat16 or wider, within the bound.
No kernel may reach another device: no remote copies, remote signals or barrier semaphores. Data moves between devices by JAX's collectives and lax.ppermute only.
A program may use at most 128 MiB of HBM per device.

```python
import math
import jax
import jax.numpy as jnp
from jax import lax

D = 4096
H = 8
DQK = 256
DV = 512
TOK_DEV = 384
TOKENS = 12288


def draw_gate_bias(key, part):
    key = jax.random.fold_in(key, 7)
    key_in, key_rate = jax.random.split(key)
    slowest = math.log(math.log(10.0) / TOKENS)
    fastest = math.log(1.0 / 30.0)
    inputs = jax.random.uniform(key_in, (H,), jnp.float32, -3.0, 3.0)
    rates = jnp.exp(jax.random.uniform(key_rate, (H,), jnp.float32, slowest, fastest))
    forget = -jnp.log(rates)
    return jnp.stack([inputs, forget]).astype(jnp.float32)


def steps_of(rng, shape, pieces, smallest, largest):
    gain, own = 1.0, jax.random.fold_in(rng, 6)
    for axis_at, blocks in pieces:
        draws = jnp.exp(jax.random.uniform(jax.random.fold_in(own, axis_at), (blocks,), jnp.float32, smallest / len(pieces), largest / len(pieces)))
        gain = gain * jnp.repeat(draws, shape[axis_at] // blocks).reshape([-1 if axis == axis_at else 1 for axis in range(len(shape))])
    return gain


def normal_values(rng, dims, width, reach, cuts=(), held_as=jnp.bfloat16):
    values = width * jax.random.normal(rng, dims, jnp.float32)
    if cuts:
        values = values * steps_of(rng, dims, cuts, -0.22, 0.18)
    return jnp.clip(values, -reach, reach).astype(held_as)


def setup_inputs(seed: int = 0) -> dict:
    streams_of = jax.random.split(jax.random.key(seed), 9)
    tokens = normal_values(streams_of[0], (TOKENS, D), 1.0, 6.0, ((0, 32), (1, 4)))
    w_query = normal_values(streams_of[1], (D, H * DQK), D ** -0.5, 0.09375, ((1, 4),))
    w_key = normal_values(streams_of[2], (D, H * DQK), D ** -0.5, 0.09375, ((1, 4),))
    w_value = normal_values(streams_of[3], (D, H, DV), D ** -0.5, 0.09375, ((2, 4),))
    w_gate = normal_values(streams_of[4], (D, 2, H), D ** -0.5, 0.09375)
    gate_bias = draw_gate_bias(jax.random.fold_in(streams_of[8], 71), 0)
    norm_gain = jnp.clip(1.0 + 0.18 * jax.random.normal(streams_of[6], (H, DV), jnp.float32), 0.1, 1.9)
    w_out = normal_values(streams_of[7], (H, DV, D), (H * DV) ** -0.5, 0.09375, ((1, 4),))
    return {"tokens": tokens, "w_query": w_query, "w_key": w_key, "w_value": w_value, "w_gate": w_gate, "gate_bias": gate_bias, "norm_gain": norm_gain, "w_out": w_out}


def combine(early, late):
    ce, ne, me, be = early
    cl, nl, ml, bl = late
    top = jnp.maximum(me + bl, ml)
    fe = jnp.exp(me + bl - top)
    fl = jnp.exp(ml - top)
    return (fe[:, None, None] * ce + fl[:, None, None] * cl, fe[:, None] * ne + fl[:, None] * nl, top, be + bl)

def summary(keys, values, igate, cumb):
    total = cumb[-1]
    weight_log = total[None] - cumb + igate
    top = lax.optimization_barrier(jnp.max(weight_log, axis=0))
    wts = jnp.exp(weight_log - top[None])
    kw = (keys.astype(jnp.float32) * wts[:, :, None]).astype(jnp.bfloat16)
    state = jnp.einsum('thd,the->hde', kw.astype(jnp.float32), values.astype(jnp.float32))
    norm = lax.optimization_barrier(jnp.sum(kw.astype(jnp.float32), axis=0))
    return (state, norm, top, total)

def block_output(queries, keys, values, igate, cumb, prefix):
    scale = DQK ** (-0.5)
    rows = queries.shape[0]
    scores = jnp.einsum('thd,shd->hts', queries.astype(jnp.float32), keys.astype(jnp.float32)) * scale
    position = jnp.arange(rows)
    causal = position[:, None] >= position[None, :]
    cumh = cumb.T
    logd = cumh[:, :, None] - cumh[:, None, :] + igate.T[:, None, :]
    logd = jnp.where(causal[None], logd, jnp.float32(-1e+30))
    rowmax = lax.optimization_barrier(jnp.max(logd, axis=-1))
    state, norm, ptop, ptotal = prefix
    top = jnp.maximum(cumh + ptop[:, None], rowmax)
    wts = jnp.where(causal[None], jnp.exp(logd - top[:, :, None]) * scores, 0.0).astype(jnp.bfloat16)
    numer = jnp.einsum('hts,she->the', wts.astype(jnp.float32), values.astype(jnp.float32))
    denom = lax.optimization_barrier(jnp.sum(wts.astype(jnp.float32), axis=-1))
    decay = jnp.exp(cumh + ptop[:, None] - top)
    qf = queries.astype(jnp.float32)
    inter = jnp.einsum('thd,hde->the', qf, state, precision=lax.Precision.HIGHEST)
    numer = numer + inter * (scale * decay.T)[:, :, None]
    denom = denom + jnp.einsum('thd,hd->ht', qf, norm, precision=lax.Precision.HIGHEST) * scale * decay
    return numer / jnp.maximum(jnp.abs(denom), 1.0).T[:, :, None]

def reference(tokens, w_query, w_key, w_value, w_gate, gate_bias, norm_gain, w_out):
    queries = jnp.dot(tokens, w_query, preferred_element_type=jnp.float32).astype(jnp.bfloat16)
    keys = jnp.dot(tokens, w_key, preferred_element_type=jnp.float32).astype(jnp.bfloat16)
    values = jnp.dot(tokens, w_value.reshape(D, H * DV), preferred_element_type=jnp.float32).astype(jnp.bfloat16)
    gates = jnp.dot(tokens, w_gate.reshape(D, 2 * H), preferred_element_type=jnp.float32).reshape(TOKENS, 2, H) + gate_bias[None]
    igate = gates[:, 0]
    logf = jax.nn.log_sigmoid(gates[:, 1])
    blocks = TOKENS // TOK_DEV
    qb = queries.reshape(blocks, TOK_DEV, H, DQK)
    kb = keys.reshape(blocks, TOK_DEV, H, DQK)
    vb = values.reshape(blocks, TOK_DEV, H, DV)
    ib = igate.reshape(blocks, TOK_DEV, H)
    lb = logf.reshape(blocks, TOK_DEV, H)

    def step(prefix, block):
        qq, kk, vv, ig, lf = block
        cumb = jnp.cumsum(lf, axis=0)
        out = block_output(qq, kk, vv, ig, cumb, prefix)
        return (combine(prefix, summary(kk, vv, ig, cumb)), out)
    start = (jnp.zeros((H, DQK, DV), jnp.float32), jnp.zeros((H, DQK), jnp.float32), jnp.full((H,), -1e+30, jnp.float32), jnp.zeros((H,), jnp.float32))
    unused, hidden = lax.scan(step, start, (qb, kb, vb, ib, lb))
    hidden = hidden.reshape(TOKENS, H, DV)
    mean = lax.optimization_barrier(jnp.mean(hidden, axis=-1))
    msq = lax.optimization_barrier(jnp.mean(hidden * hidden, axis=-1))
    normed = ((hidden - mean[..., None]) * lax.rsqrt(msq - mean * mean + 1e-06)[..., None] * norm_gain[None]).astype(jnp.bfloat16)
    return jnp.dot(normed.reshape(TOKENS, H * DV), w_out.reshape(H * DV, D), preferred_element_type=jnp.float32).astype(jnp.bfloat16)
```

```python
import jax
import jax.numpy as jnp
from jax import lax
from jax.sharding import PartitionSpec as P

F32 = jnp.float32
BF16 = jnp.bfloat16


def around(x, distance):
    n = lax.axis_size("val")
    return lax.ppermute(x, "val", [(i, (i + distance) % n) for i in range(n)])


def split3(x):
    hi = lax.reduce_precision(x, 8, 7)
    mid = lax.reduce_precision(x - hi, 8, 7)
    return [hi, mid, x - hi - mid]


def rows_of(w, chunk, size):
    return lax.dynamic_slice_in_dim(w, chunk * size, size, axis=0)


def per_device(tokens, w_query, w_key, w_value, w_gate, gate_bias, norm_gain, w_out):
    me = lax.axis_index("val")
    nval = lax.axis_size("val")
    place = lax.axis_index("seq")
    blocks = lax.axis_size("seq")
    rows, chunk = tokens.shape
    width = w_query.shape[0]
    heads, vlocal = w_value.shape[1:]
    own = heads // nval
    qsize = w_query.shape[1] // own
    vsize = vlocal * nval

    part = heads * vlocal // blocks
    wo = rows_of(w_out.reshape(heads * vlocal, -1), place, part)
    wo = wo.reshape(part, nval, chunk).transpose(1, 0, 2)
    wo = lax.all_to_all(wo, "val", 0, 0)
    wo = lax.all_gather(wo, "seq", axis=0)
    wo = wo.reshape(heads, blocks // heads, nval, part, chunk).transpose(0, 2, 1, 3, 4)
    wo = wo.reshape(heads * vsize, chunk)

    pieces = [tokens, around(tokens, 1), around(tokens, -1), around(tokens, 2)]
    index = [(me + d) % nval for d in (0, nval - 1, 1, 2)]

    wv = w_value.reshape(width, heads * vlocal)
    wg = lax.dynamic_slice_in_dim(w_gate, me * own, own, axis=2).reshape(width, 2 * own)

    def project(w):
        return sum(
            jnp.dot(x, rows_of(w, i, chunk), preferred_element_type=F32)
            for x, i in zip(pieces, index)
        )

    values = project(wv).astype(BF16).reshape(rows, nval, own, vlocal)
    values = lax.all_to_all(values, "val", 1, 0)
    values = values.transpose(1, 2, 0, 3).reshape(rows, own, vsize)
    queries = project(w_query).astype(BF16).reshape(rows, own, qsize)
    keys = project(w_key).astype(BF16).reshape(rows, own, qsize)
    gates = project(wg).reshape(rows, 2, own)
    gates = gates + lax.dynamic_slice_in_dim(gate_bias, me * own, own, axis=1)[None]
    igate = gates[:, 0].T
    logf = jax.nn.log_sigmoid(gates[:, 1]).T
    position = jnp.arange(rows)
    causal = position[:, None] >= position[None, :]
    cumb = jnp.dot(logf, causal.T.astype(F32), precision=lax.Precision.HIGHEST)
    total = cumb[:, -1]

    weight_log = total[:, None] - cumb + igate
    top = jnp.max(weight_log, axis=1)
    wts = jnp.exp(weight_log - top[:, None])
    kw = (keys.astype(F32) * wts.T[:, :, None]).astype(BF16)
    state = jnp.einsum("thd,the->hde", kw, values, preferred_element_type=F32)
    norm = jnp.sum(kw.astype(F32), axis=0)
    extra = [norm[:, :, None]] + [
        jnp.broadcast_to(x[:, None, None], (own, qsize, 1)) for x in split3(top) + split3(total)
    ]
    extra = jnp.concatenate(extra + [jnp.zeros((own, qsize, 128 - len(extra)), F32)], axis=2)
    sent = jnp.concatenate([state.astype(BF16), extra.astype(BF16)], axis=2)
    cut = own * qsize // blocks
    sent = sent.reshape(blocks, cut, vsize + 128)
    got = lax.all_to_all(sent, "seq", 0, 0)

    scale = qsize ** (-0.5)
    scores = jnp.einsum("thd,shd->hts", queries, keys, preferred_element_type=F32) * scale
    logd = cumb[:, :, None] - cumb[:, None, :] + igate[:, None, :]
    logd = jnp.where(causal[None], logd, F32(-1e30))
    rowmax = jnp.max(logd, axis=-1)
    wts = jnp.where(causal[None], jnp.exp(logd - rowmax[:, :, None]) * scores, 0.0).astype(BF16)
    numer = jnp.einsum("hts,she->hte", wts, values, preferred_element_type=F32)
    denom = jnp.sum(wts.astype(F32), axis=-1)

    small = got[:, 0, vsize : vsize + 128].astype(F32)
    tops = small[:, 1] + small[:, 2] + small[:, 3]
    totals = small[:, 4] + small[:, 5] + small[:, 6]
    body = got.astype(F32)
    held = jnp.zeros((cut, vsize + 128), F32)
    ptop = F32(-1e30)
    prefixes, ptops = [], []
    for b in range(blocks):
        prefixes.append(held)
        ptops.append(ptop)
        new = jnp.maximum(ptop + totals[b], tops[b])
        held = jnp.exp(ptop + totals[b] - new) * held + jnp.exp(tops[b] - new) * body[b]
        ptop = new
    lane = jnp.arange(vsize + 128)
    back = []
    for held, ptop in zip(prefixes, ptops):
        for k, x in enumerate(split3(ptop)):
            held = jnp.where(lane == vsize + 1 + k, x, held)
        back.append(held.astype(BF16))
    prefix = lax.all_to_all(jnp.stack(back), "seq", 0, 0)
    prefix = prefix.reshape(own, qsize, vsize + 128)
    ptop = prefix[:, 0, vsize + 1 : vsize + 4].astype(F32).sum(axis=1)
    inter = jnp.einsum("thd,hde->hte", queries, prefix, preferred_element_type=F32)
    top = jnp.maximum(cumb + ptop[:, None], rowmax)
    decay = jnp.exp(cumb + ptop[:, None] - top) * scale
    fade = jnp.exp(rowmax - top)
    numer = numer * fade[:, :, None] + inter[:, :, :vsize] * decay[:, :, None]
    denom = denom * fade + inter[:, :, vsize] * decay
    hidden = numer / jnp.maximum(jnp.abs(denom), 1.0)[:, :, None]
    mean = jnp.mean(hidden, axis=-1)
    msq = jnp.mean(hidden * hidden, axis=-1)
    gain = lax.all_gather(norm_gain, "val", axis=1, tiled=True)
    gain = lax.dynamic_slice_in_dim(gain, me * own, own, axis=0)
    normed = (hidden - mean[..., None]) * lax.rsqrt(msq - mean * mean + 1e-06)[..., None]
    normed = (normed * gain[:, None, :]).astype(BF16)
    normed = normed.transpose(1, 0, 2).reshape(rows, own * vsize)

    pieces = [normed, around(normed, 1), around(normed, -1), around(normed, 2)]
    return project_out(pieces, index, wo, chunk).astype(BF16)


def project_out(pieces, index, wo, chunk):
    return sum(
        jnp.dot(x, rows_of(wo, i, chunk), preferred_element_type=F32)
        for x, i in zip(pieces, index)
    )


def solution(mesh):
    placed = (
        P("seq", "val"),
        P(None, "val"),
        P(None, "val"),
        P(None, None, "val"),
        P(),
        P(),
        P(None, "val"),
        P(None, "val", None),
    )
    return jax.shard_map(
        per_device, mesh=mesh, in_specs=placed, out_specs=P("seq", "val"), check_vma=False
    )
```

```python
import functools

import jax
import jax.numpy as jnp
from jax import lax
from jax.experimental import pallas as pl
from jax.experimental.pallas import tpu as pltpu
from jax.sharding import PartitionSpec as P

F32 = jnp.float32
BF16 = jnp.bfloat16
LANES = 128
NEVER = -1e30
BLOCK = 256


def around(x, distance):
    n = lax.axis_size("val")
    return lax.ppermute(x, "val", [(i, (i + distance) % n) for i in range(n)])


def params():
    return pltpu.CompilerParams(vmem_limit_bytes=48 * 1024 * 1024)


def cost(flops, nbytes, exps=0):
    return pl.CostEstimate(flops=flops, bytes_accessed=nbytes, transcendentals=exps)


def ring_gather(x):
    half = x.shape[0] // 2
    left = around(x, 1)
    right = around(x, -1)
    upper = around(left[:half], 1)
    lower = around(right[half:], -1)
    return x, left, right, upper, lower


def product_kernel(counts, with_total, scalars, *refs):
    refs = list(refs)
    total = None
    weights = refs[sum(counts) : sum(counts) + len(counts)]
    at = 0
    for n, w_ref in zip(counts, weights):
        x = refs[at][...] if n == 1 else jnp.concatenate([r[...] for r in refs[at : at + n]], axis=0)
        at += n
        term = jnp.dot(x, w_ref[...], preferred_element_type=F32)
        total = term if total is None else total + term
    at += len(counts)
    if with_total:
        total = total + refs[at][...]
        at += 1
    outs = refs[at:]
    if len(outs) == 1:
        outs[0][...] = total.astype(outs[0].dtype)
        return
    step = pl.program_id(0)
    own, _, vlocal = outs[0].shape
    for k, out in enumerate(outs):

        @pl.when(step == k)
        def _():
            for h in range(own):
                out[h] = total[:, h * vlocal : (h + 1) * vlocal].astype(out.dtype)


def product(groups, index, w, total, dtype, turned=None, own=2):
    rows = sum(x.shape[0] for x in groups[0])
    chunk = groups[0][0].shape[1]
    cols = w.shape[1]
    block = min(BLOCK, cols)
    steps = cols // block
    scalars = jnp.stack(list(index) + [turned if turned is not None else jnp.int32(0)])
    last = len(groups)

    def column(j, s):
        return j if turned is None else lax.rem(j + s[last], steps)

    flat = [x for g in groups for x in g]
    in_specs = [pl.BlockSpec(x.shape, lambda j, s: (0, 0)) for x in flat]
    for g in range(len(groups)):
        in_specs.append(pl.BlockSpec((chunk, block), lambda j, s, g=g: (s[g], column(j, s))))
    args = flat + [w] * len(groups)
    if total is not None:
        in_specs.append(pl.BlockSpec((rows, block), lambda j, s: (0, column(j, s))))
        args.append(total)
    if turned is None:
        out_specs = pl.BlockSpec((rows, block), lambda j, s: (0, j))
        out_shape = jax.ShapeDtypeStruct((rows, cols), dtype)
    else:
        shape = (own, rows, block // own)
        out_specs = [pl.BlockSpec(shape, lambda j, s: (0, 0, 0))] * steps
        out_shape = [jax.ShapeDtypeStruct(shape, dtype)] * steps
    flops = 2 * rows * chunk * len(groups) * cols
    nbytes = 2 * chunk * len(groups) * (cols + rows) + 4 * rows * cols
    return pl.pallas_call(
        functools.partial(product_kernel, [len(g) for g in groups], total is not None),
        grid_spec=pltpu.PrefetchScalarGridSpec(
            num_scalar_prefetch=1, grid=(steps,), in_specs=in_specs, out_specs=out_specs
        ),
        out_shape=out_shape,
        compiler_params=params(),
        cost_estimate=cost(flops, nbytes),
    )(scalars, *args)


def within_kernel(q_ref, k_ref, g_ref, bias_ref, kwt_ref, p_ref, stat_ref, mark_ref):
    own, rows, _ = p_ref.shape
    qsize = q_ref.shape[1] // own
    g = g_ref[...] + bias_ref[...]
    logf = jnp.minimum(g, 0.0) - jnp.log1p(jnp.exp(-jnp.abs(g)))
    late = lax.broadcasted_iota(jnp.int32, (rows, rows), 0)
    early = lax.broadcasted_iota(jnp.int32, (rows, rows), 1)
    causal = late >= early
    cumb = jnp.dot(
        causal.astype(F32), logf, precision=lax.Precision.HIGHEST, preferred_element_type=F32
    )
    cumb = pltpu.roll(cumb, LANES - own, axis=1)
    gap = g - cumb
    gap_rows = gap.T
    most = jnp.max(gap, axis=0, keepdims=True)
    total = cumb[rows - 1 : rows]
    mark_ref[...] = jnp.concatenate([total + most, total, jnp.zeros((6, LANES), F32)], axis=0)
    lane = lax.broadcasted_iota(jnp.int32, (rows, LANES), 1)
    stat = jnp.zeros((rows, LANES), F32)
    for h in range(own):
        q = q_ref[:, h * qsize : (h + 1) * qsize]
        k = k_ref[:, h * qsize : (h + 1) * qsize]
        seen = jnp.where(causal, gap_rows[h : h + 1, :], F32(NEVER))
        high = jnp.max(seen, axis=1, keepdims=True)
        score = lax.dot_general(q, k, (((1,), (1,)), ((), ())), preferred_element_type=F32)
        wts = jnp.exp(seen - high) * (score * qsize ** (-0.5))
        wts = jnp.where(causal, wts, 0.0).astype(BF16)
        p_ref[h] = wts
        denom = jnp.sum(wts.astype(F32), axis=1, keepdims=True)
        stat = jnp.where(lane == h, high, jnp.where(lane == own + h, denom, stat))
        fall = jnp.exp(gap[:, h : h + 1] - most[:, h : h + 1])
        kw = (k.astype(F32) * fall).astype(BF16)
        kwt_ref[h * qsize : (h + 1) * qsize] = kw.astype(F32).T.astype(BF16)
    stat_ref[...] = stat


def within(q, k, g, bias, own):
    rows, width = q.shape
    return pl.pallas_call(
        within_kernel,
        out_shape=[
            jax.ShapeDtypeStruct((width, rows), BF16),
            jax.ShapeDtypeStruct((own, rows, rows), BF16),
            jax.ShapeDtypeStruct((rows, LANES), F32),
            jax.ShapeDtypeStruct((8, LANES), F32),
        ],
        compiler_params=params(),
        cost_estimate=cost(2 * rows * rows * width, 4 * rows * width, own * rows * rows),
    )(q, k, g, bias)


def parts_of(x):
    hi = x.astype(BF16).astype(F32)
    mid = (x - hi).astype(BF16).astype(F32)
    return [hi, mid, x - hi - mid]


def summary_kernel(scalars, kwt_ref, mark_ref, v0, v1, v2, v3, sent_ref, v_ref):
    own, rows, vlocal = v0.shape
    vsize = v_ref.shape[2]
    qsize = kwt_ref.shape[0] // own
    for n, ref in enumerate((v0, v1, v2, v3)):
        at = pl.multiple_of(scalars[n] * vlocal, vlocal)
        for h in range(own):
            v_ref[h, :, pl.ds(at, vlocal)] = ref[h]
    lane = lax.broadcasted_iota(jnp.int32, (qsize, LANES), 1)
    for h in range(own):
        kwt = kwt_ref[h * qsize : (h + 1) * qsize]
        state = jnp.dot(kwt, v_ref[h], preferred_element_type=F32)
        extra = jnp.where(lane == 0, jnp.sum(kwt.astype(F32), axis=1, keepdims=True), 0.0)
        marks = parts_of(mark_ref[0:1, h : h + 1]) + parts_of(mark_ref[1:2, h : h + 1])
        for n, x in enumerate(marks):
            extra = jnp.where(lane == 1 + n, x, extra)
        sent_ref[h * qsize : (h + 1) * qsize, :vsize] = state.astype(BF16)
        sent_ref[h * qsize : (h + 1) * qsize, vsize:] = extra.astype(BF16)


def summary(index, kwt, mark, pieces):
    own, rows, vlocal = pieces[0].shape
    vsize = vlocal * len(pieces)
    whole = lambda shape: pl.BlockSpec(shape, lambda j, s: (0,) * len(shape))
    return pl.pallas_call(
        summary_kernel,
        grid_spec=pltpu.PrefetchScalarGridSpec(
            num_scalar_prefetch=1,
            grid=(1,),
            in_specs=[whole(kwt.shape), whole(mark.shape)] + [whole(x.shape) for x in pieces],
            out_specs=[whole((kwt.shape[0], vsize + LANES)), whole((own, rows, vsize))],
        ),
        out_shape=[
            jax.ShapeDtypeStruct((kwt.shape[0], vsize + LANES), BF16),
            jax.ShapeDtypeStruct((own, rows, vsize), BF16),
        ],
        compiler_params=params(),
        cost_estimate=cost(2 * kwt.size * vsize, 3 * own * rows * vsize * 2),
    )(jnp.stack(index), kwt, mark, *pieces)


def inside_kernel(p_ref, v_ref, out_ref):
    for h in range(p_ref.shape[0]):
        out_ref[h] = jnp.dot(p_ref[h], v_ref[h], preferred_element_type=F32)


def inside(p, v):
    return pl.pallas_call(
        inside_kernel,
        out_shape=jax.ShapeDtypeStruct(v.shape, F32),
        compiler_params=params(),
        cost_estimate=cost(2 * p.size * v.shape[2], 6 * v.size),
    )(p, v)


def prefix_kernel(got_ref, out_ref):
    blocks, cut, width = got_ref.shape
    body = width - LANES
    lane = lax.broadcasted_iota(jnp.int32, (cut, LANES), 1)
    state = jnp.zeros((cut, body), F32)
    extra = jnp.zeros((cut, LANES), F32)
    ptop = jnp.full((cut, 1), NEVER, F32)
    for b in range(blocks):
        held = extra
        for n, x in enumerate(parts_of(ptop)):
            held = jnp.where(lane == 1 + n, x, held)
        out_ref[b, :, :body] = state.astype(BF16)
        out_ref[b, :, body:] = held.astype(BF16)
        if b == blocks - 1:
            break
        ext = got_ref[b, :, body:].astype(F32)
        top = ext[:, 1:2] + ext[:, 2:3] + ext[:, 3:4]
        total = ext[:, 4:5] + ext[:, 5:6] + ext[:, 6:7]
        new = jnp.maximum(ptop + total, top)
        keep = jnp.exp(ptop + total - new)
        add = jnp.exp(top - new)
        state = keep * state + add * got_ref[b, :, :body].astype(F32)
        extra = keep * extra + add * ext
        ptop = new


def prefixes(got):
    return pl.pallas_call(
        prefix_kernel,
        out_shape=jax.ShapeDtypeStruct(got.shape, BF16),
        compiler_params=params(),
        cost_estimate=cost(4 * got.size, 4 * got.size),
    )(got)


def finish_kernel(q_ref, prefix_ref, numer_ref, stat_ref, gain_ref, out_ref):
    own, rows, vsize = numer_ref.shape
    qsize = q_ref.shape[1] // own
    for h in range(own):
        inter = jnp.dot(
            q_ref[:, h * qsize : (h + 1) * qsize], prefix_ref[h], preferred_element_type=F32
        )
        ext = prefix_ref[h, 0:16, vsize:].astype(F32)[0:1]
        ptop = ext[:, 1:2] + ext[:, 2:3] + ext[:, 3:4]
        high = stat_ref[:, h : h + 1]
        top = jnp.maximum(high, ptop)
        fade = jnp.exp(high - top)
        decay = jnp.exp(ptop - top) * qsize ** (-0.5)
        denom = stat_ref[:, own + h : own + h + 1] * fade + inter[:, vsize : vsize + 1] * decay
        share = 1.0 / jnp.maximum(jnp.abs(denom), 1.0)
        hidden = numer_ref[h] * (fade * share) + inter[:, :vsize] * (decay * share)
        mean = jnp.mean(hidden, axis=1, keepdims=True)
        msq = jnp.mean(hidden * hidden, axis=1, keepdims=True)
        normed = (hidden - mean) * lax.rsqrt(msq - mean * mean + 1e-06) * gain_ref[h : h + 1]
        out_ref[:, h * vsize : (h + 1) * vsize] = normed.astype(BF16)


def finish(q, prefix, numer, stat, gain):
    own, rows, vsize = numer.shape
    return pl.pallas_call(
        finish_kernel,
        out_shape=jax.ShapeDtypeStruct((rows, own * vsize), BF16),
        compiler_params=params(),
        cost_estimate=cost(2 * q.size * vsize, 8 * numer.size),
    )(q, prefix, numer, stat, gain)


def per_device(tokens, w_query, w_key, w_value, w_gate, gate_bias, norm_gain, w_out):
    me = lax.axis_index("val")
    nval = lax.axis_size("val")
    place = lax.axis_index("seq")
    blocks = lax.axis_size("seq")
    rows, chunk = tokens.shape
    width = w_query.shape[0]
    heads, vlocal = w_value.shape[1:]
    own = heads // nval
    qsize = w_query.shape[1] // own
    vsize = vlocal * nval
    index = [(me + d) % nval for d in (0, nval - 1, 1, 2)]

    x, left, right, upper, lower = ring_gather(tokens)

    part = heads * vlocal // blocks
    wo = lax.dynamic_slice_in_dim(w_out.reshape(heads * vlocal, -1), place * part, part, axis=0)

    def exchanged(cut):
        kept = [cut((me + d) % nval) for d in range(nval)]
        return [kept[0], around(kept[1], 1), around(kept[3], -1), around(kept[2], 2)]

    def by_source(pieces):
        out = jnp.zeros((nval,) + pieces[0].shape, pieces[0].dtype)
        for i, piece in zip(index, pieces):
            out = lax.dynamic_update_index_in_dim(out, piece, i, axis=0)
        return out

    wo = by_source(
        exchanged(lambda to: lax.dynamic_slice_in_dim(wo, to * chunk, chunk, axis=1))
    )
    gain = by_source(
        exchanged(lambda to: lax.dynamic_slice_in_dim(norm_gain, to * own, own, axis=0))
    )
    gain = gain.transpose(1, 0, 2).reshape(own, vsize)
    wo = lax.all_gather(wo, "seq", axis=0)
    wo = wo.reshape(heads, blocks // heads, nval, part, chunk).transpose(0, 2, 1, 3, 4)
    wo = wo.reshape(heads * vsize, chunk)

    wv = w_value.reshape(width, heads * vlocal)
    wg = lax.dynamic_slice_in_dim(w_gate, me * own, own, axis=2).reshape(width, 2 * own)
    wg = jnp.pad(wg, ((0, 0), (0, LANES - 2 * own)))
    bias = lax.dynamic_slice_in_dim(gate_bias, me * own, own, axis=1).reshape(1, 2 * own)
    bias = jnp.pad(bias, ((0, 0), (0, LANES - 2 * own)))

    first, last = [(x,), (left,), (right,)], [(upper, lower)]

    def early(w):
        return product(first, index[:3], w, None, F32)

    v_acc, q_acc, k_acc, g_acc = early(wv), early(w_query), early(w_key), early(wg)
    v0, v1, v2, v3 = product(last, index[3:], wv, v_acc, BF16, turned=me, own=own)
    values = [v0, around(v1, 1), around(v3, -1), around(v2, 2)]
    q = product(last, index[3:], w_query, q_acc, BF16)
    k = product(last, index[3:], w_key, k_acc, BF16)
    g = product(last, index[3:], wg, g_acc, F32)
    kwt, p, stat, mark = within(q, k, g, bias, own)
    sent, v = summary(index, kwt, mark, values)
    got = lax.all_to_all(sent.reshape(blocks, -1, vsize + LANES), "seq", 0, 0)
    numer = inside(p, v)
    prefix = lax.all_to_all(prefixes(got), "seq", 0, 0)
    normed = finish(q, prefix.reshape(own, qsize, vsize + LANES), numer, stat, gain)

    x, left, right, upper, lower = ring_gather(normed)
    acc = product([(x,), (left,), (right,)], index[:3], wo, None, F32)
    return product([(upper, lower)], index[3:], wo, acc, BF16)


def solution(mesh):
    placed = (
        P("seq", "val"),
        P(None, "val"),
        P(None, "val"),
        P(None, None, "val"),
        P(),
        P(),
        P(None, "val"),
        P(None, "val", None),
    )
    return jax.shard_map(
        per_device, mesh=mesh, in_specs=placed, out_specs=P("seq", "val"), check_vma=False
    )
```

```python
import functools

import jax
import jax.numpy as jnp
from jax import lax
from jax.experimental import pallas as pl
from jax.experimental.pallas import tpu as pltpu
from jax.sharding import PartitionSpec as P

F32 = jnp.float32
BF16 = jnp.bfloat16
LANES = 128
NEVER = -1e30
BLOCK = 512
AHEAD = 3


def around(x, distance):
    n = lax.axis_size("val")
    return lax.ppermute(x, "val", [(i, (i + distance) % n) for i in range(n)])


def params(mib=48):
    return pltpu.CompilerParams(vmem_limit_bytes=mib * 1024 * 1024)


def cost(flops, nbytes, exps=0):
    return pl.CostEstimate(flops=flops, bytes_accessed=nbytes, transcendentals=exps)


class Ring:
    def __init__(self, plus, minus, later, keep):
        self.plus, self.minus = around(plus, 1), around(minus, -1)
        self.later, self.keep = later, keep

    def second(self, after):
        plus, minus = moved(self.later, [[(1, 0, 0)], [(0, 0, 0)]], after)
        self.sent = plus
        self.left = (self.plus, around(plus, 1))
        self.right = (around(minus, -1), self.minus)

    def forward(self):
        half = self.later[0].shape[0]
        cuts = [(0, half), (self.plus.shape[0] - self.keep, self.keep)]
        plus, minus = moved(
            [self.plus, self.minus], [[(n, *cut) for cut in cuts if cut[1]] for n in (0, 1)], [self.sent]
        )
        self.opposite = (around(plus, 1), around(minus, -1))


def moved_kernel(n, n_after, plan, *refs):
    sources, outs = refs[:n], refs[n + n_after :]
    for out, parts in zip(outs, plan):
        at = 0
        for source, first, count in parts:
            count = count or sources[source].shape[0] - first
            out[at : at + count] = sources[source][first : first + count]
            at += count


def moved(arrays, plan, after):
    shapes = [sum(c or arrays[n].shape[0] - f for n, f, c in parts) for parts in plan]
    anywhere, vmem = (pl.BlockSpec(memory_space=m) for m in (pl.ANY, pltpu.VMEM))
    return pl.pallas_call(
        functools.partial(moved_kernel, len(arrays), len(after), plan),
        in_specs=[vmem] * len(arrays) + [anywhere] * len(after),
        out_specs=[vmem] * len(plan),
        out_shape=[
            jax.ShapeDtypeStruct((n, arrays[0].shape[1]), arrays[0].dtype) for n in shapes
        ],
        compiler_params=params(),
        cost_estimate=cost(0, 4 * sum(shapes) * arrays[0].shape[1]),
    )(*arrays, *after)


def packed_kernel(scalars, x_ref, w_ref, plus, minus, own_ref, sems):
    rows, cols = x_ref.shape
    half, part = rows // 2, own_ref.shape[0]
    copies = Copies(sems)
    me, n = scalars[1], w_ref.shape[1] // cols

    def piece(to, first, count):
        at = pl.multiple_of(scalars[0] * part + first, 16)
        columns = pl.ds(pl.multiple_of(lax.rem(me + to, n) * cols, cols), cols)
        return w_ref.at[pl.ds(at, count), columns]

    started = []
    for out, first, to, piece_first in ((plus, 0, 1, 0), (minus, half, n - 1, part // 2)):
        started += [
            copies.start(x_ref.at[pl.ds(first, half)], out.at[pl.ds(0, half)]),
            copies.start(piece(to, 0, part), out.at[pl.ds(half, part)]),
            copies.start(
                piece(2, piece_first, part // 2), out.at[pl.ds(half + part, part // 2)]
            ),
        ]
    started.append(copies.start(piece(0, 0, part), own_ref))
    for copy in started:
        copy.wait()


def packed(x, w, place, me, part):
    rows, cols = x.shape
    shapes = [(rows // 2 + part + part // 2, cols)] * 2 + [(part, cols)]
    return pl.pallas_call(
        packed_kernel,
        in_specs=[pl.BlockSpec(memory_space=pltpu.SMEM)] + [pl.BlockSpec(memory_space=pltpu.HBM)] * 2,
        out_specs=[pl.BlockSpec(memory_space=pltpu.VMEM)] * 3,
        out_shape=[jax.ShapeDtypeStruct(shape, x.dtype) for shape in shapes],
        scratch_shapes=[pltpu.SemaphoreType.DMA((7,))],
        compiler_params=params(),
        cost_estimate=cost(0, 8 * x.size),
    )(jnp.stack([place, me]), x, w)


def flat_kernel(n, w_ref, *refs):
    refs[-2][...] = w_ref[...].reshape(refs[-2].shape)
    refs[-1][...] = jnp.zeros_like(refs[-1])


def flat(w, turn, before=None):
    rows, heads, size = w.shape
    steps = 4
    block = rows // (2 * steps)
    args = [w] if before is None else [w, before]
    return pl.pallas_call(
        functools.partial(flat_kernel, len(args)),
        grid=(steps,),
        in_specs=[
            pl.BlockSpec((block, heads, size), lambda j: (j + turn * steps, 0, 0)),
            pl.BlockSpec(memory_space=pl.ANY),
        ][: len(args)],
        out_specs=[
            pl.BlockSpec((block, heads * size), lambda j: (j + turn * steps, 0)),
            pl.BlockSpec((8, LANES), lambda j: (0, 0)),
        ],
        out_shape=[
            jax.ShapeDtypeStruct((rows, heads * size), w.dtype),
            jax.ShapeDtypeStruct((8, LANES), F32),
        ],
        input_output_aliases={} if before is None else {1: 0},
        compiler_params=params(),
        cost_estimate=cost(0, 2 * w.size),
    )(*args)


class Copies:
    def __init__(self, sems):
        self.sems = sems
        self.used = 0

    def start(self, source, target):
        copy = pltpu.make_async_copy(source, target, self.sems.at[self.used])
        self.used += 1
        copy.start()
        return copy


class Loads:
    def __init__(self, ahead):
        self.ahead = ahead
        self.waiting = []
        self.started = []

    def add(self, start):
        self.waiting.append(start)

    def next(self):
        while self.waiting and len(self.started) <= self.ahead:
            self.started.append(self.waiting.pop(0)())
        for copy in self.started.pop(0):
            copy.wait()


def fetch_rows(copies, pieces, buffer):
    started, at = [], 0
    for piece in pieces:
        n = min(piece.shape[0], buffer.shape[0] // len(pieces))
        piece = piece.at[pl.ds(0, n)]
        started.append(copies.start(piece, buffer.at[pl.ds(at, n)]))
        at += n
    return started


def fetch_weight(copies, w, chunk, columns, target, sources):
    if len(w.shape) == 2:
        n = target.shape[0]
        rows = pl.ds(pl.multiple_of(chunk * n, n), n)
        return [copies.start(w.at[rows, columns], target)]
    own, nval = target.shape[:2]
    started = []
    for h in range(own):
        for n in range(nval):
            source = w.at[chunk * own + h, :, n, :, columns]
            started.append(copies.start(source, target.at[h, sources[n]]))
    return started


def product_kernel(counts, blocks, with_total, n_after, scalars, *refs):
    refs = list(refs)
    take = lambda n: [refs.pop(0) for _ in range(n)]
    ngroups, nweights = len(counts), len(blocks)
    groups = [take(n) for n in counts]
    weights = take(nweights)
    totals = take(nweights) if with_total else None
    take(n_after)
    outs = take(nweights)
    xs = take(ngroups)
    ws = take(nweights)
    ts = take(nweights) if with_total else None
    os = take(nweights)
    copies = Copies(refs[0])
    sources = [scalars[ngroups + n] for n in range(4)]
    loads = Loads(AHEAD)
    tasks = []
    for n, block in enumerate(blocks):
        for at in range(0, ws[n].shape[-1], block):
            columns = pl.ds(at, block)
            for g in range(ngroups):
                if not tasks:
                    loads.add(lambda g=g: fetch_rows(copies, groups[g], xs[g]))
                loads.add(
                    lambda n=n, g=g, columns=columns: fetch_weight(
                        copies, weights[n], scalars[g], columns, ws[n].at[g, ..., columns], sources
                    )
                )
            if with_total:
                loads.add(
                    lambda n=n, columns=columns: [
                        copies.start(totals[n].at[:, columns], ts[n].at[:, columns])
                    ]
                )
            tasks.append((n, columns))
    last = []
    for at, (n, columns) in enumerate(tasks):
        total = None
        for g in range(ngroups):
            if at == 0:
                loads.next()
            loads.next()
            w = ws[n][g, ..., columns].reshape(xs[g].shape[1], -1)
            term = jnp.dot(xs[g][...], w, preferred_element_type=F32)
            total = term if total is None else total + term
        if with_total:
            loads.next()
            total = total + ts[n][:, columns]
        os[n][:, columns] = total.astype(os[n].dtype)
        last.append(copies.start(os[n].at[:, columns], outs[n].at[:, columns]))
    for copy in last:
        copy.wait()


def product(rows, groups, index, weights, totals, dtypes, sources, after=()):
    chunk = groups[0][0].shape[1]
    widths = [w.shape[-1] for w in weights]
    blocks = [min(BLOCK, n) for n in widths]
    steps = sum(n // block for n, block in zip(widths, blocks))
    anywhere, hbm = pl.BlockSpec(memory_space=pl.ANY), pl.BlockSpec(memory_space=pltpu.HBM)
    args = [x for g in groups for x in g]
    spaces = [anywhere] * len(args) + [hbm] * len(weights)
    args += list(weights) + list(totals or []) + list(after)
    spaces += [anywhere] * (len(args) - len(spaces))
    scratch = [pltpu.VMEM((rows, chunk), BF16) for _ in groups]
    for w in weights:
        if w.ndim == 2:
            held = (chunk, w.shape[1])
        else:
            heads, parts, nval, n, cols = w.shape
            held = (chunk // (parts * nval * n), nval, parts, n, cols)
        scratch.append(pltpu.VMEM((len(groups), *held), BF16))
    if totals is not None:
        scratch += [pltpu.VMEM((rows, n), F32) for n in widths]
    scratch += [pltpu.VMEM((rows, n), d) for n, d in zip(widths, dtypes)]
    pieces = 8
    scratch.append(pltpu.SemaphoreType.DMA((8 + steps * (len(groups) * pieces + 2),)))
    cols = sum(widths)
    return pl.pallas_call(
        functools.partial(
            product_kernel, [len(g) for g in groups], blocks, totals is not None, len(after)
        ),
        in_specs=[pl.BlockSpec(memory_space=pltpu.SMEM)]
        + spaces,
        out_specs=[anywhere] * len(weights),
        out_shape=[jax.ShapeDtypeStruct((rows, n), d) for n, d in zip(widths, dtypes)],
        scratch_shapes=scratch,
        compiler_params=params(),
        cost_estimate=cost(
            2 * rows * chunk * len(groups) * cols,
            2 * chunk * len(groups) * (cols + rows) + 4 * rows * cols,
        ),
    )(jnp.stack(list(index) + list(sources)), *args)


def values_kernel(scalars, upper, lower, w_ref, acc_ref, gain_ref, *refs):
    n = (len(refs) - 5) // 2
    outs, (x, w, acc), os, (sems, out_sems) = refs[:n], refs[n : n + 3], refs[n + 3 : -2], refs[-2:]
    own, more, vlocal = outs[0].shape
    rows, block = acc.shape[1], acc.shape[2]
    copies = Copies(sems)
    loads = Loads(AHEAD)
    order = [1, n - 1, *range(2, n - 1), 0]

    def fetch(k):
        to = lax.rem(scalars[1] + k, n)
        columns = pl.ds(pl.multiple_of(to * block, block), block)
        return fetch_weight(copies, w_ref, scalars[0], columns, w.at[k], None) + [
            copies.start(acc_ref.at[:, columns], acc.at[k])
        ]

    loads.add(lambda: fetch_rows(copies, (upper, lower), x))
    for k in order:
        loads.add(lambda k=k: fetch(k))
    loads.next()
    line = lax.broadcasted_iota(jnp.int32, (more - rows, vlocal), 0)
    out_copies = Copies(out_sems)
    last = []
    for k in order:
        to = lax.rem(scalars[1] + k, n)
        loads.next()
        total = acc[k] + jnp.dot(x[...], w[k], preferred_element_type=F32)
        total = total.astype(BF16)
        for h in range(own):
            os[k][h, :rows] = total[:, h * vlocal : (h + 1) * vlocal]
            tail = jnp.zeros((more - rows, vlocal), F32)
            for m, part in enumerate(parts_of(gain_ref[pl.ds(to * own + h, 1), :])):
                tail = jnp.where(line == m, part, tail)
            os[k][h, rows:] = tail.astype(BF16)
        last.append(out_copies.start(os[k], outs[k]))
    for copy in last:
        copy.wait()


def values_by_device(halves, index, me, w, acc, gain, own):
    rows, cols = acc.shape
    chunk = halves[0].shape[1]
    vlocal = gain.shape[1]
    block = own * vlocal
    steps = cols // block
    shape = (own, rows + 16, vlocal)
    anywhere = pl.BlockSpec(memory_space=pl.ANY)
    return pl.pallas_call(
        values_kernel,
        in_specs=[pl.BlockSpec(memory_space=pltpu.SMEM)]
        + [anywhere] * 2
        + [pl.BlockSpec(memory_space=pltpu.HBM), anywhere]
        + [pl.BlockSpec(memory_space=pltpu.VMEM)],
        out_specs=[anywhere] * steps,
        out_shape=[jax.ShapeDtypeStruct(shape, BF16)] * steps,
        scratch_shapes=[
            pltpu.VMEM((rows, chunk), BF16),
            pltpu.VMEM((steps, chunk, block), BF16),
            pltpu.VMEM((steps, rows, block), F32),
        ]
        + [pltpu.VMEM(shape, BF16)] * steps
        + [pltpu.SemaphoreType.DMA((2 + 2 * steps,)), pltpu.SemaphoreType.DMA((steps,))],
        compiler_params=params(),
        cost_estimate=cost(2 * rows * chunk * cols, 2 * chunk * (cols + rows) + 6 * rows * cols),
    )(jnp.stack([index, me]), *halves, w, acc, gain)


def exchanged(pieces):
    return [pieces[0], around(pieces[1], 1), around(pieces[3], -1), around(pieces[2], 2)]


def within_kernel(q_ref, k_ref, g_ref, bias_ref, kwt_ref, p_ref, stat_ref, mark_ref):
    own, rows, _ = p_ref.shape
    qsize = q_ref.shape[1] // own
    g = g_ref[...] + bias_ref[...]
    logf = jnp.minimum(g, 0.0) - jnp.log1p(jnp.exp(-jnp.abs(g)))
    late = lax.broadcasted_iota(jnp.int32, (rows, rows), 0)
    early = lax.broadcasted_iota(jnp.int32, (rows, rows), 1)
    causal = late >= early
    cumb = jnp.dot(
        causal.astype(F32), logf, precision=lax.Precision.HIGHEST, preferred_element_type=F32
    )
    cumb = pltpu.roll(cumb, LANES - own, axis=1)
    gap = g - cumb
    gap_rows = gap.T
    most = jnp.max(gap, axis=0, keepdims=True)
    total = cumb[rows - 1 : rows]
    mark_ref[...] = jnp.concatenate([total + most, total, jnp.zeros((6, LANES), F32)], axis=0)
    lane = lax.broadcasted_iota(jnp.int32, (rows, LANES), 1)
    stat = jnp.zeros((rows, LANES), F32)
    for h in range(own):
        q = q_ref[:, h * qsize : (h + 1) * qsize]
        k = k_ref[:, h * qsize : (h + 1) * qsize]
        seen = jnp.where(causal, gap_rows[h : h + 1, :], F32(NEVER))
        high = jnp.max(seen, axis=1, keepdims=True)
        score = lax.dot_general(q, k, (((1,), (1,)), ((), ())), preferred_element_type=F32)
        wts = jnp.exp(seen - high) * (score * qsize ** (-0.5))
        wts = jnp.where(causal, wts, 0.0).astype(BF16)
        p_ref[h] = wts
        denom = jnp.sum(wts.astype(F32), axis=1, keepdims=True)
        stat = jnp.where(lane == h, high, jnp.where(lane == own + h, denom, stat))
        fall = jnp.exp(gap[:, h : h + 1] - most[:, h : h + 1])
        kw = (k.astype(F32) * fall).astype(BF16)
        kwt_ref[h * qsize : (h + 1) * qsize] = kw.astype(F32).T.astype(BF16)
    stat_ref[...] = stat


def within(q, k, g, bias, own):
    rows, width = q.shape
    return pl.pallas_call(
        within_kernel,
        out_shape=[
            jax.ShapeDtypeStruct((width, rows), BF16),
            jax.ShapeDtypeStruct((own, rows, rows), BF16),
            jax.ShapeDtypeStruct((rows, LANES), F32),
            jax.ShapeDtypeStruct((8, LANES), F32),
        ],
        compiler_params=params(),
        cost_estimate=cost(2 * rows * rows * width, 4 * rows * width, own * rows * rows),
    )(q, k, g, bias)


def parts_of(x):
    hi = x.astype(BF16).astype(F32)
    mid = (x - hi).astype(BF16).astype(F32)
    return [hi, mid, x - hi - mid]


def summary_kernel(scalars, kwt_ref, mark_ref, v0, v1, v2, v3, sent_ref, v_ref, gain_ref):
    vlocal = v0.shape[2]
    own, rows, vsize = v_ref.shape
    gain_ref[...] = jnp.zeros_like(gain_ref)
    qsize = kwt_ref.shape[0] // own
    for n, ref in enumerate((v0, v1, v2, v3)):
        at = pl.multiple_of(scalars[n] * vlocal, vlocal)
        for h in range(own):
            v_ref[h, :, pl.ds(at, vlocal)] = ref[h, :rows]
            tail = ref[h, rows:].astype(F32)
            gain_ref[h : h + 1, pl.ds(at, vlocal)] = tail[0:1] + tail[1:2] + tail[2:3]
    lane = lax.broadcasted_iota(jnp.int32, (qsize, LANES), 1)
    for h in range(own):
        kwt = kwt_ref[h * qsize : (h + 1) * qsize]
        state = jnp.dot(kwt, v_ref[h], preferred_element_type=F32)
        extra = jnp.where(lane == 0, jnp.sum(kwt.astype(F32), axis=1, keepdims=True), 0.0)
        marks = parts_of(mark_ref[0:1, h : h + 1]) + parts_of(mark_ref[1:2, h : h + 1])
        for n, x in enumerate(marks):
            extra = jnp.where(lane == 1 + n, x, extra)
        sent_ref[h * qsize : (h + 1) * qsize, :vsize] = state.astype(BF16)
        sent_ref[h * qsize : (h + 1) * qsize, vsize:] = extra.astype(BF16)


def summary(index, kwt, mark, pieces):
    own, _, vlocal = pieces[0].shape
    rows = kwt.shape[1]
    vsize = vlocal * len(pieces)
    whole = lambda shape: pl.BlockSpec(shape, lambda j, s: (0,) * len(shape))
    return pl.pallas_call(
        summary_kernel,
        grid_spec=pltpu.PrefetchScalarGridSpec(
            num_scalar_prefetch=1,
            grid=(1,),
            in_specs=[whole(kwt.shape), whole(mark.shape)] + [whole(x.shape) for x in pieces],
            out_specs=[whole((kwt.shape[0], vsize + LANES)), whole((own, rows, vsize)), whole((8, vsize))],
        ),
        out_shape=[
            jax.ShapeDtypeStruct((kwt.shape[0], vsize + LANES), BF16),
            jax.ShapeDtypeStruct((own, rows, vsize), BF16),
            jax.ShapeDtypeStruct((8, vsize), F32),
        ],
        compiler_params=params(),
        cost_estimate=cost(2 * kwt.size * vsize, 3 * own * rows * vsize * 2),
    )(jnp.stack(index), kwt, mark, *pieces)


def inside_kernel(p_ref, v_ref, out_ref):
    for h in range(p_ref.shape[0]):
        out_ref[h] = jnp.dot(p_ref[h], v_ref[h], preferred_element_type=F32)


def inside(p, v):
    return pl.pallas_call(
        inside_kernel,
        out_shape=jax.ShapeDtypeStruct(v.shape, F32),
        compiler_params=params(),
        cost_estimate=cost(2 * p.size * v.shape[2], 6 * v.size),
    )(p, v)


def prefix_kernel(got_ref, out_ref):
    blocks, cut, width = got_ref.shape
    body = width - LANES
    lane = lax.broadcasted_iota(jnp.int32, (cut, LANES), 1)
    source = lax.broadcasted_iota(jnp.int32, (LANES, 2 * LANES), 0)
    target = lax.broadcasted_iota(jnp.int32, (LANES, 2 * LANES), 1)
    first = jnp.where(target < LANES, 1, 4)
    spread = ((source >= first) & (source < first + 3)).astype(F32).astype(BF16)
    marks = jnp.dot(
        got_ref[:, :, body:].reshape(blocks * cut, LANES), spread, preferred_element_type=F32
    )
    state = [jnp.zeros((cut, LANES), F32) for _ in range(width // LANES)]
    ptop = jnp.full((cut, LANES), NEVER, F32)
    for b in range(blocks):
        held = state[-1]
        for n, x in enumerate(parts_of(ptop)):
            held = jnp.where(lane == 1 + n, x, held)
        for n, x in enumerate(state[:-1] + [held]):
            out_ref[b, :, n * LANES : (n + 1) * LANES] = x.astype(BF16)
        if b == blocks - 1:
            break
        top = marks[b * cut : (b + 1) * cut, :LANES]
        total = marks[b * cut : (b + 1) * cut, LANES:]
        new = jnp.maximum(ptop + total, top)
        keep = jnp.exp(ptop + total - new)
        add = jnp.exp(top - new)
        state = [
            keep * x + add * got_ref[b, :, n * LANES : (n + 1) * LANES].astype(F32)
            for n, x in enumerate(state)
        ]
        ptop = new


def prefixes(got):
    return pl.pallas_call(
        prefix_kernel,
        out_shape=jax.ShapeDtypeStruct(got.shape, BF16),
        compiler_params=params(),
        cost_estimate=cost(4 * got.size, 4 * got.size),
    )(got)


def finish_kernel(q_ref, prefix_ref, numer_ref, stat_ref, gain_ref, upper, lower):
    own, rows, vsize = numer_ref.shape
    qsize = q_ref.shape[1] // own
    for h in range(own):
        inter = jnp.dot(
            q_ref[:, h * qsize : (h + 1) * qsize], prefix_ref[h], preferred_element_type=F32
        )
        ext = prefix_ref[h, 0:16, vsize:].astype(F32)[0:1]
        ptop = ext[:, 1:2] + ext[:, 2:3] + ext[:, 3:4]
        high = stat_ref[:, h : h + 1]
        top = jnp.maximum(high, ptop)
        fade = jnp.exp(high - top)
        decay = jnp.exp(ptop - top) * qsize ** (-0.5)
        denom = stat_ref[:, own + h : own + h + 1] * fade + inter[:, vsize : vsize + 1] * decay
        share = 1.0 / jnp.maximum(jnp.abs(denom), 1.0)
        hidden = numer_ref[h] * (fade * share) + inter[:, :vsize] * (decay * share)
        mean = jnp.mean(hidden, axis=1, keepdims=True)
        msq = jnp.mean(hidden * hidden, axis=1, keepdims=True)
        normed = (hidden - mean) * lax.rsqrt(msq - mean * mean + 1e-06) * gain_ref[h : h + 1]
        normed = normed.astype(BF16)
        upper[:, h * vsize : (h + 1) * vsize] = normed[: rows // 2]
        lower[:, h * vsize : (h + 1) * vsize] = normed[rows // 2 :]


def finish(q, prefix, numer, stat, gain):
    own, rows, vsize = numer.shape
    return pl.pallas_call(
        finish_kernel,
        out_shape=[jax.ShapeDtypeStruct((rows // 2, own * vsize), BF16)] * 2,
        compiler_params=params(),
        cost_estimate=cost(2 * q.size * vsize, 8 * numer.size),
    )(q, prefix, numer, stat, gain)


def per_device(tokens, w_query, w_key, w_value, w_gate, gate_bias, norm_gain, w_out):
    me = lax.axis_index("val")
    nval = lax.axis_size("val")
    place = lax.axis_index("seq")
    blocks = lax.axis_size("seq")
    rows, chunk = tokens.shape
    width = w_query.shape[0]
    heads, vlocal = w_value.shape[1:]
    own = heads // nval
    qsize = w_query.shape[1] // own
    vsize = vlocal * nval
    index = [(me + d) % nval for d in (0, nval - 1, 1, 2)]

    part = heads * vlocal // blocks
    half = rows // 2
    plus, minus, kept = packed(tokens, w_out.reshape(heads * vlocal, -1), place, me, part)
    ring = Ring(plus, minus, [tokens[:half], tokens[half:]], part // 2)
    wv, mark = flat(w_value, 0)
    ring.second([mark])
    ring.forward()
    wv, _ = flat(w_value, 1, wv)
    wg = lax.dynamic_slice_in_dim(w_gate, me * own, own, axis=2).reshape(width, 2 * own)
    wg = jnp.pad(wg, ((0, 0), (0, LANES - 2 * own)))
    bias = lax.dynamic_slice_in_dim(gate_bias, me * own, own, axis=1).reshape(1, 2 * own)
    bias = jnp.pad(bias, ((0, 0), (0, LANES - 2 * own)))
    groups = [(tokens,), ring.left, ring.right]
    acc = product(rows, groups, index[:3], [wv], None, [F32], index, [wg])[0]
    values = values_by_device(ring.opposite, index[3], me, wv, acc, norm_gain, own)
    first = values[0]
    q, k, g = product(
        rows,
        groups + [ring.opposite],
        index,
        [w_query, w_key, wg],
        None,
        [BF16, BF16, F32],
        index,
        [first],
    )
    arrived = [kept, ring.plus, ring.minus, *ring.opposite]
    cuts = [(0, 0, 0), (1, half, part), (2, half, part), (3, half, 0), (4, half, 0)]
    wo = moved(arrived, [cuts], [acc])[0]
    wo = lax.all_gather(wo, "seq", axis=0)
    wo = wo.reshape(heads, blocks // heads, nval, part, chunk)

    values = exchanged(values)
    kwt, p, stat, mark = within(q, k, g, bias, own)
    sent, v, gain = summary(index, kwt, mark, values)
    got = lax.all_to_all(sent.reshape(blocks, -1, vsize + LANES), "seq", 0, 0)
    numer = inside(p, v)
    prefix = lax.all_to_all(prefixes(got), "seq", 0, 0)
    upper, lower = finish(q, prefix.reshape(own, qsize, vsize + LANES), numer, stat, gain)

    ring = Ring(upper, lower, [upper, lower], 0)
    accs = product(rows, [(upper, lower)], index[:1], [wo], None, [F32], index)
    ring.second(accs)
    ring.forward()
    accs = product(rows, [ring.left, ring.right], index[1:3], [wo], accs, [F32], index)
    return product(rows, [ring.opposite], index[3:], [wo], accs, [BF16], index)[0]


def solution(mesh):
    placed = (
        P("seq", "val"),
        P(None, "val"),
        P(None, "val"),
        P(None, None, "val"),
        P(),
        P(),
        P(None, "val"),
        P(None, "val", None),
    )
    return jax.shard_map(
        per_device, mesh=mesh, in_specs=placed, out_specs=P("seq", "val"), check_vma=False
    )
```

```python
import functools

import jax
import jax.numpy as jnp
from jax import lax
from jax.experimental import pallas as pl
from jax.experimental.pallas import tpu as pltpu
from jax.sharding import PartitionSpec as P

F32 = jnp.float32
BF16 = jnp.bfloat16
LANES = 128
NEVER = -1e30
BLOCK = 512
AHEAD = 4


def around(x, distance):
    n = lax.axis_size("val")
    return lax.ppermute(x, "val", [(i, (i + distance) % n) for i in range(n)])


def params(mib=48):
    return pltpu.CompilerParams(vmem_limit_bytes=mib * 1024 * 1024)


def cost(flops, nbytes, exps=0):
    return pl.CostEstimate(flops=flops, bytes_accessed=nbytes, transcendentals=exps)


class Ring:
    def __init__(self, plus, minus, later):
        self.plus, self.minus = around(plus, 1), around(minus, -1)
        self.later = later

    def second(self, after):
        plus, minus = moved(self.later, [[(1, 0, 0)], [(0, 0, 0)]], after)
        self.sent = plus
        self.left = (self.plus, around(plus, 1))
        self.right = (around(minus, -1), self.minus)

    def forward(self, after=()):
        half = self.later[0].shape[0]
        plus, minus = moved(
            [self.plus, self.minus], [[(0, 0, half)], [(1, 0, half)]], [self.sent, *after]
        )
        self.opposite = (around(plus, 1), around(minus, -1))


def moved_kernel(n, n_after, plan, *refs):
    sources, outs = refs[:n], refs[n + n_after :]
    for out, parts in zip(outs, plan):
        at = 0
        for source, first, count in parts:
            count = count or sources[source].shape[0] - first
            out[at : at + count] = sources[source][first : first + count]
            at += count


def moved(arrays, plan, after):
    shapes = [sum(c or arrays[n].shape[0] - f for n, f, c in parts) for parts in plan]
    anywhere, vmem = (pl.BlockSpec(memory_space=m) for m in (pl.ANY, pltpu.VMEM))
    return pl.pallas_call(
        functools.partial(moved_kernel, len(arrays), len(after), plan),
        in_specs=[vmem] * len(arrays) + [anywhere] * len(after),
        out_specs=[vmem] * len(plan),
        out_shape=[
            jax.ShapeDtypeStruct((n, arrays[0].shape[1]), arrays[0].dtype) for n in shapes
        ],
        compiler_params=params(),
        cost_estimate=cost(0, 4 * sum(shapes) * arrays[0].shape[1]),
    )(*arrays, *after)


def packed_kernel(scalars, x_ref, w_ref, plus, minus, across, kept, sems):
    rows, cols = x_ref.shape
    half, part = rows // 2, kept.shape[0]
    copies = Copies(sems)
    me, n = scalars[1], w_ref.shape[1] // cols

    def piece(to):
        at = pl.multiple_of(scalars[0] * part, part)
        columns = pl.ds(pl.multiple_of(lax.rem(me + to, n) * cols, cols), cols)
        return w_ref.at[pl.ds(at, part), columns]

    started = [
        copies.start(piece(1), plus.at[pl.ds(half, part)]),
        copies.start(piece(n - 1), minus.at[pl.ds(half, part)]),
        copies.start(piece(2), across),
        copies.start(piece(0), kept),
    ]
    plus[:half] = x_ref[:half]
    minus[:half] = x_ref[half:]
    for copy in started:
        copy.wait()


def packed(x, w, place, me, part):
    rows, cols = x.shape
    shapes = [(rows // 2 + part, cols)] * 2 + [(part, cols)] * 2
    return pl.pallas_call(
        packed_kernel,
        in_specs=[pl.BlockSpec(memory_space=m) for m in (pltpu.SMEM, pltpu.VMEM, pl.ANY)],
        out_specs=[pl.BlockSpec(memory_space=pltpu.VMEM)] * 4,
        out_shape=[jax.ShapeDtypeStruct(shape, x.dtype) for shape in shapes],
        scratch_shapes=[pltpu.SemaphoreType.DMA((4,))],
        compiler_params=params(),
        cost_estimate=cost(0, 8 * x.size),
    )(jnp.stack([place, me]), x, w)


def flat_kernel(n, w_ref, *refs):
    refs[-2][...] = w_ref[...].reshape(refs[-2].shape)
    refs[-1][...] = jnp.zeros_like(refs[-1])


def flat(w, turn, before=None):
    rows, heads, size = w.shape
    steps = 4
    block = rows // (2 * steps)
    args = [w] if before is None else [w, before]
    return pl.pallas_call(
        functools.partial(flat_kernel, len(args)),
        grid=(steps,),
        in_specs=[
            pl.BlockSpec((block, heads, size), lambda j: (j + turn * steps, 0, 0)),
            pl.BlockSpec(memory_space=pl.ANY),
        ][: len(args)],
        out_specs=[
            pl.BlockSpec((block, heads * size), lambda j: (j + turn * steps, 0)),
            pl.BlockSpec((8, LANES), lambda j: (0, 0)),
        ],
        out_shape=[
            jax.ShapeDtypeStruct((rows, heads * size), w.dtype),
            jax.ShapeDtypeStruct((8, LANES), F32),
        ],
        input_output_aliases={} if before is None else {1: 0},
        compiler_params=params(),
        cost_estimate=cost(0, 2 * w.size),
    )(*args)


class Copies:
    def __init__(self, sems):
        self.sems = sems
        self.used = 0

    def start(self, source, target):
        copy = pltpu.make_async_copy(source, target, self.sems.at[self.used])
        self.used += 1
        copy.start()
        return copy


class Loads:
    def __init__(self, ahead):
        self.ahead = ahead
        self.waiting = []
        self.started = []

    def add(self, start):
        self.waiting.append(start)

    def begin(self):
        while self.waiting and len(self.started) <= self.ahead:
            self.started.append(self.waiting.pop(0)())

    def next(self):
        self.begin()
        for copy in self.started.pop(0):
            copy.wait()


def put_rows(pieces, buffer):
    n = buffer.shape[0] // len(pieces)
    for at, piece in enumerate(pieces):
        buffer[at * n : (at + 1) * n] = piece[:n]


def fetch_weight(copies, w, chunk, columns, target, sources):
    if len(w.shape) == 2:
        n = target.shape[0]
        rows = pl.ds(pl.multiple_of(chunk * n, n), n)
        return [copies.start(w.at[rows, columns], target)]
    own, nval = target.shape[:2]
    started = []
    for h in range(own):
        for n in range(nval):
            source = w.at[chunk * own + h, :, n, :, columns]
            started.append(copies.start(source, target.at[h, sources[n]]))
    return started


def product_kernel(counts, tasks, with_total, n_after, staged, scalars, *refs):
    refs = list(refs)
    take = lambda n: [refs.pop(0) for _ in range(n)]
    ngroups, nweights = len(counts), 1 + max(n for _, segments in tasks for n, _ in segments)
    groups = [take(n) for n in counts]
    weights = take(nweights)
    totals = take(nweights) if with_total else None
    take(n_after)
    outs = take(nweights)
    x, ws = take(2)
    os = take(nweights) if staged else outs
    copies = Copies(refs[0])
    chunk = x.shape[1] // ngroups
    sources = [scalars[ngroups + n] for n in range(4)]
    part = lambda g: x.at[:, pl.ds(g * chunk, chunk)]

    def load(g, at, segments):
        started = []
        for n, columns in segments:
            target = ws.at[g, ..., pl.ds(at, columns.size)]
            started += fetch_weight(copies, weights[n], scalars[g], columns, target, sources)
            at += columns.size
        return started

    loads = Loads(AHEAD)
    for at, segments in tasks:
        for g in range(ngroups):
            loads.add(functools.partial(load, g, at, segments))
    loads.begin()
    for g in range(ngroups):
        put_rows(groups[g], part(g))
    last = []
    for at, segments in tasks:
        width = sum(columns.size for _, columns in segments)
        total = None
        for g in range(ngroups):
            loads.next()
            w = ws[g, ..., at : at + width].reshape(chunk, -1)
            term = jnp.dot(part(g)[...], w, preferred_element_type=F32)
            total = term if total is None else total + term
        at = 0
        for n, columns in segments:
            out = total[:, at : at + columns.size]
            if with_total:
                out = out + totals[n][:, columns]
            os[n][:, columns] = out.astype(os[n].dtype)
            if staged:
                last.append(copies.start(os[n].at[:, columns], outs[n].at[:, columns]))
            at += columns.size
    for copy in last:
        copy.wait()


def product(rows, groups, index, weights, totals, dtypes, sources, after=(), staged=False):
    chunk = groups[0][0].shape[1]
    widths = [w.shape[-1] for w in weights]
    tasks, held = [], 0
    for n, width in enumerate(widths):
        for at in range(0, width, BLOCK):
            tasks.append((held, [(n, pl.ds(at, min(BLOCK, width)))]))
            held += min(BLOCK, width)
    anywhere, vmem = (pl.BlockSpec(memory_space=m) for m in (pl.ANY, pltpu.VMEM))
    pieces = [x for g in groups for x in g]
    specs = [vmem] * len(pieces) + [anywhere] * len(weights)
    specs += [vmem] * len(totals or []) + [anywhere] * len(after)
    args = pieces + list(weights) + list(totals or []) + list(after)
    shape = (chunk, held)
    if weights[0].ndim > 2:
        heads, parts, nval, n, cols = weights[0].shape
        shape = (chunk // (parts * nval * n), nval, parts, n, cols)
    scratch = [pltpu.VMEM((rows, len(groups) * chunk), BF16)]
    scratch.append(pltpu.VMEM((len(groups), *shape), BF16))
    if staged:
        scratch += [pltpu.VMEM((rows, n), d) for n, d in zip(widths, dtypes)]
    copies = len(tasks) * (len(groups) * 8 + 2)
    scratch.append(pltpu.SemaphoreType.DMA((copies,)))
    cols = sum(widths)
    return pl.pallas_call(
        functools.partial(
            product_kernel,
            [len(g) for g in groups],
            tasks,
            totals is not None,
            len(after),
            staged,
        ),
        in_specs=[pl.BlockSpec(memory_space=pltpu.SMEM)] + specs,
        out_specs=[anywhere if staged else vmem] * len(weights),
        out_shape=[jax.ShapeDtypeStruct((rows, n), d) for n, d in zip(widths, dtypes)],
        scratch_shapes=scratch,
        compiler_params=params(),
        cost_estimate=cost(
            2 * rows * chunk * len(groups) * cols,
            2 * chunk * len(groups) * (cols + rows) + 4 * rows * cols,
        ),
    )(jnp.stack(list(index) + list(sources)), *args)


def values_kernel(scalars, upper, lower, w_ref, acc_ref, gain_ref, *refs):
    n = len(refs) - 3
    outs, (x, w, sems) = refs[:n], refs[n:]
    own, more, vlocal = outs[0].shape
    rows, block = acc_ref.shape[0], own * vlocal
    copies = Copies(sems)
    loads = Loads(AHEAD)
    order = [1, n - 1, *range(2, n - 1), 0]

    def spot(k):
        to = lax.rem(scalars[1] + k, n)
        return to, pl.ds(pl.multiple_of(to * block, block), block)

    for k in order:
        loads.add(lambda k=k: fetch_weight(copies, w_ref, scalars[0], spot(k)[1], w.at[k], None))
    loads.begin()
    put_rows((upper, lower), x)
    line = lax.broadcasted_iota(jnp.int32, (more - rows, vlocal), 0)
    for k in order:
        to, columns = spot(k)
        loads.next()
        total = acc_ref[:, columns] + jnp.dot(x[...], w[k], preferred_element_type=F32)
        total = total.astype(BF16)
        for h in range(own):
            outs[k][h, :rows] = total[:, h * vlocal : (h + 1) * vlocal]
            tail = jnp.zeros((more - rows, vlocal), F32)
            for m, part in enumerate(parts_of(gain_ref[pl.ds(to * own + h, 1), :])):
                tail = jnp.where(line == m, part, tail)
            outs[k][h, rows:] = tail.astype(BF16)


def values_by_device(halves, index, me, w, acc, gain, own):
    rows, cols = acc.shape
    chunk = halves[0].shape[1]
    vlocal = gain.shape[1]
    block = own * vlocal
    steps = cols // block
    shape = (own, rows + 16, vlocal)
    vmem = pl.BlockSpec(memory_space=pltpu.VMEM)
    return pl.pallas_call(
        values_kernel,
        in_specs=[
            pl.BlockSpec(memory_space=pltpu.SMEM),
            vmem,
            vmem,
            pl.BlockSpec(memory_space=pl.ANY),
            vmem,
            vmem,
        ],
        out_specs=[vmem] * steps,
        out_shape=[jax.ShapeDtypeStruct(shape, BF16)] * steps,
        scratch_shapes=[
            pltpu.VMEM((rows, chunk), BF16),
            pltpu.VMEM((steps, chunk, block), BF16),
            pltpu.SemaphoreType.DMA((steps,)),
        ],
        compiler_params=params(),
        cost_estimate=cost(2 * rows * chunk * cols, 2 * chunk * (cols + rows) + 6 * rows * cols),
    )(jnp.stack([index, me]), *halves, w, acc, gain)


def exchanged(pieces):
    return [pieces[0], around(pieces[1], 1), around(pieces[3], -1), around(pieces[2], 2)]


def within_kernel(counts, scalars, *refs):
    pieces = iter(refs[: sum(counts)])
    wg_ref, bias_ref, q_ref, k_ref, kwt_ref, p_ref, stat_ref, mark_ref = refs[sum(counts) :]
    own, rows, _ = p_ref.shape
    qsize = q_ref.shape[1] // own
    chunk = refs[0].shape[1]
    g = bias_ref[...]
    for n, count in enumerate(counts):
        w = wg_ref[pl.ds(pl.multiple_of(scalars[n] * chunk, chunk), chunk), :]
        terms = []
        for _ in range(count):
            x = next(pieces)[: rows // count]
            terms.append(jnp.dot(x, w, preferred_element_type=F32))
        g = g + (terms[0] if count == 1 else jnp.concatenate(terms, axis=0))
    logf = jnp.minimum(g, 0.0) - jnp.log1p(jnp.exp(-jnp.abs(g)))
    late = lax.broadcasted_iota(jnp.int32, (rows, rows), 0)
    early = lax.broadcasted_iota(jnp.int32, (rows, rows), 1)
    causal = late >= early
    cumb = jnp.dot(
        causal.astype(F32), logf, precision=lax.Precision.HIGHEST, preferred_element_type=F32
    )
    cumb = pltpu.roll(cumb, LANES - own, axis=1)
    gap = g - cumb
    gap_rows = gap.T
    most = jnp.max(gap, axis=0, keepdims=True)
    total = cumb[rows - 1 : rows]
    mark_ref[...] = jnp.concatenate([total + most, total, jnp.zeros((6, LANES), F32)], axis=0)
    lane = lax.broadcasted_iota(jnp.int32, (rows, LANES), 1)
    stat = jnp.zeros((rows, LANES), F32)
    for h in range(own):
        q = q_ref[:, h * qsize : (h + 1) * qsize]
        k = k_ref[:, h * qsize : (h + 1) * qsize]
        seen = jnp.where(causal, gap_rows[h : h + 1, :], F32(NEVER))
        high = jnp.max(seen, axis=1, keepdims=True)
        score = lax.dot_general(q, k, (((1,), (1,)), ((), ())), preferred_element_type=F32)
        wts = jnp.exp(seen - high) * (score * qsize ** (-0.5))
        wts = jnp.where(causal, wts, 0.0).astype(BF16)
        p_ref[h] = wts
        denom = jnp.sum(wts.astype(F32), axis=1, keepdims=True)
        stat = jnp.where(lane == h, high, jnp.where(lane == own + h, denom, stat))
        fall = jnp.exp(gap[:, h : h + 1] - most[:, h : h + 1])
        kw = (k.astype(F32) * fall).astype(BF16)
        kwt_ref[h * qsize : (h + 1) * qsize] = kw.astype(F32).T.astype(BF16)
    stat_ref[...] = stat


def within(groups, index, wg, bias, q, k, own):
    rows, width = q.shape
    pieces = [x for g in groups for x in g]
    vmem = pl.BlockSpec(memory_space=pltpu.VMEM)
    return pl.pallas_call(
        functools.partial(within_kernel, [len(g) for g in groups]),
        in_specs=[pl.BlockSpec(memory_space=pltpu.SMEM)] + [vmem] * (len(pieces) + 4),
        out_specs=[vmem] * 4,
        out_shape=[
            jax.ShapeDtypeStruct((width, rows), BF16),
            jax.ShapeDtypeStruct((own, rows, rows), BF16),
            jax.ShapeDtypeStruct((rows, LANES), F32),
            jax.ShapeDtypeStruct((8, LANES), F32),
        ],
        compiler_params=params(),
        cost_estimate=cost(4 * rows * rows * width, 8 * rows * width, own * rows * rows),
    )(jnp.stack(list(index)), *pieces, wg, bias, q, k)


def parts_of(x):
    hi = x.astype(BF16).astype(F32)
    mid = (x - hi).astype(BF16).astype(F32)
    return [hi, mid, x - hi - mid]


def of_head(head, rows):
    return jnp.where(head == 0, rows[:, 0:1], rows[:, 1:2])


def marked(extra, top, total):
    lane = lax.broadcasted_iota(jnp.int32, extra.shape, 1)
    for n, x in enumerate(parts_of(top) + ([] if total is None else parts_of(total))):
        extra = jnp.where(lane == 1 + n, x, extra)
    return extra


def marks_of(extra):
    top = extra[:, 1:2] + extra[:, 2:3] + extra[:, 3:4]
    total = extra[:, 4:5] + extra[:, 5:6] + extra[:, 6:7]
    return top, total


def summary_kernel(scalars, kwt_ref, mark_ref, v0, v1, v2, v3, mine, other, v_ref, gain_ref):
    vlocal = v0.shape[2]
    own, rows, vsize = v_ref.shape
    gain_ref[...] = jnp.zeros_like(gain_ref)
    qsize = kwt_ref.shape[0] // own
    for n, ref in enumerate((v0, v1, v2, v3)):
        at = pl.multiple_of(scalars[n] * vlocal, vlocal)
        for h in range(own):
            v_ref[h, :, pl.ds(at, vlocal)] = ref[h, :rows]
            tail = ref[h, rows:].astype(F32)
            gain_ref[h : h + 1, pl.ds(at, vlocal)] = tail[0:1] + tail[1:2] + tail[2:3]
    lane = lax.broadcasted_iota(jnp.int32, (qsize, LANES), 1)
    core = scalars[4]
    for h, out in ((core, mine), (1 - core, other)):
        kwt = kwt_ref[pl.ds(pl.multiple_of(h * qsize, qsize), qsize), :]
        out[:, :vsize] = jnp.dot(kwt, v_ref[h], preferred_element_type=F32).astype(BF16)
        extra = jnp.where(lane == 0, jnp.sum(kwt.astype(F32), axis=1, keepdims=True), 0.0)
        top, total = of_head(h, mark_ref[0:1, :]), of_head(h, mark_ref[1:2, :])
        out[:, vsize:] = marked(extra, top, total).astype(BF16)


def summary(index, core, kwt, mark, pieces):
    own, _, vlocal = pieces[0].shape
    rows = kwt.shape[1]
    vsize = vlocal * len(pieces)
    whole = lambda shape: pl.BlockSpec(shape, lambda j, s: (0,) * len(shape))
    shapes = [((kwt.shape[0] // own, vsize + LANES), BF16)] * 2
    shapes += [((own, rows, vsize), BF16), ((8, vsize), F32)]
    return pl.pallas_call(
        summary_kernel,
        grid_spec=pltpu.PrefetchScalarGridSpec(
            num_scalar_prefetch=1,
            grid=(1,),
            in_specs=[whole(kwt.shape), whole(mark.shape)] + [whole(x.shape) for x in pieces],
            out_specs=[whole(shape) for shape, _ in shapes],
        ),
        out_shape=[jax.ShapeDtypeStruct(shape, dtype) for shape, dtype in shapes],
        compiler_params=params(),
        cost_estimate=cost(2 * kwt.size * vsize, 3 * own * rows * vsize * 2),
    )(jnp.stack(list(index) + [core]), kwt, mark, *pieces)


def pair_kernel(scalars, mine, got, out):
    first = scalars[0] == 0
    body = mine.shape[1] - LANES
    a, b = mine[:, body:].astype(F32), got[:, body:].astype(F32)
    early, late = jnp.where(first, a, b), jnp.where(first, b, a)
    (etop, etotal), (ltop, ltotal) = marks_of(early), marks_of(late)
    top = jnp.maximum(etop + ltotal, ltop)
    fe, fl = jnp.exp(etop + ltotal - top), jnp.exp(ltop - top)
    fa, fb = jnp.where(first, fe, fl), jnp.where(first, fl, fe)
    state = fa * mine[:, :body].astype(F32) + fb * got[:, :body].astype(F32)
    out[:, :body] = state.astype(BF16)
    out[:, body:] = marked(fa * a + fb * b, top, etotal + ltotal).astype(BF16)


def pair(core, mine, got):
    vmem = pl.BlockSpec(memory_space=pltpu.VMEM)
    return pl.pallas_call(
        pair_kernel,
        in_specs=[pl.BlockSpec(memory_space=pltpu.SMEM), vmem, vmem],
        out_specs=vmem,
        out_shape=jax.ShapeDtypeStruct(mine.shape, BF16),
        compiler_params=params(),
        cost_estimate=cost(4 * mine.size, 6 * mine.size),
    )(jnp.stack([core]), mine, got)


def unpair_kernel(scalars, prefix, mine, got, keep, send):
    first = scalars[0] == 0
    body = mine.shape[1] - LANES
    p = prefix[:, body:].astype(F32)
    s = jnp.where(first, mine[:, body:].astype(F32), got[:, body:].astype(F32))
    ptop, _ = marks_of(p)
    stop, stotal = marks_of(s)
    top = jnp.maximum(ptop + stotal, stop)
    fp, fs = jnp.exp(ptop + stotal - top), jnp.exp(stop - top)
    state = jnp.where(first, mine[:, :body], got[:, :body]).astype(F32)
    state = (fp * prefix[:, :body].astype(F32) + fs * state).astype(BF16)
    extra = marked(fp * p + fs * s, top, None).astype(BF16)
    keep[:, :body] = jnp.where(first, prefix[:, :body], state)
    send[:, :body] = jnp.where(first, state, prefix[:, :body])
    keep[:, body:] = jnp.where(first, prefix[:, body:], extra)
    send[:, body:] = jnp.where(first, extra, prefix[:, body:])


def unpair(core, prefix, mine, got):
    vmem = pl.BlockSpec(memory_space=pltpu.VMEM)
    return pl.pallas_call(
        unpair_kernel,
        in_specs=[pl.BlockSpec(memory_space=pltpu.SMEM)] + [vmem] * 3,
        out_specs=[vmem] * 2,
        out_shape=[jax.ShapeDtypeStruct(mine.shape, BF16)] * 2,
        compiler_params=params(),
        cost_estimate=cost(4 * mine.size, 10 * mine.size),
    )(jnp.stack([core]), prefix, mine, got)


def inside_kernel(p_ref, v_ref, out_ref):
    for h in range(p_ref.shape[0]):
        out_ref[h] = jnp.dot(p_ref[h], v_ref[h], preferred_element_type=F32)


def inside(p, v):
    return pl.pallas_call(
        inside_kernel,
        out_shape=jax.ShapeDtypeStruct(v.shape, F32),
        compiler_params=params(),
        cost_estimate=cost(2 * p.size * v.shape[2], 6 * v.size),
    )(p, v)


def prefix_kernel(got_ref, out_ref):
    blocks, cut, width = got_ref.shape
    body = width - LANES
    lane = lax.broadcasted_iota(jnp.int32, (cut, LANES), 1)
    source = lax.broadcasted_iota(jnp.int32, (LANES, 2 * LANES), 0)
    target = lax.broadcasted_iota(jnp.int32, (LANES, 2 * LANES), 1)
    first = jnp.where(target < LANES, 1, 4)
    spread = ((source >= first) & (source < first + 3)).astype(F32).astype(BF16)
    marks = jnp.dot(
        got_ref[:, :, body:].reshape(blocks * cut, LANES), spread, preferred_element_type=F32
    )
    state = [jnp.zeros((cut, LANES), F32) for _ in range(width // LANES)]
    ptop = jnp.full((cut, LANES), NEVER, F32)
    for b in range(blocks):
        held = state[-1]
        for n, x in enumerate(parts_of(ptop)):
            held = jnp.where(lane == 1 + n, x, held)
        for n, x in enumerate(state[:-1] + [held]):
            out_ref[b, :, n * LANES : (n + 1) * LANES] = x.astype(BF16)
        if b == blocks - 1:
            break
        top = marks[b * cut : (b + 1) * cut, :LANES]
        total = marks[b * cut : (b + 1) * cut, LANES:]
        new = jnp.maximum(ptop + total, top)
        keep = jnp.exp(ptop + total - new)
        add = jnp.exp(top - new)
        state = [
            keep * x + add * got_ref[b, :, n * LANES : (n + 1) * LANES].astype(F32)
            for n, x in enumerate(state)
        ]
        ptop = new


def prefixes(got):
    return pl.pallas_call(
        prefix_kernel,
        out_shape=jax.ShapeDtypeStruct(got.shape, BF16),
        compiler_params=params(),
        cost_estimate=cost(4 * got.size, 4 * got.size),
    )(got)


def finish_kernel(scalars, q_ref, mine, got, numer_ref, stat_ref, gain_ref, upper, lower):
    own, rows, vsize = numer_ref.shape
    qsize = q_ref.shape[1] // own
    core = scalars[0]
    for h, prefix_ref in ((core, mine), (1 - core, got)):
        q = q_ref[:, pl.ds(pl.multiple_of(h * qsize, qsize), qsize)]
        inter = jnp.dot(q, prefix_ref[...], preferred_element_type=F32)
        ptop, _ = marks_of(prefix_ref[0:16, vsize:].astype(F32)[0:1])
        high = of_head(h, stat_ref[...])
        top = jnp.maximum(high, ptop)
        fade = jnp.exp(high - top)
        decay = jnp.exp(ptop - top) * qsize ** (-0.5)
        denom = of_head(h, stat_ref[:, own : 2 * own])
        denom = denom * fade + inter[:, vsize : vsize + 1] * decay
        share = 1.0 / jnp.maximum(jnp.abs(denom), 1.0)
        hidden = numer_ref[h] * (fade * share) + inter[:, :vsize] * (decay * share)
        mean = jnp.mean(hidden, axis=1, keepdims=True)
        msq = jnp.mean(hidden * hidden, axis=1, keepdims=True)
        gain = gain_ref[pl.ds(h, 1), :]
        normed = (hidden - mean) * lax.rsqrt(msq - mean * mean + 1e-06) * gain
        normed = normed.astype(BF16)
        columns = pl.ds(pl.multiple_of(h * vsize, vsize), vsize)
        upper[:, columns] = normed[: rows // 2]
        lower[:, columns] = normed[rows // 2 :]


def finish(core, q, mine, got, numer, stat, gain):
    own, rows, vsize = numer.shape
    vmem = pl.BlockSpec(memory_space=pltpu.VMEM)
    return pl.pallas_call(
        finish_kernel,
        in_specs=[pl.BlockSpec(memory_space=pltpu.SMEM)] + [vmem] * 6,
        out_specs=[vmem] * 2,
        out_shape=[jax.ShapeDtypeStruct((rows // 2, own * vsize), BF16)] * 2,
        compiler_params=params(),
        cost_estimate=cost(2 * q.size * vsize, 8 * numer.size),
    )(jnp.stack([core]), q, mine, got, numer, stat, gain)


def per_device(tokens, w_query, w_key, w_value, w_gate, gate_bias, norm_gain, w_out):
    me = lax.axis_index("val")
    nval = lax.axis_size("val")
    place = lax.axis_index("seq")
    blocks = lax.axis_size("seq")
    rows, chunk = tokens.shape
    width = w_query.shape[0]
    heads, vlocal = w_value.shape[1:]
    own = heads // nval
    qsize = w_query.shape[1] // own
    vsize = vlocal * nval
    index = [(me + d) % nval for d in (0, nval - 1, 1, 2)]

    part = heads * vlocal // blocks
    half = rows // 2
    plus, minus, across, kept = packed(
        tokens, w_out.reshape(heads * vlocal, -1), place, me, part
    )
    ring = Ring(plus, minus, [tokens[:half], tokens[half:]])
    across = around(across, 2)
    wg = lax.dynamic_slice_in_dim(w_gate, me * own, own, axis=2).reshape(width, 2 * own)
    wg = jnp.pad(wg, ((0, 0), (0, LANES - 2 * own)))
    bias = lax.dynamic_slice_in_dim(gate_bias, me * own, own, axis=1).reshape(1, 2 * own)
    bias = jnp.pad(bias, ((0, 0), (0, LANES - 2 * own)))
    wv, early = flat(w_value, 0)
    ring.second([early, wg])
    wv, late = flat(w_value, 1, wv)
    ring.forward([late])
    groups = [(tokens,), ring.left, ring.right]
    acc = product(rows, groups, index[:3], [wv], None, [F32], index)[0]
    values = values_by_device(ring.opposite, index[3], me, wv, acc, norm_gain, own)
    groups.append(ring.opposite)
    q, k = product(
        rows, groups, index, [w_query, w_key], None, [BF16] * 2, index, values[:1]
    )
    cuts = [(0, 0, 0), (1, half, part), (2, half, part), (3, 0, 0)]
    wo = moved([kept, ring.plus, ring.minus, across], [cuts], [early])[0]
    wo = lax.all_gather(wo, "seq", axis=0)
    wo = wo.reshape(heads, blocks // heads, nval, part, chunk)

    values = exchanged(values)
    kwt, p, stat, mark = within(groups, index, wg, bias, q, k, own)
    core = place % 2
    mine, other, v, gain = summary(index, core, kwt, mark, values)
    cores = [(i, i ^ 1) for i in range(blocks)]
    got = lax.ppermute(other, "seq", cores)
    chips = [list(range(n, blocks, 2)) for n in range(2)]
    sliced = (blocks // 2, -1, vsize + LANES)
    both = pair(core, mine, got).reshape(sliced)
    both = lax.all_to_all(both, "seq", 0, 0, axis_index_groups=chips)
    numer = inside(p, v)
    prefix = lax.all_to_all(prefixes(both), "seq", 0, 0, axis_index_groups=chips)
    keep, send = unpair(core, prefix.reshape(mine.shape), mine, got)
    came = lax.ppermute(send, "seq", cores)
    upper, lower = finish(core, q, keep, came, numer, stat, gain)

    ring = Ring(upper, lower, [upper, lower])
    accs = product(rows, [(upper, lower)], index[:1], [wo], None, [F32], index)
    ring.second(accs)
    ring.forward()
    accs = product(rows, [ring.left, ring.right], index[1:3], [wo], accs, [F32], index)
    return product(rows, [ring.opposite], index[3:], [wo], accs, [BF16], index, staged=True)[0]


def solution(mesh):
    placed = (
        P("seq", "val"),
        P(None, "val"),
        P(None, "val"),
        P(None, None, "val"),
        P(),
        P(),
        P(None, "val"),
        P(None, "val", None),
    )
    return jax.shard_map(
        per_device, mesh=mesh, in_specs=placed, out_specs=P("seq", "val"), check_vma=False
    )
```

```python
import functools

import jax
import jax.numpy as jnp
from jax import lax
from jax.experimental import pallas as pl
from jax.experimental.pallas import tpu as pltpu
from jax.sharding import PartitionSpec as P

F32 = jnp.float32
BF16 = jnp.bfloat16
LANES = 128
NEVER = -1e30
BLOCK = 512
AHEAD = 4


def around(x, distance):
    n = lax.axis_size("val")
    return lax.ppermute(x, "val", [(i, (i + distance) % n) for i in range(n)])


def params(mib=48):
    return pltpu.CompilerParams(vmem_limit_bytes=mib * 1024 * 1024)


def cost(flops, nbytes, exps=0):
    return pl.CostEstimate(flops=flops, bytes_accessed=nbytes, transcendentals=exps)


class Ring:
    def __init__(self, plus, minus, later):
        self.own = (plus, minus)
        self.plus, self.minus = around(plus, 1), around(minus, -1)
        self.later = later

    def second(self, after):
        plus, minus = moved(self.later, [[(1, 0, 0)], [(0, 0, 0)]], after)
        self.sent = plus
        self.left = (self.plus, around(plus, 1))
        self.right = (around(minus, -1), self.minus)

    def forward(self, after=()):
        self.plus, self.minus = tied([self.plus, self.minus], [self.sent, *after])
        self.left = (self.plus, self.left[1])
        self.right = (self.right[0], self.minus)
        self.opposite = (around(self.plus, 1), around(self.minus, -1))


def nothing(*refs):
    pass


def tied(arrays, after):
    anywhere = pl.BlockSpec(memory_space=pl.ANY)
    return pl.pallas_call(
        nothing,
        in_specs=[anywhere] * (len(arrays) + len(after)),
        out_specs=[anywhere] * len(arrays),
        out_shape=[jax.ShapeDtypeStruct(x.shape, x.dtype) for x in arrays],
        input_output_aliases={n: n for n in range(len(arrays))},
        compiler_params=params(),
    )(*arrays, *after)


def moved_kernel(n, n_after, plan, *refs):
    sources, outs = refs[:n], refs[n + n_after :]
    for out, parts in zip(outs, plan):
        at = 0
        for source, first, count in parts:
            count = count or sources[source].shape[0] - first
            out[at : at + count] = sources[source][first : first + count]
            at += count


def moved(arrays, plan, after):
    shapes = [sum(c or arrays[n].shape[0] - f for n, f, c in parts) for parts in plan]
    anywhere, vmem = (pl.BlockSpec(memory_space=m) for m in (pl.ANY, pltpu.VMEM))
    return pl.pallas_call(
        functools.partial(moved_kernel, len(arrays), len(after), plan),
        in_specs=[vmem] * len(arrays) + [anywhere] * len(after),
        out_specs=[vmem] * len(plan),
        out_shape=[
            jax.ShapeDtypeStruct((n, arrays[0].shape[1]), arrays[0].dtype) for n in shapes
        ],
        compiler_params=params(32),
        cost_estimate=cost(0, 4 * sum(shapes) * arrays[0].shape[1]),
    )(*arrays, *after)


def flat_kernel(n, w_ref, *refs):
    refs[-2][...] = w_ref[...].reshape(refs[-2].shape)
    refs[-1][...] = jnp.zeros_like(refs[-1])


def flat(w, turn, before=None):
    rows, heads, size = w.shape
    steps = 4
    block = rows // (2 * steps)
    args = [w] if before is None else [w, before]
    return pl.pallas_call(
        functools.partial(flat_kernel, len(args)),
        grid=(steps,),
        in_specs=[
            pl.BlockSpec((block, heads, size), lambda j: (j + turn * steps, 0, 0)),
            pl.BlockSpec(memory_space=pl.ANY),
        ][: len(args)],
        out_specs=[
            pl.BlockSpec((block, heads * size), lambda j: (j + turn * steps, 0)),
            pl.BlockSpec((8, LANES), lambda j: (0, 0)),
        ],
        out_shape=[
            jax.ShapeDtypeStruct((rows, heads * size), w.dtype),
            jax.ShapeDtypeStruct((8, LANES), F32),
        ],
        input_output_aliases={} if before is None else {1: 0},
        compiler_params=params(),
        cost_estimate=cost(0, 2 * w.size),
    )(*args)


class Copies:
    def __init__(self, sems):
        self.sems = sems
        self.used = 0

    def start(self, source, target):
        copy = pltpu.make_async_copy(source, target, self.sems.at[self.used])
        self.used += 1
        copy.start()
        return copy


class Loads:
    def __init__(self, ahead):
        self.ahead = ahead
        self.waiting = []
        self.started = []

    def add(self, start):
        self.waiting.append(start)

    def begin(self):
        while self.waiting and len(self.started) <= self.ahead:
            self.started.append(self.waiting.pop(0)())

    def next(self):
        self.begin()
        for copy in self.started.pop(0):
            copy.wait()


def put_rows(pieces, buffer):
    n = buffer.shape[0] // len(pieces)
    for at, piece in enumerate(pieces):
        buffer[at * n : (at + 1) * n] = piece[:n]


def fetch_weight(copies, w, chunk, columns, target):
    n = target.shape[0]
    return [copies.start(w.at[pl.ds(pl.multiple_of(chunk * n, n), n), columns], target)]


def product_kernel(counts, tasks, n_after, scalars, *refs):
    refs = list(refs)
    take = lambda n: [refs.pop(0) for _ in range(n)]
    ngroups, nweights = len(counts), 1 + max(n for n, *_ in tasks)
    groups = [take(n) for n in counts]
    weights = take(nweights)
    take(n_after)
    outs = take(nweights)
    x, ws, sems = refs
    copies = Copies(sems)
    chunk = x.shape[1] // ngroups
    part = lambda g: x.at[:, pl.ds(g * chunk, chunk)]

    def load(g, n, at, columns):
        target = ws.at[g, :, pl.ds(at, columns.size)]
        return fetch_weight(copies, weights[n], scalars[g], columns, target)

    loads = Loads(AHEAD)
    for task in tasks:
        for g in range(ngroups):
            loads.add(functools.partial(load, g, *task))
    loads.begin()
    for g in range(ngroups):
        put_rows(groups[g], part(g))
    for n, at, columns in tasks:
        total = None
        for g in range(ngroups):
            loads.next()
            w = ws[g, :, at : at + columns.size]
            term = jnp.dot(part(g)[...], w, preferred_element_type=F32)
            total = term if total is None else total + term
        outs[n][:, columns] = total.astype(outs[n].dtype)


def product(rows, groups, index, weights, dtypes, after=()):
    chunk = groups[0][0].shape[1]
    widths = [w.shape[1] for w in weights]
    tasks, held = [], 0
    for n, width in enumerate(widths):
        for at in range(0, width, BLOCK):
            tasks.append((n, held, pl.ds(at, BLOCK)))
            held += BLOCK
    anywhere, vmem = (pl.BlockSpec(memory_space=m) for m in (pl.ANY, pltpu.VMEM))
    pieces = [x for g in groups for x in g]
    cols = sum(widths)
    return pl.pallas_call(
        functools.partial(product_kernel, [len(g) for g in groups], tasks, len(after)),
        in_specs=[pl.BlockSpec(memory_space=pltpu.SMEM)]
        + [vmem] * len(pieces)
        + [anywhere] * (len(weights) + len(after)),
        out_specs=[vmem] * len(weights),
        out_shape=[jax.ShapeDtypeStruct((rows, n), d) for n, d in zip(widths, dtypes)],
        scratch_shapes=[
            pltpu.VMEM((rows, len(groups) * chunk), BF16),
            pltpu.VMEM((len(groups), chunk, held), BF16),
            pltpu.SemaphoreType.DMA((len(tasks) * len(groups),)),
        ],
        compiler_params=params(),
        cost_estimate=cost(
            2 * rows * chunk * len(groups) * cols,
            2 * chunk * len(groups) * (cols + rows) + 4 * rows * cols,
        ),
    )(jnp.stack(list(index)), *pieces, *weights, *after)


def cut_kernel(n_after, scalars, w_ref, *refs):
    outs, sems = refs[n_after:-1], refs[-1]
    copies = Copies(sems)
    cols = outs[0].shape[1]
    n = w_ref.shape[1] // (2 * cols)
    spots = [2 * scalars[0] + scalars[1], 2 * scalars[0] + 1 - scalars[1]]
    spots += [2 * lax.rem(scalars[0] + to, n) + scalars[1] for to in range(1, n)]
    started = []
    for at, out in zip(spots, outs):
        started.append(
            copies.start(w_ref.at[:, pl.ds(pl.multiple_of(at * cols, cols), cols)], out)
        )
    for copy in started:
        copy.wait()


def cut_by_device(w, me, core, nval, after):
    rows, cols = w.shape[0], w.shape[1] // (2 * nval)
    anywhere, vmem = (pl.BlockSpec(memory_space=m) for m in (pl.ANY, pltpu.VMEM))
    return pl.pallas_call(
        functools.partial(cut_kernel, len(after)),
        in_specs=[pl.BlockSpec(memory_space=pltpu.SMEM)] + [anywhere] * (1 + len(after)),
        out_specs=[vmem] * (nval + 1),
        out_shape=[jax.ShapeDtypeStruct((rows, cols), w.dtype)] * (nval + 1),
        scratch_shapes=[pltpu.SemaphoreType.DMA((nval + 1,))],
        compiler_params=params(),
        cost_estimate=cost(0, 4 * rows * cols * (nval + 1)),
    )(jnp.stack([me, core]), w, *after)


def out_kernel(counts, with_total, scalars, *refs):
    refs = list(refs)
    take = lambda n: [refs.pop(0) for _ in range(n)]
    ngroups = len(counts)
    groups = [take(n) for n in counts]
    halves = [take(4), take(4)]
    total_ref = take(1)[0] if with_total else None
    out, x, ws, held, sems, out_sems = refs
    copies, out_copies = Copies(sems), Copies(out_sems)
    sources = [scalars[ngroups + n] for n in range(4)]
    core = scalars[ngroups + 4]
    chunk = x.shape[1] // ngroups
    cols, vlocal = ws.shape[2], chunk // 8
    row = lambda n: pl.ds(pl.multiple_of(n * vlocal, vlocal), vlocal)

    def load(t):
        started = []
        for g in range(ngroups):
            for n, w in enumerate(halves[t]):
                for h in range(2):
                    to = row(g * 8 + h * 4 + sources[n])
                    source = w.at[row(scalars[g] * 2 + h), :]
                    started.append(copies.start(source, ws.at[t, to, :]))
        return started

    started = [load(t) for t in range(2)]
    for g in range(ngroups):
        put_rows(groups[g], x.at[:, pl.ds(g * chunk, chunk)])
    last = []
    for t, side in enumerate((core, 1 - core)):
        columns = pl.ds(pl.multiple_of(side * cols, cols), cols)
        for copy in started[t]:
            copy.wait()
        total = jnp.dot(x[...], ws[t], preferred_element_type=F32)
        if with_total:
            total = total + total_ref[:, columns]
        held[t] = total.astype(held.dtype)
        last.append(out_copies.start(held.at[t], out.at[:, columns]))
    for copy in last:
        copy.wait()


def out_product(rows, groups, index, sources, core, mine, others, total, dtype):
    chunk = groups[0][0].shape[1]
    cols = mine[0].shape[1]
    anywhere, vmem = (pl.BlockSpec(memory_space=m) for m in (pl.ANY, pltpu.VMEM))
    pieces = [x for g in groups for x in g]
    totals = [] if total is None else [total]
    args = [*pieces, *mine, *others, *totals]
    n = len(groups)
    return pl.pallas_call(
        functools.partial(out_kernel, [len(g) for g in groups], total is not None),
        in_specs=[pl.BlockSpec(memory_space=pltpu.SMEM)]
        + [vmem] * len(pieces)
        + [anywhere] * 8
        + [vmem] * len(totals),
        out_specs=anywhere,
        out_shape=jax.ShapeDtypeStruct((rows, 2 * cols), dtype),
        scratch_shapes=[
            pltpu.VMEM((rows, n * chunk), BF16),
            pltpu.VMEM((2, n * chunk, cols), BF16),
            pltpu.VMEM((2, rows, cols), dtype),
            pltpu.SemaphoreType.DMA((16 * n,)),
            pltpu.SemaphoreType.DMA((2,)),
        ],
        compiler_params=params(56),
        cost_estimate=cost(4 * rows * chunk * n * cols, 4 * chunk * n * cols + 8 * rows * cols),
    )(jnp.stack(list(index) + list(sources) + [core]), *args)


def values_kernel(scalars, upper, lower, w_ref, acc_ref, gain_ref, after, *refs):
    n = len(refs) - 3
    outs, (x, w, sems) = refs[:n], refs[n:]
    own, more, vlocal = outs[0].shape
    rows, block = acc_ref.shape[0], own * vlocal
    copies = Copies(sems)
    loads = Loads(AHEAD)
    order = [1, n - 1, *range(2, n - 1), 0]

    def spot(k):
        to = lax.rem(scalars[1] + k, n)
        return to, pl.ds(pl.multiple_of(to * block, block), block)

    for k in order:
        loads.add(lambda k=k: fetch_weight(copies, w_ref, scalars[0], spot(k)[1], w.at[k]))
    loads.begin()
    put_rows((upper, lower), x)
    line = lax.broadcasted_iota(jnp.int32, (more - rows, vlocal), 0)
    for k in order:
        to, columns = spot(k)
        loads.next()
        total = acc_ref[:, columns] + jnp.dot(x[...], w[k], preferred_element_type=F32)
        total = total.astype(BF16)
        for h in range(own):
            outs[k][h, :rows] = total[:, h * vlocal : (h + 1) * vlocal]
            tail = jnp.zeros((more - rows, vlocal), F32)
            for m, part in enumerate(parts_of(gain_ref[pl.ds(to * own + h, 1), :])):
                tail = jnp.where(line == m, part, tail)
            outs[k][h, rows:] = tail.astype(BF16)


def values_by_device(halves, index, me, w, acc, gain, own, after):
    rows, cols = acc.shape
    chunk = halves[0].shape[1]
    vlocal = gain.shape[1]
    block = own * vlocal
    steps = cols // block
    shape = (own, rows + 16, vlocal)
    vmem = pl.BlockSpec(memory_space=pltpu.VMEM)
    return pl.pallas_call(
        values_kernel,
        in_specs=[
            pl.BlockSpec(memory_space=pltpu.SMEM),
            vmem,
            vmem,
            pl.BlockSpec(memory_space=pl.ANY),
            vmem,
            vmem,
            pl.BlockSpec(memory_space=pl.ANY),
        ],
        out_specs=[vmem] * steps,
        out_shape=[jax.ShapeDtypeStruct(shape, BF16)] * steps,
        scratch_shapes=[
            pltpu.VMEM((rows, chunk), BF16),
            pltpu.VMEM((steps, chunk, block), BF16),
            pltpu.SemaphoreType.DMA((steps,)),
        ],
        compiler_params=params(),
        cost_estimate=cost(2 * rows * chunk * cols, 2 * chunk * (cols + rows) + 6 * rows * cols),
    )(jnp.stack([index, me]), *halves, w, acc, gain, after)


def exchanged(pieces):
    return [pieces[0], around(pieces[1], 1), around(pieces[3], -1), around(pieces[2], 2)]


def within_kernel(counts, scalars, *refs):
    pieces = iter(refs[: sum(counts)])
    wg_ref, bias_ref, q_ref, k_ref, kwt_ref, p_ref, stat_ref, mark_ref = refs[sum(counts) :]
    own, rows, _ = p_ref.shape
    qsize = q_ref.shape[1] // own
    chunk = refs[0].shape[1]
    g = bias_ref[...]
    for n, count in enumerate(counts):
        w = wg_ref[pl.ds(pl.multiple_of(scalars[n] * chunk, chunk), chunk), :]
        terms = []
        for _ in range(count):
            x = next(pieces)[: rows // count]
            terms.append(jnp.dot(x, w, preferred_element_type=F32))
        g = g + (terms[0] if count == 1 else jnp.concatenate(terms, axis=0))
    logf = jnp.minimum(g, 0.0) - jnp.log1p(jnp.exp(-jnp.abs(g)))
    late = lax.broadcasted_iota(jnp.int32, (rows, rows), 0)
    early = lax.broadcasted_iota(jnp.int32, (rows, rows), 1)
    causal = late >= early
    cumb = jnp.dot(
        causal.astype(F32), logf, precision=lax.Precision.HIGHEST, preferred_element_type=F32
    )
    cumb = pltpu.roll(cumb, LANES - own, axis=1)
    gap = g - cumb
    gap_rows = gap.T
    most = jnp.max(gap, axis=0, keepdims=True)
    total = cumb[rows - 1 : rows]
    mark_ref[...] = jnp.concatenate([total + most, total, jnp.zeros((6, LANES), F32)], axis=0)
    lane = lax.broadcasted_iota(jnp.int32, (rows, LANES), 1)
    stat = jnp.zeros((rows, LANES), F32)
    for h in range(own):
        q = q_ref[:, h * qsize : (h + 1) * qsize]
        k = k_ref[:, h * qsize : (h + 1) * qsize]
        seen = jnp.where(causal, gap_rows[h : h + 1, :], F32(NEVER))
        high = jnp.max(seen, axis=1, keepdims=True)
        score = lax.dot_general(q, k, (((1,), (1,)), ((), ())), preferred_element_type=F32)
        wts = jnp.exp(seen - high) * (score * qsize ** (-0.5))
        wts = jnp.where(causal, wts, 0.0).astype(BF16)
        p_ref[h] = wts
        denom = jnp.sum(wts.astype(F32), axis=1, keepdims=True)
        stat = jnp.where(lane == h, high, jnp.where(lane == own + h, denom, stat))
        fall = jnp.exp(gap[:, h : h + 1] - most[:, h : h + 1])
        kw = (k.astype(F32) * fall).astype(BF16)
        kwt_ref[h * qsize : (h + 1) * qsize] = kw.astype(F32).T.astype(BF16)
    stat_ref[...] = stat


def within(groups, index, wg, bias, q, k, own):
    rows, width = q.shape
    pieces = [x for g in groups for x in g]
    vmem = pl.BlockSpec(memory_space=pltpu.VMEM)
    return pl.pallas_call(
        functools.partial(within_kernel, [len(g) for g in groups]),
        in_specs=[pl.BlockSpec(memory_space=pltpu.SMEM)] + [vmem] * (len(pieces) + 4),
        out_specs=[vmem] * 4,
        out_shape=[
            jax.ShapeDtypeStruct((width, rows), BF16),
            jax.ShapeDtypeStruct((own, rows, rows), BF16),
            jax.ShapeDtypeStruct((rows, LANES), F32),
            jax.ShapeDtypeStruct((8, LANES), F32),
        ],
        compiler_params=params(),
        cost_estimate=cost(4 * rows * rows * width, 8 * rows * width, own * rows * rows),
    )(jnp.stack(list(index)), *pieces, wg, bias, q, k)


def parts_of(x):
    hi = x.astype(BF16).astype(F32)
    mid = (x - hi).astype(BF16).astype(F32)
    return [hi, mid, x - hi - mid]


def of_head(head, rows):
    return jnp.where(head == 0, rows[:, 0:1], rows[:, 1:2])


def marked(extra, top, total):
    lane = lax.broadcasted_iota(jnp.int32, extra.shape, 1)
    for n, x in enumerate(parts_of(top) + ([] if total is None else parts_of(total))):
        extra = jnp.where(lane == 1 + n, x, extra)
    return extra


def marks_of(extra):
    top = extra[:, 1:2] + extra[:, 2:3] + extra[:, 3:4]
    total = extra[:, 4:5] + extra[:, 5:6] + extra[:, 6:7]
    return top, total


def summary_kernel(scalars, kwt_ref, mark_ref, v0, v1, v2, v3, mine, other, v_ref, gain_ref):
    vlocal = v0.shape[2]
    own, rows, vsize = v_ref.shape
    gain_ref[...] = jnp.zeros_like(gain_ref)
    qsize = kwt_ref.shape[0] // own
    for n, ref in enumerate((v0, v1, v2, v3)):
        at = pl.multiple_of(scalars[n] * vlocal, vlocal)
        for h in range(own):
            v_ref[h, :, pl.ds(at, vlocal)] = ref[h, :rows]
            tail = ref[h, rows:].astype(F32)
            gain_ref[h : h + 1, pl.ds(at, vlocal)] = tail[0:1] + tail[1:2] + tail[2:3]
    lane = lax.broadcasted_iota(jnp.int32, (qsize, LANES), 1)
    core = scalars[4]
    for h, out in ((core, mine), (1 - core, other)):
        kwt = kwt_ref[pl.ds(pl.multiple_of(h * qsize, qsize), qsize), :]
        out[:, :vsize] = jnp.dot(kwt, v_ref[h], preferred_element_type=F32).astype(BF16)
        extra = jnp.where(lane == 0, jnp.sum(kwt.astype(F32), axis=1, keepdims=True), 0.0)
        top, total = of_head(h, mark_ref[0:1, :]), of_head(h, mark_ref[1:2, :])
        out[:, vsize:] = marked(extra, top, total).astype(BF16)


def summary(index, core, kwt, mark, pieces):
    own, _, vlocal = pieces[0].shape
    rows = kwt.shape[1]
    vsize = vlocal * len(pieces)
    whole = lambda shape: pl.BlockSpec(shape, lambda j, s: (0,) * len(shape))
    shapes = [((kwt.shape[0] // own, vsize + LANES), BF16)] * 2
    shapes += [((own, rows, vsize), BF16), ((8, vsize), F32)]
    return pl.pallas_call(
        summary_kernel,
        grid_spec=pltpu.PrefetchScalarGridSpec(
            num_scalar_prefetch=1,
            grid=(1,),
            in_specs=[whole(kwt.shape), whole(mark.shape)] + [whole(x.shape) for x in pieces],
            out_specs=[whole(shape) for shape, _ in shapes],
        ),
        out_shape=[jax.ShapeDtypeStruct(shape, dtype) for shape, dtype in shapes],
        compiler_params=params(32),
        cost_estimate=cost(2 * kwt.size * vsize, 3 * own * rows * vsize * 2),
    )(jnp.stack(list(index) + [core]), kwt, mark, *pieces)


def pair_kernel(scalars, mine, got, out):
    first = scalars[0] == 0
    body = mine.shape[1] - LANES
    a, b = mine[:, body:].astype(F32), got[:, body:].astype(F32)
    early, late = jnp.where(first, a, b), jnp.where(first, b, a)
    (etop, etotal), (ltop, ltotal) = marks_of(early), marks_of(late)
    top = jnp.maximum(etop + ltotal, ltop)
    fe, fl = jnp.exp(etop + ltotal - top), jnp.exp(ltop - top)
    fa, fb = jnp.where(first, fe, fl), jnp.where(first, fl, fe)
    state = fa * mine[:, :body].astype(F32) + fb * got[:, :body].astype(F32)
    out[:, :body] = state.astype(BF16)
    out[:, body:] = marked(fa * a + fb * b, top, etotal + ltotal).astype(BF16)


def pair(core, mine, got):
    vmem = pl.BlockSpec(memory_space=pltpu.VMEM)
    return pl.pallas_call(
        pair_kernel,
        in_specs=[pl.BlockSpec(memory_space=pltpu.SMEM), vmem, vmem],
        out_specs=vmem,
        out_shape=jax.ShapeDtypeStruct(mine.shape, BF16),
        compiler_params=params(32),
        cost_estimate=cost(4 * mine.size, 6 * mine.size),
    )(jnp.stack([core]), mine, got)


def unpair_kernel(scalars, prefix, mine, got, keep, send):
    first = scalars[0] == 0
    body = mine.shape[1] - LANES
    p = prefix[:, body:].astype(F32)
    s = jnp.where(first, mine[:, body:].astype(F32), got[:, body:].astype(F32))
    ptop, _ = marks_of(p)
    stop, stotal = marks_of(s)
    top = jnp.maximum(ptop + stotal, stop)
    fp, fs = jnp.exp(ptop + stotal - top), jnp.exp(stop - top)
    state = jnp.where(first, mine[:, :body], got[:, :body]).astype(F32)
    state = (fp * prefix[:, :body].astype(F32) + fs * state).astype(BF16)
    extra = marked(fp * p + fs * s, top, None).astype(BF16)
    keep[:, :body] = jnp.where(first, prefix[:, :body], state)
    send[:, :body] = jnp.where(first, state, prefix[:, :body])
    keep[:, body:] = jnp.where(first, prefix[:, body:], extra)
    send[:, body:] = jnp.where(first, extra, prefix[:, body:])


def unpair(core, prefix, mine, got):
    vmem = pl.BlockSpec(memory_space=pltpu.VMEM)
    return pl.pallas_call(
        unpair_kernel,
        in_specs=[pl.BlockSpec(memory_space=pltpu.SMEM)] + [vmem] * 3,
        out_specs=[vmem] * 2,
        out_shape=[jax.ShapeDtypeStruct(mine.shape, BF16)] * 2,
        compiler_params=params(32),
        cost_estimate=cost(4 * mine.size, 10 * mine.size),
    )(jnp.stack([core]), prefix, mine, got)


def inside_kernel(p_ref, v_ref, out_ref):
    for h in range(p_ref.shape[0]):
        out_ref[h] = jnp.dot(p_ref[h], v_ref[h], preferred_element_type=F32)


def inside(p, v):
    return pl.pallas_call(
        inside_kernel,
        out_shape=jax.ShapeDtypeStruct(v.shape, F32),
        compiler_params=params(32),
        cost_estimate=cost(2 * p.size * v.shape[2], 6 * v.size),
    )(p, v)


def prefix_kernel(got_ref, out_ref):
    blocks, cut, width = got_ref.shape
    body = width - LANES
    lane = lax.broadcasted_iota(jnp.int32, (cut, LANES), 1)
    source = lax.broadcasted_iota(jnp.int32, (LANES, 2 * LANES), 0)
    target = lax.broadcasted_iota(jnp.int32, (LANES, 2 * LANES), 1)
    first = jnp.where(target < LANES, 1, 4)
    spread = ((source >= first) & (source < first + 3)).astype(F32).astype(BF16)
    marks = jnp.dot(
        got_ref[:, :, body:].reshape(blocks * cut, LANES), spread, preferred_element_type=F32
    )
    state = [jnp.zeros((cut, LANES), F32) for _ in range(width // LANES)]
    ptop = jnp.full((cut, LANES), NEVER, F32)
    for b in range(blocks):
        held = state[-1]
        for n, x in enumerate(parts_of(ptop)):
            held = jnp.where(lane == 1 + n, x, held)
        for n, x in enumerate(state[:-1] + [held]):
            out_ref[b, :, n * LANES : (n + 1) * LANES] = x.astype(BF16)
        if b == blocks - 1:
            break
        top = marks[b * cut : (b + 1) * cut, :LANES]
        total = marks[b * cut : (b + 1) * cut, LANES:]
        new = jnp.maximum(ptop + total, top)
        keep = jnp.exp(ptop + total - new)
        add = jnp.exp(top - new)
        state = [
            keep * x + add * got_ref[b, :, n * LANES : (n + 1) * LANES].astype(F32)
            for n, x in enumerate(state)
        ]
        ptop = new


def prefixes(got):
    return pl.pallas_call(
        prefix_kernel,
        out_shape=jax.ShapeDtypeStruct(got.shape, BF16),
        compiler_params=params(32),
        cost_estimate=cost(4 * got.size, 4 * got.size),
    )(got)


def finish_kernel(scalars, q_ref, mine, got, numer_ref, stat_ref, gain_ref, upper, lower):
    own, rows, vsize = numer_ref.shape
    qsize = q_ref.shape[1] // own
    core = scalars[0]
    for h, prefix_ref in ((core, mine), (1 - core, got)):
        q = q_ref[:, pl.ds(pl.multiple_of(h * qsize, qsize), qsize)]
        inter = jnp.dot(q, prefix_ref[...], preferred_element_type=F32)
        ptop, _ = marks_of(prefix_ref[0:16, vsize:].astype(F32)[0:1])
        high = of_head(h, stat_ref[...])
        top = jnp.maximum(high, ptop)
        fade = jnp.exp(high - top)
        decay = jnp.exp(ptop - top) * qsize ** (-0.5)
        denom = of_head(h, stat_ref[:, own : 2 * own])
        denom = denom * fade + inter[:, vsize : vsize + 1] * decay
        share = 1.0 / jnp.maximum(jnp.abs(denom), 1.0)
        hidden = numer_ref[h] * (fade * share) + inter[:, :vsize] * (decay * share)
        mean = jnp.mean(hidden, axis=1, keepdims=True)
        msq = jnp.mean(hidden * hidden, axis=1, keepdims=True)
        gain = gain_ref[pl.ds(h, 1), :]
        normed = (hidden - mean) * lax.rsqrt(msq - mean * mean + 1e-06) * gain
        normed = normed.astype(BF16)
        columns = pl.ds(pl.multiple_of(h * vsize, vsize), vsize)
        upper[:, columns] = normed[: rows // 2]
        lower[:, columns] = normed[rows // 2 :]


def finish(core, q, mine, got, numer, stat, gain):
    own, rows, vsize = numer.shape
    vmem = pl.BlockSpec(memory_space=pltpu.VMEM)
    return pl.pallas_call(
        finish_kernel,
        in_specs=[pl.BlockSpec(memory_space=pltpu.SMEM)] + [vmem] * 6,
        out_specs=[vmem] * 2,
        out_shape=[jax.ShapeDtypeStruct((rows // 2, own * vsize), BF16)] * 2,
        compiler_params=params(32),
        cost_estimate=cost(2 * q.size * vsize, 8 * numer.size),
    )(jnp.stack([core]), q, mine, got, numer, stat, gain)


def per_device(tokens, w_query, w_key, w_value, w_gate, gate_bias, norm_gain, w_out):
    me = lax.axis_index("val")
    nval = lax.axis_size("val")
    place = lax.axis_index("seq")
    blocks = lax.axis_size("seq")
    rows, chunk = tokens.shape
    width = w_query.shape[0]
    heads, vlocal = w_value.shape[1:]
    own = heads // nval
    qsize = w_query.shape[1] // own
    vsize = vlocal * nval
    index = [(me + d) % nval for d in (0, nval - 1, 1, 2)]

    half = rows // 2
    upper, lower = moved([tokens], [[(0, 0, half)], [(0, half, half)]], [])
    ring = Ring(upper, lower, [upper, lower])
    wg = lax.dynamic_slice_in_dim(w_gate, me * own, own, axis=2).reshape(width, 2 * own)
    wg = jnp.pad(wg, ((0, 0), (0, LANES - 2 * own)))
    bias = lax.dynamic_slice_in_dim(gate_bias, me * own, own, axis=1).reshape(1, 2 * own)
    bias = jnp.pad(bias, ((0, 0), (0, LANES - 2 * own)))
    wv, early = flat(w_value, 0)
    ring.second([early, wg])
    wv, late = flat(w_value, 1, wv)
    ring.forward([late])
    groups = [(tokens,), ring.left, ring.right]
    acc = product(rows, groups, index[:3], [wv], [F32])[0]
    core = place % 2
    cores = [(i, i ^ 1) for i in range(blocks)]
    kept, away, *pieces = cut_by_device(
        w_out.reshape(heads * vlocal, -1), me, core, nval, [acc]
    )
    values = values_by_device(ring.opposite, index[3], me, wv, acc, norm_gain, own, kept)
    halves = exchanged([None, *tied(pieces, values[:1])])[1:]
    groups.append(ring.opposite)
    q, k = product(rows, groups, index, [w_query, w_key], [BF16] * 2, values[:1])

    values = exchanged(values)
    kwt, p, stat, mark = within(groups, index, wg, bias, q, k, own)
    mine, other, v, gain = summary(index, core, kwt, mark, values)
    got = lax.ppermute(other, "seq", cores)
    chips = [list(range(n, blocks, 2)) for n in range(2)]
    sliced = (blocks // 2, -1, vsize + LANES)
    both = pair(core, mine, got).reshape(sliced)
    both = lax.all_to_all(both, "seq", 0, 0, axis_index_groups=chips)
    numer = inside(p, v)
    prefix = lax.all_to_all(prefixes(both), "seq", 0, 0, axis_index_groups=chips)
    keep, send = unpair(core, prefix.reshape(mine.shape), mine, got)
    came = lax.ppermute(send, "seq", cores)
    upper, lower = finish(core, q, keep, came, numer, stat, gain)

    ring = Ring(upper, lower, [upper, lower])
    halves = tied(halves, [upper])
    others = [lax.ppermute(x, "seq", cores) for x in halves]
    ring.second(others)
    ring.forward()
    halves, others = [kept, *halves], [away, *others]
    groups = [ring.own, ring.left, ring.right]
    weights = (index, core, halves, others)
    acc = out_product(rows, groups, index[:3], *weights, None, F32)
    return out_product(rows, [ring.opposite], index[3:], *weights, acc, BF16)


def solution(mesh):
    placed = (
        P("seq", "val"),
        P(None, "val"),
        P(None, "val"),
        P(None, None, "val"),
        P(),
        P(),
        P(None, "val"),
        P(None, "val", None),
    )
    return jax.shard_map(
        per_device, mesh=mesh, in_specs=placed, out_specs=P("seq", "val"), check_vma=False
    )
```

```python
import functools

import jax
import jax.numpy as jnp
from jax import lax
from jax.experimental import pallas as pl
from jax.experimental.pallas import tpu as pltpu
from jax.sharding import PartitionSpec as P

F32 = jnp.float32
BF16 = jnp.bfloat16
LANES = 128
NEVER = -1e30
BLOCK = 512
AHEAD = 4


def around(x, distance):
    n = lax.axis_size("val")
    return lax.ppermute(x, "val", [(i, (i + distance) % n) for i in range(n)])


def params(mib=48):
    return pltpu.CompilerParams(vmem_limit_bytes=mib * 1024 * 1024)


def cost(flops, nbytes, exps=0):
    return pl.CostEstimate(flops=flops, bytes_accessed=nbytes, transcendentals=exps)


class Ring:
    def __init__(self, plus, minus, later):
        self.own = (plus, minus)
        self.plus, self.minus = around(plus, 1), around(minus, -1)
        self.later = later

    def second(self, after):
        plus, minus = moved(self.later, [[(1, 0, 0)], [(0, 0, 0)]], after)
        self.sent = plus
        self.left = (self.plus, around(plus, 1))
        self.right = (around(minus, -1), self.minus)

    def forward(self, after=()):
        self.plus, self.minus = tied([self.plus, self.minus], [self.sent, *after])
        self.left = (self.plus, self.left[1])
        self.right = (self.right[0], self.minus)
        self.opposite = (around(self.plus, 1), around(self.minus, -1))


def tied_kernel(with_mark, *refs):
    if with_mark:
        refs[-1][...] = jnp.zeros_like(refs[-1])


def tied(arrays, after, with_mark=False):
    anywhere = pl.BlockSpec(memory_space=pl.ANY)
    marks = int(with_mark)
    return pl.pallas_call(
        functools.partial(tied_kernel, with_mark),
        in_specs=[anywhere] * (len(arrays) + len(after)),
        out_specs=[anywhere] * len(arrays) + [pl.BlockSpec(memory_space=pltpu.VMEM)] * marks,
        out_shape=[jax.ShapeDtypeStruct(x.shape, x.dtype) for x in arrays]
        + [jax.ShapeDtypeStruct((8, LANES), F32)] * marks,
        input_output_aliases={n: n for n in range(len(arrays))},
        compiler_params=params(),
    )(*arrays, *after)


def moved_kernel(n, n_after, plan, *refs):
    sources, outs = refs[:n], refs[n + n_after :]
    for out, parts in zip(outs, plan):
        at = 0
        for source, first, count in parts:
            count = count or sources[source].shape[0] - first
            out[at : at + count] = sources[source][first : first + count]
            at += count


def moved(arrays, plan, after):
    shapes = [sum(c or arrays[n].shape[0] - f for n, f, c in parts) for parts in plan]
    anywhere, vmem = (pl.BlockSpec(memory_space=m) for m in (pl.ANY, pltpu.VMEM))
    return pl.pallas_call(
        functools.partial(moved_kernel, len(arrays), len(after), plan),
        in_specs=[vmem] * len(arrays) + [anywhere] * len(after),
        out_specs=[vmem] * len(plan),
        out_shape=[
            jax.ShapeDtypeStruct((n, arrays[0].shape[1]), arrays[0].dtype) for n in shapes
        ],
        compiler_params=params(32),
        cost_estimate=cost(0, 4 * sum(shapes) * arrays[0].shape[1]),
    )(*arrays, *after)


def flat_kernel(n, w_ref, *refs):
    refs[-2][...] = w_ref[...].reshape(refs[-2].shape)
    refs[-1][...] = jnp.zeros_like(refs[-1])


def flat(w, first, steps, before=None):
    rows, heads, size = w.shape
    block = rows // 8
    args = [w] if before is None else [w, before]
    return pl.pallas_call(
        functools.partial(flat_kernel, len(args)),
        grid=(steps,),
        in_specs=[
            pl.BlockSpec((block, heads, size), lambda j: (j + first, 0, 0)),
            pl.BlockSpec(memory_space=pl.ANY),
        ][: len(args)],
        out_specs=[
            pl.BlockSpec((block, heads * size), lambda j: (j + first, 0)),
            pl.BlockSpec((8, LANES), lambda j: (0, 0)),
        ],
        out_shape=[
            jax.ShapeDtypeStruct((rows, heads * size), w.dtype),
            jax.ShapeDtypeStruct((8, LANES), F32),
        ],
        input_output_aliases={} if before is None else {1: 0},
        compiler_params=params(),
        cost_estimate=cost(0, 2 * w.size * steps // 8),
    )(*args)


class Copies:
    def __init__(self, sems):
        self.sems = sems
        self.used = 0

    def start(self, source, target):
        copy = pltpu.make_async_copy(source, target, self.sems.at[self.used])
        self.used += 1
        copy.start()
        return copy


class Loads:
    def __init__(self, ahead):
        self.ahead = ahead
        self.waiting = []
        self.started = []

    def add(self, start):
        self.waiting.append(start)

    def begin(self):
        while self.waiting and len(self.started) <= self.ahead:
            self.started.append(self.waiting.pop(0)())

    def next(self):
        self.begin()
        for copy in self.started.pop(0):
            copy.wait()


def put_rows(pieces, buffer):
    n = buffer.shape[0] // len(pieces)
    for at, piece in enumerate(pieces):
        buffer[at * n : (at + 1) * n] = piece[:n]


def fetch_weight(copies, w, chunk, columns, target):
    n = target.shape[0]
    return [copies.start(w.at[pl.ds(pl.multiple_of(chunk * n, n), n), columns], target)]


def product_kernel(counts, tasks, n_after, scalars, *refs):
    refs = list(refs)
    take = lambda n: [refs.pop(0) for _ in range(n)]
    ngroups, nweights = len(counts), 1 + max(n for n, *_ in tasks)
    groups = [take(n) for n in counts]
    weights = take(nweights)
    take(n_after)
    outs = take(nweights)
    x, ws, sems = refs
    copies = Copies(sems)
    chunk = x.shape[1] // ngroups
    part = lambda g: x.at[:, pl.ds(g * chunk, chunk)]

    def load(g, n, at, columns):
        target = ws.at[g, :, pl.ds(at, columns.size)]
        return fetch_weight(copies, weights[n], scalars[g], columns, target)

    loads = Loads(AHEAD)
    for task in tasks:
        for g in range(ngroups):
            loads.add(functools.partial(load, g, *task))
    loads.begin()
    for g in range(ngroups):
        put_rows(groups[g], part(g))
    for n, at, columns in tasks:
        total = None
        for g in range(ngroups):
            loads.next()
            w = ws[g, :, at : at + columns.size]
            term = jnp.dot(part(g)[...], w, preferred_element_type=F32)
            total = term if total is None else total + term
        outs[n][:, columns] = total.astype(outs[n].dtype)


def product(rows, groups, index, weights, dtypes, after=()):
    chunk = groups[0][0].shape[1]
    widths = [w.shape[1] for w in weights]
    tasks, held = [], 0
    for n, width in enumerate(widths):
        for at in range(0, width, BLOCK):
            tasks.append((n, held, pl.ds(at, BLOCK)))
            held += BLOCK
    anywhere, vmem = (pl.BlockSpec(memory_space=m) for m in (pl.ANY, pltpu.VMEM))
    pieces = [x for g in groups for x in g]
    cols = sum(widths)
    return pl.pallas_call(
        functools.partial(product_kernel, [len(g) for g in groups], tasks, len(after)),
        in_specs=[pl.BlockSpec(memory_space=pltpu.SMEM)]
        + [vmem] * len(pieces)
        + [anywhere] * (len(weights) + len(after)),
        out_specs=[vmem] * len(weights),
        out_shape=[jax.ShapeDtypeStruct((rows, n), d) for n, d in zip(widths, dtypes)],
        scratch_shapes=[
            pltpu.VMEM((rows, len(groups) * chunk), BF16),
            pltpu.VMEM((len(groups), chunk, held), BF16),
            pltpu.SemaphoreType.DMA((len(tasks) * len(groups),)),
        ],
        compiler_params=params(),
        cost_estimate=cost(
            2 * rows * chunk * len(groups) * cols,
            2 * chunk * len(groups) * (cols + rows) + 4 * rows * cols,
        ),
    )(jnp.stack(list(index)), *pieces, *weights, *after)


def cut_kernel(n_after, scalars, w_ref, *refs):
    outs, mark, sems = refs[n_after:-2], refs[-2], refs[-1]
    copies = Copies(sems)
    cols = outs[0].shape[1]
    n = w_ref.shape[1] // (2 * cols)
    started = []
    for to, out in enumerate(outs):
        at = 2 * lax.rem(scalars[0] + 1 + to, n) + scalars[1]
        started.append(
            copies.start(w_ref.at[:, pl.ds(pl.multiple_of(at * cols, cols), cols)], out)
        )
    mark[...] = jnp.zeros_like(mark)
    for copy in started:
        copy.wait()


def cut_by_device(w, me, core, nval, after):
    rows, cols = w.shape[0], w.shape[1] // (2 * nval)
    anywhere, vmem = (pl.BlockSpec(memory_space=m) for m in (pl.ANY, pltpu.VMEM))
    return pl.pallas_call(
        functools.partial(cut_kernel, len(after)),
        in_specs=[pl.BlockSpec(memory_space=pltpu.SMEM)] + [anywhere] * (1 + len(after)),
        out_specs=[vmem] * nval,
        out_shape=[jax.ShapeDtypeStruct((rows, cols), w.dtype)] * (nval - 1)
        + [jax.ShapeDtypeStruct((8, LANES), F32)],
        scratch_shapes=[pltpu.SemaphoreType.DMA((nval - 1,))],
        compiler_params=params(),
        cost_estimate=cost(0, 4 * rows * cols * (nval - 1)),
    )(jnp.stack([me, core]), w, *after)


def out_kernel(counts, with_total, scalars, *refs):
    refs = list(refs)
    take = lambda n: [refs.pop(0) for _ in range(n)]
    ngroups = len(counts)
    groups = [take(n) for n in counts]
    (local,) = take(1)
    halves = [take(3), take(3)]
    total_ref = take(1)[0] if with_total else None
    out, x, ws, held, sems, out_sems = refs
    copies, out_copies = Copies(sems), Copies(out_sems)
    sources = [scalars[ngroups + n] for n in range(4)]
    core = scalars[ngroups + 4]
    chunk = x.shape[1] // ngroups
    cols, vlocal = ws.shape[2], chunk // 8
    row = lambda n: pl.ds(pl.multiple_of(n * vlocal, vlocal), vlocal)

    sides = (core, 1 - core)

    def load(t):
        at = (2 * sources[0] + sides[t]) * cols
        mine = local.at[:, pl.ds(pl.multiple_of(at, cols), cols)]
        started = []
        for g in range(ngroups):
            for n, w in enumerate([mine, *halves[t]]):
                for h in range(2):
                    to = row(g * 8 + h * 4 + sources[n])
                    source = w.at[row(scalars[g] * 2 + h), :]
                    started.append(copies.start(source, ws.at[t, to, :]))
        return started

    started = [load(t) for t in range(2)]
    for g in range(ngroups):
        put_rows(groups[g], x.at[:, pl.ds(g * chunk, chunk)])
    last = []
    for t, side in enumerate(sides):
        columns = pl.ds(pl.multiple_of(side * cols, cols), cols)
        for copy in started[t]:
            copy.wait()
        total = jnp.dot(x[...], ws[t], preferred_element_type=F32)
        if with_total:
            total = total + total_ref[:, columns]
        held[t] = total.astype(held.dtype)
        last.append(out_copies.start(held.at[t], out.at[:, columns]))
    for copy in last:
        copy.wait()


def out_product(rows, groups, index, sources, core, local, mine, others, total, dtype):
    chunk = groups[0][0].shape[1]
    cols = mine[0].shape[1]
    anywhere, vmem = (pl.BlockSpec(memory_space=m) for m in (pl.ANY, pltpu.VMEM))
    pieces = [x for g in groups for x in g]
    totals = [] if total is None else [total]
    args = [*pieces, local, *mine, *others, *totals]
    n = len(groups)
    return pl.pallas_call(
        functools.partial(out_kernel, [len(g) for g in groups], total is not None),
        in_specs=[pl.BlockSpec(memory_space=pltpu.SMEM)]
        + [vmem] * len(pieces)
        + [anywhere] * 7
        + [vmem] * len(totals),
        out_specs=anywhere,
        out_shape=jax.ShapeDtypeStruct((rows, 2 * cols), dtype),
        scratch_shapes=[
            pltpu.VMEM((rows, n * chunk), BF16),
            pltpu.VMEM((2, n * chunk, cols), BF16),
            pltpu.VMEM((2, rows, cols), dtype),
            pltpu.SemaphoreType.DMA((16 * n,)),
            pltpu.SemaphoreType.DMA((2,)),
        ],
        compiler_params=params(56),
        cost_estimate=cost(4 * rows * chunk * n * cols, 4 * chunk * n * cols + 8 * rows * cols),
    )(jnp.stack(list(index) + list(sources) + [core]), *args)


def values_kernel(scalars, upper, lower, w_ref, acc_ref, gain_ref, after, *refs):
    n = len(refs) - 3
    outs, (x, w, sems) = refs[:n], refs[n:]
    own, more, vlocal = outs[0].shape
    rows, block = acc_ref.shape[0], own * vlocal
    copies = Copies(sems)
    loads = Loads(AHEAD)
    order = [1, n - 1, *range(2, n - 1), 0]

    def spot(k):
        to = lax.rem(scalars[1] + k, n)
        return to, pl.ds(pl.multiple_of(to * block, block), block)

    for k in order:
        loads.add(lambda k=k: fetch_weight(copies, w_ref, scalars[0], spot(k)[1], w.at[k]))
    loads.begin()
    put_rows((upper, lower), x)
    line = lax.broadcasted_iota(jnp.int32, (more - rows, vlocal), 0)
    for k in order:
        to, columns = spot(k)
        loads.next()
        total = acc_ref[:, columns] + jnp.dot(x[...], w[k], preferred_element_type=F32)
        total = total.astype(BF16)
        for h in range(own):
            outs[k][h, :rows] = total[:, h * vlocal : (h + 1) * vlocal]
            tail = jnp.zeros((more - rows, vlocal), F32)
            for m, part in enumerate(parts_of(gain_ref[pl.ds(to * own + h, 1), :])):
                tail = jnp.where(line == m, part, tail)
            outs[k][h, rows:] = tail.astype(BF16)


def values_by_device(halves, index, me, w, acc, gain, own, after):
    rows, cols = acc.shape
    chunk = halves[0].shape[1]
    vlocal = gain.shape[1]
    block = own * vlocal
    steps = cols // block
    shape = (own, rows + 16, vlocal)
    vmem = pl.BlockSpec(memory_space=pltpu.VMEM)
    return pl.pallas_call(
        values_kernel,
        in_specs=[
            pl.BlockSpec(memory_space=pltpu.SMEM),
            vmem,
            vmem,
            pl.BlockSpec(memory_space=pl.ANY),
            vmem,
            vmem,
            pl.BlockSpec(memory_space=pl.ANY),
        ],
        out_specs=[vmem] * steps,
        out_shape=[jax.ShapeDtypeStruct(shape, BF16)] * steps,
        scratch_shapes=[
            pltpu.VMEM((rows, chunk), BF16),
            pltpu.VMEM((steps, chunk, block), BF16),
            pltpu.SemaphoreType.DMA((steps,)),
        ],
        compiler_params=params(),
        cost_estimate=cost(2 * rows * chunk * cols, 2 * chunk * (cols + rows) + 6 * rows * cols),
    )(jnp.stack([index, me]), *halves, w, acc, gain, after)


def exchanged(pieces):
    return [pieces[0], around(pieces[1], 1), around(pieces[3], -1), around(pieces[2], 2)]


def within_kernel(counts, scalars, bias_ref, *refs):
    pieces = iter(refs[: sum(counts)])
    wg_ref, q_ref, k_ref, kwt_ref, p_ref, stat_ref, mark_ref, g_ref = refs[sum(counts) :]
    own, rows, _ = p_ref.shape
    qsize = q_ref.shape[1] // own
    chunk = refs[0].shape[1]
    heads = bias_ref.shape[1]
    gates = None
    for n, count in enumerate(counts):
        w = wg_ref[:, pl.ds(pl.multiple_of(scalars[n] * chunk, chunk), chunk)]
        x = [next(pieces)[: rows // count] for _ in range(count)]
        x = x[0] if count == 1 else jnp.concatenate(x, axis=0)
        term = lax.dot_general(w, x, (((1,), (1,)), ((), ())), preferred_element_type=F32)
        gates = term if gates is None else gates + term
    g_ref[...] = gates
    late = lax.broadcasted_iota(jnp.int32, (rows, rows), 0)
    early = lax.broadcasted_iota(jnp.int32, (rows, rows), 1)
    causal = late >= early
    line = lax.broadcasted_iota(jnp.int32, (8, rows), 0)
    igate, forget = jnp.zeros((8, rows), F32), jnp.zeros((8, rows), F32)
    for h in range(own):
        head = scalars[0] * own + h
        igate = jnp.where(line == h, g_ref[pl.ds(head, 1), :] + bias_ref[0, head], igate)
        row = g_ref[pl.ds(heads + head, 1), :] + bias_ref[1, head]
        forget = jnp.where(line == h, row, forget)
    logf = jnp.minimum(forget, 0.0) - jnp.log1p(jnp.exp(-jnp.abs(forget)))
    cumb = jnp.dot(
        logf,
        (early >= late).astype(F32),
        precision=lax.Precision.HIGHEST,
        preferred_element_type=F32,
    )
    gap_rows = igate - cumb
    both = jnp.concatenate([gap_rows, cumb, jnp.zeros((LANES - 16, rows), F32)], axis=0).T
    gap = both
    most = jnp.max(gap, axis=0, keepdims=True)
    total = pltpu.roll(both[rows - 8 : rows], LANES - 8, axis=1)[7:8]
    mark_ref[...] = jnp.concatenate([total + most, total, jnp.zeros((6, LANES), F32)], axis=0)
    lane = lax.broadcasted_iota(jnp.int32, (rows, LANES), 1)
    stat = jnp.zeros((rows, LANES), F32)
    for h in range(own):
        q = q_ref[:, h * qsize : (h + 1) * qsize]
        k = k_ref[:, h * qsize : (h + 1) * qsize]
        seen = jnp.where(causal, gap_rows[h : h + 1, :], F32(NEVER))
        high = jnp.max(seen, axis=1, keepdims=True)
        score = lax.dot_general(q, k, (((1,), (1,)), ((), ())), preferred_element_type=F32)
        wts = jnp.exp(seen - high) * (score * qsize ** (-0.5))
        wts = jnp.where(causal, wts, 0.0).astype(BF16)
        p_ref[h] = wts
        denom = jnp.sum(wts.astype(F32), axis=1, keepdims=True)
        stat = jnp.where(lane == h, high, jnp.where(lane == own + h, denom, stat))
        fall = jnp.exp(gap[:, h : h + 1] - most[:, h : h + 1])
        kw = (k.astype(F32) * fall).astype(BF16)
        kwt_ref[h * qsize : (h + 1) * qsize] = kw.astype(F32).T.astype(BF16)
    stat_ref[...] = stat


def within(groups, index, wg, bias, q, k, own):
    rows, width = q.shape
    pieces = [x for g in groups for x in g]
    vmem = pl.BlockSpec(memory_space=pltpu.VMEM)
    return pl.pallas_call(
        functools.partial(within_kernel, [len(g) for g in groups]),
        in_specs=[pl.BlockSpec(memory_space=pltpu.SMEM)] * 2 + [vmem] * (len(pieces) + 3),
        out_specs=[vmem] * 4,
        out_shape=[
            jax.ShapeDtypeStruct((width, rows), BF16),
            jax.ShapeDtypeStruct((own, rows, rows), BF16),
            jax.ShapeDtypeStruct((rows, LANES), F32),
            jax.ShapeDtypeStruct((8, LANES), F32),
        ],
        scratch_shapes=[pltpu.VMEM((wg.shape[0], rows), F32)],
        compiler_params=params(),
        cost_estimate=cost(4 * rows * rows * width, 8 * rows * width, own * rows * rows),
    )(jnp.stack(list(index)), bias, *pieces, wg, q, k)


def parts_of(x):
    hi = x.astype(BF16).astype(F32)
    mid = (x - hi).astype(BF16).astype(F32)
    return [hi, mid, x - hi - mid]


def of_head(head, rows):
    return jnp.where(head == 0, rows[:, 0:1], rows[:, 1:2])


def marked(extra, top, total):
    lane = lax.broadcasted_iota(jnp.int32, extra.shape, 1)
    for n, x in enumerate(parts_of(top) + ([] if total is None else parts_of(total))):
        extra = jnp.where(lane == 1 + n, x, extra)
    return extra


def marks_of(extra):
    top = extra[:, 1:2] + extra[:, 2:3] + extra[:, 3:4]
    total = extra[:, 4:5] + extra[:, 5:6] + extra[:, 6:7]
    return top, total


def summary_kernel(scalars, kwt_ref, mark_ref, v0, v1, v2, v3, mine, other, v_ref, gain_ref):
    vlocal = v0.shape[2]
    own, rows, vsize = v_ref.shape
    gain_ref[...] = jnp.zeros_like(gain_ref)
    qsize = kwt_ref.shape[0] // own
    for n, ref in enumerate((v0, v1, v2, v3)):
        at = pl.multiple_of(scalars[n] * vlocal, vlocal)
        for h in range(own):
            v_ref[h, :, pl.ds(at, vlocal)] = ref[h, :rows]
            tail = ref[h, rows:].astype(F32)
            gain_ref[h : h + 1, pl.ds(at, vlocal)] = tail[0:1] + tail[1:2] + tail[2:3]
    lane = lax.broadcasted_iota(jnp.int32, (qsize, LANES), 1)
    core = scalars[4]
    for h, out in ((core, mine), (1 - core, other)):
        kwt = kwt_ref[pl.ds(pl.multiple_of(h * qsize, qsize), qsize), :]
        out[:, :vsize] = jnp.dot(kwt, v_ref[h], preferred_element_type=F32).astype(BF16)
        extra = jnp.where(lane == 0, jnp.sum(kwt.astype(F32), axis=1, keepdims=True), 0.0)
        top, total = of_head(h, mark_ref[0:1, :]), of_head(h, mark_ref[1:2, :])
        out[:, vsize:] = marked(extra, top, total).astype(BF16)


def summary(index, core, kwt, mark, pieces):
    own, _, vlocal = pieces[0].shape
    rows = kwt.shape[1]
    vsize = vlocal * len(pieces)
    whole = lambda shape: pl.BlockSpec(shape, lambda j, s: (0,) * len(shape))
    shapes = [((kwt.shape[0] // own, vsize + LANES), BF16)] * 2
    shapes += [((own, rows, vsize), BF16), ((8, vsize), F32)]
    return pl.pallas_call(
        summary_kernel,
        grid_spec=pltpu.PrefetchScalarGridSpec(
            num_scalar_prefetch=1,
            grid=(1,),
            in_specs=[whole(kwt.shape), whole(mark.shape)] + [whole(x.shape) for x in pieces],
            out_specs=[whole(shape) for shape, _ in shapes],
        ),
        out_shape=[jax.ShapeDtypeStruct(shape, dtype) for shape, dtype in shapes],
        compiler_params=params(32),
        cost_estimate=cost(2 * kwt.size * vsize, 3 * own * rows * vsize * 2),
    )(jnp.stack(list(index) + [core]), kwt, mark, *pieces)


def pair_kernel(scalars, mine, got, out):
    first = scalars[0] == 0
    body = mine.shape[1] - LANES
    a, b = mine[:, body:].astype(F32), got[:, body:].astype(F32)
    early, late = jnp.where(first, a, b), jnp.where(first, b, a)
    (etop, etotal), (ltop, ltotal) = marks_of(early), marks_of(late)
    top = jnp.maximum(etop + ltotal, ltop)
    fe, fl = jnp.exp(etop + ltotal - top), jnp.exp(ltop - top)
    fa, fb = jnp.where(first, fe, fl), jnp.where(first, fl, fe)
    state = fa * mine[:, :body].astype(F32) + fb * got[:, :body].astype(F32)
    out[:, :body] = state.astype(BF16)
    out[:, body:] = marked(fa * a + fb * b, top, etotal + ltotal).astype(BF16)


def pair(core, mine, got):
    vmem = pl.BlockSpec(memory_space=pltpu.VMEM)
    return pl.pallas_call(
        pair_kernel,
        in_specs=[pl.BlockSpec(memory_space=pltpu.SMEM), vmem, vmem],
        out_specs=vmem,
        out_shape=jax.ShapeDtypeStruct(mine.shape, BF16),
        compiler_params=params(32),
        cost_estimate=cost(4 * mine.size, 6 * mine.size),
    )(jnp.stack([core]), mine, got)


def unpair_kernel(scalars, prefix, mine, got, keep, send):
    first = scalars[0] == 0
    body = mine.shape[1] - LANES
    p = prefix[:, body:].astype(F32)
    s = jnp.where(first, mine[:, body:].astype(F32), got[:, body:].astype(F32))
    ptop, _ = marks_of(p)
    stop, stotal = marks_of(s)
    top = jnp.maximum(ptop + stotal, stop)
    fp, fs = jnp.exp(ptop + stotal - top), jnp.exp(stop - top)
    state = jnp.where(first, mine[:, :body], got[:, :body]).astype(F32)
    state = (fp * prefix[:, :body].astype(F32) + fs * state).astype(BF16)
    extra = marked(fp * p + fs * s, top, None).astype(BF16)
    keep[:, :body] = jnp.where(first, prefix[:, :body], state)
    send[:, :body] = jnp.where(first, state, prefix[:, :body])
    keep[:, body:] = jnp.where(first, prefix[:, body:], extra)
    send[:, body:] = jnp.where(first, extra, prefix[:, body:])


def unpair(core, prefix, mine, got):
    vmem = pl.BlockSpec(memory_space=pltpu.VMEM)
    return pl.pallas_call(
        unpair_kernel,
        in_specs=[pl.BlockSpec(memory_space=pltpu.SMEM)] + [vmem] * 3,
        out_specs=[vmem] * 2,
        out_shape=[jax.ShapeDtypeStruct(mine.shape, BF16)] * 2,
        compiler_params=params(32),
        cost_estimate=cost(4 * mine.size, 10 * mine.size),
    )(jnp.stack([core]), prefix, mine, got)


def inside_kernel(p_ref, v_ref, out_ref):
    for h in range(p_ref.shape[0]):
        out_ref[h] = jnp.dot(p_ref[h], v_ref[h], preferred_element_type=F32)


def inside(p, v):
    return pl.pallas_call(
        inside_kernel,
        out_shape=jax.ShapeDtypeStruct(v.shape, F32),
        compiler_params=params(32),
        cost_estimate=cost(2 * p.size * v.shape[2], 6 * v.size),
    )(p, v)


def prefix_kernel(got_ref, out_ref):
    blocks, cut, width = got_ref.shape
    body = width - LANES
    lane = lax.broadcasted_iota(jnp.int32, (cut, LANES), 1)
    source = lax.broadcasted_iota(jnp.int32, (LANES, 2 * LANES), 0)
    target = lax.broadcasted_iota(jnp.int32, (LANES, 2 * LANES), 1)
    first = jnp.where(target < LANES, 1, 4)
    spread = ((source >= first) & (source < first + 3)).astype(F32).astype(BF16)
    marks = jnp.dot(
        got_ref[:, :, body:].reshape(blocks * cut, LANES), spread, preferred_element_type=F32
    )
    state = [jnp.zeros((cut, LANES), F32) for _ in range(width // LANES)]
    ptop = jnp.full((cut, LANES), NEVER, F32)
    for b in range(blocks):
        held = state[-1]
        for n, x in enumerate(parts_of(ptop)):
            held = jnp.where(lane == 1 + n, x, held)
        for n, x in enumerate(state[:-1] + [held]):
            out_ref[b, :, n * LANES : (n + 1) * LANES] = x.astype(BF16)
        if b == blocks - 1:
            break
        top = marks[b * cut : (b + 1) * cut, :LANES]
        total = marks[b * cut : (b + 1) * cut, LANES:]
        new = jnp.maximum(ptop + total, top)
        keep = jnp.exp(ptop + total - new)
        add = jnp.exp(top - new)
        state = [
            keep * x + add * got_ref[b, :, n * LANES : (n + 1) * LANES].astype(F32)
            for n, x in enumerate(state)
        ]
        ptop = new


def prefixes(got):
    return pl.pallas_call(
        prefix_kernel,
        out_shape=jax.ShapeDtypeStruct(got.shape, BF16),
        compiler_params=params(32),
        cost_estimate=cost(4 * got.size, 4 * got.size),
    )(got)


def finish_kernel(scalars, q_ref, mine, got, numer_ref, stat_ref, gain_ref, upper, lower):
    own, rows, vsize = numer_ref.shape
    qsize = q_ref.shape[1] // own
    core = scalars[0]
    for h, prefix_ref in ((core, mine), (1 - core, got)):
        q = q_ref[:, pl.ds(pl.multiple_of(h * qsize, qsize), qsize)]
        inter = jnp.dot(q, prefix_ref[...], preferred_element_type=F32)
        ptop, _ = marks_of(prefix_ref[0:16, vsize:].astype(F32)[0:1])
        high = of_head(h, stat_ref[...])
        top = jnp.maximum(high, ptop)
        fade = jnp.exp(high - top)
        decay = jnp.exp(ptop - top) * qsize ** (-0.5)
        denom = of_head(h, stat_ref[:, own : 2 * own])
        denom = denom * fade + inter[:, vsize : vsize + 1] * decay
        share = 1.0 / jnp.maximum(jnp.abs(denom), 1.0)
        hidden = numer_ref[h] * (fade * share) + inter[:, :vsize] * (decay * share)
        mean = jnp.mean(hidden, axis=1, keepdims=True)
        msq = jnp.mean(hidden * hidden, axis=1, keepdims=True)
        gain = gain_ref[pl.ds(h, 1), :]
        normed = (hidden - mean) * lax.rsqrt(msq - mean * mean + 1e-06) * gain
        normed = normed.astype(BF16)
        columns = pl.ds(pl.multiple_of(h * vsize, vsize), vsize)
        upper[:, columns] = normed[: rows // 2]
        lower[:, columns] = normed[rows // 2 :]


def finish(core, q, mine, got, numer, stat, gain):
    own, rows, vsize = numer.shape
    vmem = pl.BlockSpec(memory_space=pltpu.VMEM)
    return pl.pallas_call(
        finish_kernel,
        in_specs=[pl.BlockSpec(memory_space=pltpu.SMEM)] + [vmem] * 6,
        out_specs=[vmem] * 2,
        out_shape=[jax.ShapeDtypeStruct((rows // 2, own * vsize), BF16)] * 2,
        compiler_params=params(32),
        cost_estimate=cost(2 * q.size * vsize, 8 * numer.size),
    )(jnp.stack([core]), q, mine, got, numer, stat, gain)


def per_device(tokens, w_query, w_key, w_value, w_gate, gate_bias, norm_gain, w_out):
    me = lax.axis_index("val")
    nval = lax.axis_size("val")
    place = lax.axis_index("seq")
    blocks = lax.axis_size("seq")
    rows, chunk = tokens.shape
    width = w_query.shape[0]
    heads, vlocal = w_value.shape[1:]
    own = heads // nval
    qsize = w_query.shape[1] // own
    vsize = vlocal * nval
    index = [(me + d) % nval for d in (0, nval - 1, 1, 2)]

    half = rows // 2
    upper, lower = moved([tokens], [[(0, 0, half)], [(0, half, half)]], [])
    ring = Ring(upper, lower, [upper, lower])
    wg = w_gate.transpose(1, 2, 0).reshape(2 * heads, width)
    wv, early = flat(w_value, 0, 2)
    ring.second([early])
    wv, late = flat(w_value, 2, 2, wv)
    ring.forward([late])
    wv, _ = flat(w_value, 4, 4, wv)
    groups = [(tokens,), ring.left, ring.right]
    acc = product(rows, groups, index[:3], [wv], [F32])[0]
    core = place % 2
    cores = [(i, i ^ 1) for i in range(blocks)]
    local = w_out.reshape(heads * vlocal, -1)
    *pieces, mark = cut_by_device(local, me, core, nval, [acc])
    values = values_by_device(ring.opposite, index[3], me, wv, acc, norm_gain, own, mark)
    pieces = tied(pieces, values[:1])
    halves = exchanged([None, *pieces])[1:]
    groups.append(ring.opposite)
    q, k = product(rows, groups, index, [w_query, w_key], [BF16] * 2, values[:1])

    values = exchanged(values)
    kwt, p, stat, mark = within(groups, index, wg, gate_bias, q, k, own)
    mine, other, v, gain = summary(index, core, kwt, mark, values)
    got = lax.ppermute(other, "seq", cores)
    chips = [list(range(n, blocks, 2)) for n in range(2)]
    sliced = (blocks // 2, -1, vsize + LANES)
    both = pair(core, mine, got).reshape(sliced)
    both = lax.all_to_all(both, "seq", 0, 0, axis_index_groups=chips)
    numer = inside(p, v)
    prefix = lax.all_to_all(prefixes(both), "seq", 0, 0, axis_index_groups=chips)
    keep, send = unpair(core, prefix.reshape(mine.shape), mine, got)
    came = lax.ppermute(send, "seq", cores)
    upper, lower = finish(core, q, keep, came, numer, stat, gain)

    ring = Ring(upper, lower, [upper, lower])
    halves = tied(halves, [upper])
    others = [lax.ppermute(x, "seq", cores) for x in halves]
    *others, there = tied(others, [], with_mark=True)
    ring.second([there])
    ring.forward()
    groups = [ring.own, ring.left, ring.right]
    weights = (index, core, local, halves, others)
    acc = out_product(rows, groups, index[:3], *weights, None, F32)
    return out_product(rows, [ring.opposite], index[3:], *weights, acc, BF16)


def solution(mesh):
    placed = (
        P("seq", "val"),
        P(None, "val"),
        P(None, "val"),
        P(None, None, "val"),
        P(),
        P(),
        P(None, "val"),
        P(None, "val", None),
    )
    return jax.shard_map(
        per_device, mesh=mesh, in_specs=placed, out_specs=P("seq", "val"), check_vma=False
    )
```

```python
import functools

import jax
import jax.numpy as jnp
from jax import lax
from jax.experimental import pallas as pl
from jax.experimental.pallas import tpu as pltpu
from jax.sharding import PartitionSpec as P

F32 = jnp.float32
BF16 = jnp.bfloat16
LANES = 128
NEVER = -1e30
BLOCK = 512
AHEAD = 4


def around(x, distance):
    n = lax.axis_size("val")
    return lax.ppermute(x, "val", [(i, (i + distance) % n) for i in range(n)])


def params(mib=48):
    return pltpu.CompilerParams(vmem_limit_bytes=mib * 1024 * 1024)


def cost(flops, nbytes, exps=0):
    return pl.CostEstimate(flops=flops, bytes_accessed=nbytes, transcendentals=exps)


class Ring:
    def __init__(self, plus, minus, later):
        self.own = (plus, minus)
        self.plus, self.minus = around(plus, 1), around(minus, -1)
        self.later = later

    def second(self, after):
        plus, minus = moved(self.later, [[(1, 0, 0)], [(0, 0, 0)]], after)
        self.sent = plus
        self.left = (self.plus, around(plus, 1))
        self.right = (around(minus, -1), self.minus)

    def forward(self, after=()):
        self.plus, self.minus = tied([self.plus, self.minus], [self.sent, *after])
        self.left = (self.plus, self.left[1])
        self.right = (self.right[0], self.minus)
        self.opposite = (around(self.plus, 1), around(self.minus, -1))


def tied_kernel(with_mark, *refs):
    if with_mark:
        refs[-1][...] = jnp.zeros_like(refs[-1])


def tied(arrays, after, with_mark=False):
    anywhere = pl.BlockSpec(memory_space=pl.ANY)
    marks = int(with_mark)
    return pl.pallas_call(
        functools.partial(tied_kernel, with_mark),
        in_specs=[anywhere] * (len(arrays) + len(after)),
        out_specs=[anywhere] * len(arrays) + [pl.BlockSpec(memory_space=pltpu.VMEM)] * marks,
        out_shape=[jax.ShapeDtypeStruct(x.shape, x.dtype) for x in arrays]
        + [jax.ShapeDtypeStruct((8, LANES), F32)] * marks,
        input_output_aliases={n: n for n in range(len(arrays))},
        compiler_params=params(),
    )(*arrays, *after)


def moved_kernel(n, n_after, plan, *refs):
    sources, outs = refs[:n], refs[n + n_after :]
    for out, parts in zip(outs, plan):
        at = 0
        for source, first, count in parts:
            count = count or sources[source].shape[0] - first
            out[at : at + count] = sources[source][first : first + count]
            at += count


def moved(arrays, plan, after):
    shapes = [sum(c or arrays[n].shape[0] - f for n, f, c in parts) for parts in plan]
    anywhere, vmem = (pl.BlockSpec(memory_space=m) for m in (pl.ANY, pltpu.VMEM))
    return pl.pallas_call(
        functools.partial(moved_kernel, len(arrays), len(after), plan),
        in_specs=[vmem] * len(arrays) + [anywhere] * len(after),
        out_specs=[vmem] * len(plan),
        out_shape=[
            jax.ShapeDtypeStruct((n, arrays[0].shape[1]), arrays[0].dtype) for n in shapes
        ],
        compiler_params=params(32),
        cost_estimate=cost(0, 4 * sum(shapes) * arrays[0].shape[1]),
    )(*arrays, *after)


def flat_kernel(n, w_ref, *refs):
    refs[-2][...] = w_ref[...].reshape(refs[-2].shape)
    refs[-1][...] = jnp.zeros_like(refs[-1])


def flat(w, first, steps, before=None):
    rows, heads, size = w.shape
    block = rows // 8
    args = [w] if before is None else [w, before]
    return pl.pallas_call(
        functools.partial(flat_kernel, len(args)),
        grid=(steps,),
        in_specs=[
            pl.BlockSpec((block, heads, size), lambda j: (j + first, 0, 0)),
            pl.BlockSpec(memory_space=pl.ANY),
        ][: len(args)],
        out_specs=[
            pl.BlockSpec((block, heads * size), lambda j: (j + first, 0)),
            pl.BlockSpec((8, LANES), lambda j: (0, 0)),
        ],
        out_shape=[
            jax.ShapeDtypeStruct((rows, heads * size), w.dtype),
            jax.ShapeDtypeStruct((8, LANES), F32),
        ],
        input_output_aliases={} if before is None else {1: 0},
        compiler_params=params(),
        cost_estimate=cost(0, 2 * w.size * steps // 8),
    )(*args)


class Copies:
    def __init__(self, sems):
        self.sems = sems
        self.used = 0

    def start(self, source, target):
        copy = pltpu.make_async_copy(source, target, self.sems.at[self.used])
        self.used += 1
        copy.start()
        return copy


class Loads:
    def __init__(self, ahead):
        self.ahead = ahead
        self.waiting = []
        self.started = []

    def add(self, start):
        self.waiting.append(start)

    def begin(self):
        while self.waiting and len(self.started) <= self.ahead:
            self.started.append(self.waiting.pop(0)())

    def next(self):
        self.begin()
        for copy in self.started.pop(0):
            copy.wait()


def put_rows(pieces, buffer):
    n = buffer.shape[0] // len(pieces)
    for at, piece in enumerate(pieces):
        buffer[at * n : (at + 1) * n] = piece[:n]


def fetch_weight(copies, w, chunk, columns, target):
    n = target.shape[0]
    return [copies.start(w.at[pl.ds(pl.multiple_of(chunk * n, n), n), columns], target)]


def product_kernel(counts, tasks, n_after, scalars, *refs):
    refs = list(refs)
    take = lambda n: [refs.pop(0) for _ in range(n)]
    ngroups, nweights = len(counts), 1 + max(n for n, *_ in tasks)
    groups = [take(n) for n in counts]
    weights = take(nweights)
    take(n_after)
    outs = take(nweights)
    x, ws, sems = refs
    copies = Copies(sems)
    chunk = x.shape[1] // ngroups
    part = lambda g: x.at[:, pl.ds(g * chunk, chunk)]

    def load(g, n, at, columns):
        target = ws.at[g, :, pl.ds(at, columns.size)]
        return fetch_weight(copies, weights[n], scalars[g], columns, target)

    loads = Loads(AHEAD)
    for task in tasks:
        for g in range(ngroups):
            loads.add(functools.partial(load, g, *task))
    loads.begin()
    for g in range(ngroups):
        put_rows(groups[g], part(g))
    for n, at, columns in tasks:
        total = None
        for g in range(ngroups):
            loads.next()
            w = ws[g, :, at : at + columns.size]
            term = jnp.dot(part(g)[...], w, preferred_element_type=F32)
            total = term if total is None else total + term
        outs[n][:, columns] = total.astype(outs[n].dtype)


def product(rows, groups, index, weights, dtypes, after=()):
    chunk = groups[0][0].shape[1]
    widths = [w.shape[1] for w in weights]
    tasks, held = [], 0
    for n, width in enumerate(widths):
        for at in range(0, width, BLOCK):
            tasks.append((n, held, pl.ds(at, BLOCK)))
            held += BLOCK
    anywhere, vmem = (pl.BlockSpec(memory_space=m) for m in (pl.ANY, pltpu.VMEM))
    pieces = [x for g in groups for x in g]
    cols = sum(widths)
    return pl.pallas_call(
        functools.partial(product_kernel, [len(g) for g in groups], tasks, len(after)),
        in_specs=[pl.BlockSpec(memory_space=pltpu.SMEM)]
        + [vmem] * len(pieces)
        + [anywhere] * (len(weights) + len(after)),
        out_specs=[vmem] * len(weights),
        out_shape=[jax.ShapeDtypeStruct((rows, n), d) for n, d in zip(widths, dtypes)],
        scratch_shapes=[
            pltpu.VMEM((rows, len(groups) * chunk), BF16),
            pltpu.VMEM((len(groups), chunk, held), BF16),
            pltpu.SemaphoreType.DMA((len(tasks) * len(groups),)),
        ],
        compiler_params=params(),
        cost_estimate=cost(
            2 * rows * chunk * len(groups) * cols,
            2 * chunk * len(groups) * (cols + rows) + 4 * rows * cols,
        ),
    )(jnp.stack(list(index)), *pieces, *weights, *after)


def cut_kernel(n_after, scalars, w_ref, *refs):
    outs, mark, sems = refs[n_after:-2], refs[-2], refs[-1]
    copies = Copies(sems)
    cols = outs[0].shape[1]
    n = w_ref.shape[1] // (2 * cols)
    started = []
    for to, out in enumerate(outs):
        at = 2 * lax.rem(scalars[0] + 1 + to, n) + scalars[1]
        started.append(
            copies.start(w_ref.at[:, pl.ds(pl.multiple_of(at * cols, cols), cols)], out)
        )
    mark[...] = jnp.zeros_like(mark)
    for copy in started:
        copy.wait()


def cut_by_device(w, me, core, nval, after):
    rows, cols = w.shape[0], w.shape[1] // (2 * nval)
    anywhere, vmem = (pl.BlockSpec(memory_space=m) for m in (pl.ANY, pltpu.VMEM))
    return pl.pallas_call(
        functools.partial(cut_kernel, len(after)),
        in_specs=[pl.BlockSpec(memory_space=pltpu.SMEM)] + [anywhere] * (1 + len(after)),
        out_specs=[vmem] * nval,
        out_shape=[jax.ShapeDtypeStruct((rows, cols), w.dtype)] * (nval - 1)
        + [jax.ShapeDtypeStruct((8, LANES), F32)],
        scratch_shapes=[pltpu.SemaphoreType.DMA((nval - 1,))],
        compiler_params=params(),
        cost_estimate=cost(0, 4 * rows * cols * (nval - 1)),
    )(jnp.stack([me, core]), w, *after)


def out_kernel(counts, with_total, scalars, *refs):
    refs = list(refs)
    take = lambda n: [refs.pop(0) for _ in range(n)]
    ngroups = len(counts)
    groups = [take(n) for n in counts]
    (local,) = take(1)
    halves = [take(3), take(3)]
    total_ref = take(1)[0] if with_total else None
    out, x, ws, held, sems, out_sems = refs
    copies, out_copies = Copies(sems), Copies(out_sems)
    sources = [scalars[ngroups + n] for n in range(4)]
    core = scalars[ngroups + 4]
    chunk = x.shape[1] // ngroups
    cols, vlocal = ws.shape[2], chunk // 8
    row = lambda n: pl.ds(pl.multiple_of(n * vlocal, vlocal), vlocal)

    sides = (core, 1 - core)

    def load(t):
        at = (2 * sources[0] + sides[t]) * cols
        mine = local.at[:, pl.ds(pl.multiple_of(at, cols), cols)]
        started = []
        for g in range(ngroups):
            for n, w in enumerate([mine, *halves[t]]):
                for h in range(2):
                    to = row(g * 8 + h * 4 + sources[n])
                    source = w.at[row(scalars[g] * 2 + h), :]
                    started.append(copies.start(source, ws.at[t, to, :]))
        return started

    started = [load(0)]
    for g in range(ngroups):
        put_rows(groups[g], x.at[:, pl.ds(g * chunk, chunk)])
    last = []
    for t, side in enumerate(sides):
        columns = pl.ds(pl.multiple_of(side * cols, cols), cols)
        for copy in started[t]:
            copy.wait()
        if t == 0:
            started.append(load(1))
        total = jnp.dot(x[...], ws[t], preferred_element_type=F32)
        if with_total:
            total = total + total_ref[:, columns]
        held[t] = total.astype(held.dtype)
        last.append(out_copies.start(held.at[t], out.at[:, columns]))
    for copy in last:
        copy.wait()


def out_product(rows, groups, index, sources, core, local, mine, others, total, dtype):
    chunk = groups[0][0].shape[1]
    cols = mine[0].shape[1]
    anywhere, vmem = (pl.BlockSpec(memory_space=m) for m in (pl.ANY, pltpu.VMEM))
    pieces = [x for g in groups for x in g]
    totals = [] if total is None else [total]
    args = [*pieces, local, *mine, *others, *totals]
    n = len(groups)
    return pl.pallas_call(
        functools.partial(out_kernel, [len(g) for g in groups], total is not None),
        in_specs=[pl.BlockSpec(memory_space=pltpu.SMEM)]
        + [vmem] * len(pieces)
        + [anywhere] * 7
        + [vmem] * len(totals),
        out_specs=anywhere,
        out_shape=jax.ShapeDtypeStruct((rows, 2 * cols), dtype),
        scratch_shapes=[
            pltpu.VMEM((rows, n * chunk), BF16),
            pltpu.VMEM((2, n * chunk, cols), BF16),
            pltpu.VMEM((2, rows, cols), dtype),
            pltpu.SemaphoreType.DMA((16 * n,)),
            pltpu.SemaphoreType.DMA((2,)),
        ],
        compiler_params=params(56),
        cost_estimate=cost(4 * rows * chunk * n * cols, 4 * chunk * n * cols + 8 * rows * cols),
    )(jnp.stack(list(index) + list(sources) + [core]), *args)


def values_kernel(scalars, upper, lower, w_ref, acc_ref, gain_ref, after, *refs):
    n = len(refs) - 3
    outs, (x, w, sems) = refs[:n], refs[n:]
    own, more, vlocal = outs[0].shape
    rows, block = acc_ref.shape[0], own * vlocal
    copies = Copies(sems)
    loads = Loads(AHEAD)
    order = [1, n - 1, *range(2, n - 1), 0]

    def spot(k):
        to = lax.rem(scalars[1] + k, n)
        return to, pl.ds(pl.multiple_of(to * block, block), block)

    for k in order:
        loads.add(lambda k=k: fetch_weight(copies, w_ref, scalars[0], spot(k)[1], w.at[k]))
    loads.begin()
    put_rows((upper, lower), x)
    line = lax.broadcasted_iota(jnp.int32, (more - rows, vlocal), 0)
    for k in order:
        to, columns = spot(k)
        loads.next()
        total = acc_ref[:, columns] + jnp.dot(x[...], w[k], preferred_element_type=F32)
        total = total.astype(BF16)
        for h in range(own):
            outs[k][h, :rows] = total[:, h * vlocal : (h + 1) * vlocal]
            tail = jnp.zeros((more - rows, vlocal), F32)
            for m, part in enumerate(parts_of(gain_ref[pl.ds(to * own + h, 1), :])):
                tail = jnp.where(line == m, part, tail)
            outs[k][h, rows:] = tail.astype(BF16)


def values_by_device(halves, index, me, w, acc, gain, own, after):
    rows, cols = acc.shape
    chunk = halves[0].shape[1]
    vlocal = gain.shape[1]
    block = own * vlocal
    steps = cols // block
    shape = (own, rows + 16, vlocal)
    vmem = pl.BlockSpec(memory_space=pltpu.VMEM)
    return pl.pallas_call(
        values_kernel,
        in_specs=[
            pl.BlockSpec(memory_space=pltpu.SMEM),
            vmem,
            vmem,
            pl.BlockSpec(memory_space=pl.ANY),
            vmem,
            vmem,
            pl.BlockSpec(memory_space=pl.ANY),
        ],
        out_specs=[vmem] * steps,
        out_shape=[jax.ShapeDtypeStruct(shape, BF16)] * steps,
        scratch_shapes=[
            pltpu.VMEM((rows, chunk), BF16),
            pltpu.VMEM((steps, chunk, block), BF16),
            pltpu.SemaphoreType.DMA((steps,)),
        ],
        compiler_params=params(),
        cost_estimate=cost(2 * rows * chunk * cols, 2 * chunk * (cols + rows) + 6 * rows * cols),
    )(jnp.stack([index, me]), *halves, w, acc, gain, after)


def exchanged(pieces):
    return [pieces[0], around(pieces[1], 1), around(pieces[3], -1), around(pieces[2], 2)]


def within_kernel(counts, scalars, bias_ref, *refs):
    pieces = iter(refs[: sum(counts)])
    wg_ref, q_ref, k_ref, kwt_ref, p_ref, stat_ref, mark_ref, g_ref = refs[sum(counts) :]
    own, rows, _ = p_ref.shape
    qsize = q_ref.shape[1] // own
    chunk = refs[0].shape[1]
    heads = bias_ref.shape[1]
    gates = None
    for n, count in enumerate(counts):
        w = wg_ref[:, pl.ds(pl.multiple_of(scalars[n] * chunk, chunk), chunk)]
        x = [next(pieces)[: rows // count] for _ in range(count)]
        x = x[0] if count == 1 else jnp.concatenate(x, axis=0)
        term = lax.dot_general(w, x, (((1,), (1,)), ((), ())), preferred_element_type=F32)
        gates = term if gates is None else gates + term
    g_ref[...] = gates
    late = lax.broadcasted_iota(jnp.int32, (rows, rows), 0)
    early = lax.broadcasted_iota(jnp.int32, (rows, rows), 1)
    causal = late >= early
    line = lax.broadcasted_iota(jnp.int32, (8, rows), 0)
    igate, forget = jnp.zeros((8, rows), F32), jnp.zeros((8, rows), F32)
    for h in range(own):
        head = scalars[0] * own + h
        igate = jnp.where(line == h, g_ref[pl.ds(head, 1), :] + bias_ref[0, head], igate)
        row = g_ref[pl.ds(heads + head, 1), :] + bias_ref[1, head]
        forget = jnp.where(line == h, row, forget)
    logf = jnp.minimum(forget, 0.0) - jnp.log1p(jnp.exp(-jnp.abs(forget)))
    cumb = jnp.dot(
        logf,
        (early >= late).astype(F32),
        precision=lax.Precision.HIGHEST,
        preferred_element_type=F32,
    )
    gap_rows = igate - cumb
    both = jnp.concatenate([gap_rows, cumb, jnp.zeros((LANES - 16, rows), F32)], axis=0).T
    gap = both
    most = jnp.max(gap, axis=0, keepdims=True)
    total = pltpu.roll(both[rows - 8 : rows], LANES - 8, axis=1)[7:8]
    mark_ref[...] = jnp.concatenate([total + most, total, jnp.zeros((6, LANES), F32)], axis=0)
    lane = lax.broadcasted_iota(jnp.int32, (rows, LANES), 1)
    stat = jnp.zeros((rows, LANES), F32)
    for h in range(own):
        q = q_ref[:, h * qsize : (h + 1) * qsize]
        k = k_ref[:, h * qsize : (h + 1) * qsize]
        seen = jnp.where(causal, gap_rows[h : h + 1, :], F32(NEVER))
        high = jnp.max(seen, axis=1, keepdims=True)
        score = lax.dot_general(q, k, (((1,), (1,)), ((), ())), preferred_element_type=F32)
        wts = jnp.exp(seen - high) * (score * qsize ** (-0.5))
        wts = jnp.where(causal, wts, 0.0).astype(BF16)
        p_ref[h] = wts
        denom = jnp.sum(wts.astype(F32), axis=1, keepdims=True)
        stat = jnp.where(lane == h, high, jnp.where(lane == own + h, denom, stat))
        fall = jnp.exp(gap[:, h : h + 1] - most[:, h : h + 1])
        kw = (k.astype(F32) * fall).astype(BF16)
        kwt_ref[h * qsize : (h + 1) * qsize] = kw.astype(F32).T.astype(BF16)
    stat_ref[...] = stat


def within(groups, index, wg, bias, q, k, own):
    rows, width = q.shape
    pieces = [x for g in groups for x in g]
    vmem = pl.BlockSpec(memory_space=pltpu.VMEM)
    return pl.pallas_call(
        functools.partial(within_kernel, [len(g) for g in groups]),
        in_specs=[pl.BlockSpec(memory_space=pltpu.SMEM)] * 2 + [vmem] * (len(pieces) + 3),
        out_specs=[vmem] * 4,
        out_shape=[
            jax.ShapeDtypeStruct((width, rows), BF16),
            jax.ShapeDtypeStruct((own, rows, rows), BF16),
            jax.ShapeDtypeStruct((rows, LANES), F32),
            jax.ShapeDtypeStruct((8, LANES), F32),
        ],
        scratch_shapes=[pltpu.VMEM((wg.shape[0], rows), F32)],
        compiler_params=params(),
        cost_estimate=cost(4 * rows * rows * width, 8 * rows * width, own * rows * rows),
    )(jnp.stack(list(index)), bias, *pieces, wg, q, k)


def parts_of(x):
    hi = x.astype(BF16).astype(F32)
    mid = (x - hi).astype(BF16).astype(F32)
    return [hi, mid, x - hi - mid]


def of_head(head, rows):
    return jnp.where(head == 0, rows[:, 0:1], rows[:, 1:2])


def marked(extra, top, total):
    lane = lax.broadcasted_iota(jnp.int32, extra.shape, 1)
    for n, x in enumerate(parts_of(top) + ([] if total is None else parts_of(total))):
        extra = jnp.where(lane == 1 + n, x, extra)
    return extra


def marks_of(extra):
    top = extra[:, 1:2] + extra[:, 2:3] + extra[:, 3:4]
    total = extra[:, 4:5] + extra[:, 5:6] + extra[:, 6:7]
    return top, total


def summary_kernel(scalars, kwt_ref, mark_ref, v0, v1, v2, v3, mine, other, v_ref, gain_ref):
    vlocal = v0.shape[2]
    own, rows, vsize = v_ref.shape
    gain_ref[...] = jnp.zeros_like(gain_ref)
    qsize = kwt_ref.shape[0] // own
    for n, ref in enumerate((v0, v1, v2, v3)):
        at = pl.multiple_of(scalars[n] * vlocal, vlocal)
        for h in range(own):
            v_ref[h, :, pl.ds(at, vlocal)] = ref[h, :rows]
            tail = ref[h, rows:].astype(F32)
            gain_ref[h : h + 1, pl.ds(at, vlocal)] = tail[0:1] + tail[1:2] + tail[2:3]
    lane = lax.broadcasted_iota(jnp.int32, (qsize, LANES), 1)
    core = scalars[4]
    for h, out in ((core, mine), (1 - core, other)):
        kwt = kwt_ref[pl.ds(pl.multiple_of(h * qsize, qsize), qsize), :]
        out[:, :vsize] = jnp.dot(kwt, v_ref[h], preferred_element_type=F32).astype(BF16)
        extra = jnp.where(lane == 0, jnp.sum(kwt.astype(F32), axis=1, keepdims=True), 0.0)
        top, total = of_head(h, mark_ref[0:1, :]), of_head(h, mark_ref[1:2, :])
        out[:, vsize:] = marked(extra, top, total).astype(BF16)


def summary(index, core, kwt, mark, pieces):
    own, _, vlocal = pieces[0].shape
    rows = kwt.shape[1]
    vsize = vlocal * len(pieces)
    whole = lambda shape: pl.BlockSpec(shape, lambda j, s: (0,) * len(shape))
    shapes = [((kwt.shape[0] // own, vsize + LANES), BF16)] * 2
    shapes += [((own, rows, vsize), BF16), ((8, vsize), F32)]
    return pl.pallas_call(
        summary_kernel,
        grid_spec=pltpu.PrefetchScalarGridSpec(
            num_scalar_prefetch=1,
            grid=(1,),
            in_specs=[whole(kwt.shape), whole(mark.shape)] + [whole(x.shape) for x in pieces],
            out_specs=[whole(shape) for shape, _ in shapes],
        ),
        out_shape=[jax.ShapeDtypeStruct(shape, dtype) for shape, dtype in shapes],
        compiler_params=params(32),
        cost_estimate=cost(2 * kwt.size * vsize, 3 * own * rows * vsize * 2),
    )(jnp.stack(list(index) + [core]), kwt, mark, *pieces)


def pair_kernel(scalars, mine, got, out):
    first = scalars[0] == 0
    body = mine.shape[1] - LANES
    a, b = mine[:, body:].astype(F32), got[:, body:].astype(F32)
    early, late = jnp.where(first, a, b), jnp.where(first, b, a)
    (etop, etotal), (ltop, ltotal) = marks_of(early), marks_of(late)
    top = jnp.maximum(etop + ltotal, ltop)
    fe, fl = jnp.exp(etop + ltotal - top), jnp.exp(ltop - top)
    fa, fb = jnp.where(first, fe, fl), jnp.where(first, fl, fe)
    state = fa * mine[:, :body].astype(F32) + fb * got[:, :body].astype(F32)
    out[:, :body] = state.astype(BF16)
    out[:, body:] = marked(fa * a + fb * b, top, etotal + ltotal).astype(BF16)


def pair(core, mine, got):
    vmem = pl.BlockSpec(memory_space=pltpu.VMEM)
    return pl.pallas_call(
        pair_kernel,
        in_specs=[pl.BlockSpec(memory_space=pltpu.SMEM), vmem, vmem],
        out_specs=vmem,
        out_shape=jax.ShapeDtypeStruct(mine.shape, BF16),
        compiler_params=params(32),
        cost_estimate=cost(4 * mine.size, 6 * mine.size),
    )(jnp.stack([core]), mine, got)


def unpair_kernel(scalars, prefix, mine, got, keep, send):
    first = scalars[0] == 0
    body = mine.shape[1] - LANES
    p = prefix[:, body:].astype(F32)
    s = jnp.where(first, mine[:, body:].astype(F32), got[:, body:].astype(F32))
    ptop, _ = marks_of(p)
    stop, stotal = marks_of(s)
    top = jnp.maximum(ptop + stotal, stop)
    fp, fs = jnp.exp(ptop + stotal - top), jnp.exp(stop - top)
    state = jnp.where(first, mine[:, :body], got[:, :body]).astype(F32)
    state = (fp * prefix[:, :body].astype(F32) + fs * state).astype(BF16)
    extra = marked(fp * p + fs * s, top, None).astype(BF16)
    keep[:, :body] = jnp.where(first, prefix[:, :body], state)
    send[:, :body] = jnp.where(first, state, prefix[:, :body])
    keep[:, body:] = jnp.where(first, prefix[:, body:], extra)
    send[:, body:] = jnp.where(first, extra, prefix[:, body:])


def unpair(core, prefix, mine, got):
    vmem = pl.BlockSpec(memory_space=pltpu.VMEM)
    return pl.pallas_call(
        unpair_kernel,
        in_specs=[pl.BlockSpec(memory_space=pltpu.SMEM)] + [vmem] * 3,
        out_specs=[vmem] * 2,
        out_shape=[jax.ShapeDtypeStruct(mine.shape, BF16)] * 2,
        compiler_params=params(32),
        cost_estimate=cost(4 * mine.size, 10 * mine.size),
    )(jnp.stack([core]), prefix, mine, got)


def inside_kernel(p_ref, v_ref, out_ref):
    for h in range(p_ref.shape[0]):
        out_ref[h] = jnp.dot(p_ref[h], v_ref[h], preferred_element_type=F32)


def inside(p, v):
    return pl.pallas_call(
        inside_kernel,
        out_shape=jax.ShapeDtypeStruct(v.shape, F32),
        compiler_params=params(32),
        cost_estimate=cost(2 * p.size * v.shape[2], 6 * v.size),
    )(p, v)


def prefix_kernel(got_ref, out_ref):
    blocks, cut, width = got_ref.shape
    body = width - LANES
    lane = lax.broadcasted_iota(jnp.int32, (cut, LANES), 1)
    source = lax.broadcasted_iota(jnp.int32, (LANES, 2 * LANES), 0)
    target = lax.broadcasted_iota(jnp.int32, (LANES, 2 * LANES), 1)
    first = jnp.where(target < LANES, 1, 4)
    spread = ((source >= first) & (source < first + 3)).astype(F32).astype(BF16)
    marks = jnp.dot(
        got_ref[:, :, body:].reshape(blocks * cut, LANES), spread, preferred_element_type=F32
    )
    state = [jnp.zeros((cut, LANES), F32) for _ in range(width // LANES)]
    ptop = jnp.full((cut, LANES), NEVER, F32)
    for b in range(blocks):
        held = state[-1]
        for n, x in enumerate(parts_of(ptop)):
            held = jnp.where(lane == 1 + n, x, held)
        for n, x in enumerate(state[:-1] + [held]):
            out_ref[b, :, n * LANES : (n + 1) * LANES] = x.astype(BF16)
        if b == blocks - 1:
            break
        top = marks[b * cut : (b + 1) * cut, :LANES]
        total = marks[b * cut : (b + 1) * cut, LANES:]
        new = jnp.maximum(ptop + total, top)
        keep = jnp.exp(ptop + total - new)
        add = jnp.exp(top - new)
        state = [
            keep * x + add * got_ref[b, :, n * LANES : (n + 1) * LANES].astype(F32)
            for n, x in enumerate(state)
        ]
        ptop = new


def prefixes(got):
    return pl.pallas_call(
        prefix_kernel,
        out_shape=jax.ShapeDtypeStruct(got.shape, BF16),
        compiler_params=params(32),
        cost_estimate=cost(4 * got.size, 4 * got.size),
    )(got)


def finish_kernel(scalars, q_ref, mine, got, numer_ref, stat_ref, gain_ref, upper, lower):
    own, rows, vsize = numer_ref.shape
    qsize = q_ref.shape[1] // own
    core = scalars[0]
    for h, prefix_ref in ((core, mine), (1 - core, got)):
        q = q_ref[:, pl.ds(pl.multiple_of(h * qsize, qsize), qsize)]
        inter = jnp.dot(q, prefix_ref[...], preferred_element_type=F32)
        ptop, _ = marks_of(prefix_ref[0:16, vsize:].astype(F32)[0:1])
        high = of_head(h, stat_ref[...])
        top = jnp.maximum(high, ptop)
        fade = jnp.exp(high - top)
        decay = jnp.exp(ptop - top) * qsize ** (-0.5)
        denom = of_head(h, stat_ref[:, own : 2 * own])
        denom = denom * fade + inter[:, vsize : vsize + 1] * decay
        share = 1.0 / jnp.maximum(jnp.abs(denom), 1.0)
        hidden = numer_ref[h] * (fade * share) + inter[:, :vsize] * (decay * share)
        mean = jnp.mean(hidden, axis=1, keepdims=True)
        msq = jnp.mean(hidden * hidden, axis=1, keepdims=True)
        gain = gain_ref[pl.ds(h, 1), :]
        normed = (hidden - mean) * lax.rsqrt(msq - mean * mean + 1e-06) * gain
        normed = normed.astype(BF16)
        columns = pl.ds(pl.multiple_of(h * vsize, vsize), vsize)
        upper[:, columns] = normed[: rows // 2]
        lower[:, columns] = normed[rows // 2 :]


def finish(core, q, mine, got, numer, stat, gain):
    own, rows, vsize = numer.shape
    vmem = pl.BlockSpec(memory_space=pltpu.VMEM)
    return pl.pallas_call(
        finish_kernel,
        in_specs=[pl.BlockSpec(memory_space=pltpu.SMEM)] + [vmem] * 6,
        out_specs=[vmem] * 2,
        out_shape=[jax.ShapeDtypeStruct((rows // 2, own * vsize), BF16)] * 2,
        compiler_params=params(32),
        cost_estimate=cost(2 * q.size * vsize, 8 * numer.size),
    )(jnp.stack([core]), q, mine, got, numer, stat, gain)


def per_device(tokens, w_query, w_key, w_value, w_gate, gate_bias, norm_gain, w_out):
    me = lax.axis_index("val")
    nval = lax.axis_size("val")
    place = lax.axis_index("seq")
    blocks = lax.axis_size("seq")
    rows, chunk = tokens.shape
    width = w_query.shape[0]
    heads, vlocal = w_value.shape[1:]
    own = heads // nval
    qsize = w_query.shape[1] // own
    vsize = vlocal * nval
    index = [(me + d) % nval for d in (0, nval - 1, 1, 2)]

    half = rows // 2
    upper, lower = moved([tokens], [[(0, 0, half)], [(0, half, half)]], [])
    ring = Ring(upper, lower, [upper, lower])
    wg = w_gate.transpose(1, 2, 0).reshape(2 * heads, width)
    wv, early = flat(w_value, 0, 2)
    ring.second([early])
    wv, late = flat(w_value, 2, 2, wv)
    ring.forward([late])
    wv, _ = flat(w_value, 4, 4, wv)
    groups = [(tokens,), ring.left, ring.right]
    acc = product(rows, groups, index[:3], [wv], [F32])[0]
    core = place % 2
    cores = [(i, i ^ 1) for i in range(blocks)]
    local = w_out.reshape(heads * vlocal, -1)
    *pieces, mark = cut_by_device(local, me, core, nval, [acc])
    values = values_by_device(ring.opposite, index[3], me, wv, acc, norm_gain, own, mark)
    pieces = tied(pieces, values[:1])
    halves = exchanged([None, *pieces])[1:]
    groups.append(ring.opposite)
    q, k = product(rows, groups, index, [w_query, w_key], [BF16] * 2, values[:1])

    values = exchanged(values)
    kwt, p, stat, mark = within(groups, index, wg, gate_bias, q, k, own)
    mine, other, v, gain = summary(index, core, kwt, mark, values)
    got = lax.ppermute(other, "seq", cores)
    chips = [list(range(n, blocks, 2)) for n in range(2)]
    sliced = (blocks // 2, -1, vsize + LANES)
    both = pair(core, mine, got).reshape(sliced)
    both = lax.all_to_all(both, "seq", 0, 0, axis_index_groups=chips)
    numer = inside(p, v)
    prefix = lax.all_to_all(prefixes(both), "seq", 0, 0, axis_index_groups=chips)
    keep, send = unpair(core, prefix.reshape(mine.shape), mine, got)
    came = lax.ppermute(send, "seq", cores)
    upper, lower = finish(core, q, keep, came, numer, stat, gain)

    ring = Ring(upper, lower, [upper, lower])
    halves = tied(halves, [upper])
    others = [lax.ppermute(x, "seq", cores) for x in halves]
    *others, there = tied(others, [], with_mark=True)
    ring.second([there])
    ring.forward()
    groups = [ring.own, ring.left, ring.right]
    weights = (index, core, local, halves, others)
    acc = out_product(rows, groups, index[:3], *weights, None, F32)
    return out_product(rows, [ring.opposite], index[3:], *weights, acc, BF16)


def solution(mesh):
    placed = (
        P("seq", "val"),
        P(None, "val"),
        P(None, "val"),
        P(None, None, "val"),
        P(),
        P(),
        P(None, "val"),
        P(None, "val", None),
    )
    return jax.shard_map(
        per_device, mesh=mesh, in_specs=placed, out_specs=P("seq", "val"), check_vma=False
    )
```

```python
import functools

import jax
import jax.numpy as jnp
from jax import lax
from jax.experimental import pallas as pl
from jax.experimental.pallas import tpu as pltpu
from jax.sharding import PartitionSpec as P

F32 = jnp.float32
BF16 = jnp.bfloat16
LANES = 128
NEVER = -1e30
BLOCK = 512
AHEAD = 8


def around(x, distance):
    n = lax.axis_size("val")
    return lax.ppermute(x, "val", [(i, (i + distance) % n) for i in range(n)])


def params(mib=48):
    return pltpu.CompilerParams(vmem_limit_bytes=mib * 1024 * 1024)


def cost(flops, nbytes, exps=0):
    return pl.CostEstimate(flops=flops, bytes_accessed=nbytes, transcendentals=exps)


class Ring:
    def __init__(self, plus, minus, later):
        self.own = (plus, minus)
        self.plus, self.minus = around(plus, 1), around(minus, -1)
        self.later = later

    def second(self, after):
        plus, minus = moved(self.later, [[(1, 0, 0)], [(0, 0, 0)]], after)
        self.sent = plus
        self.left = (self.plus, around(plus, 1))
        self.right = (around(minus, -1), self.minus)

    def forward(self, after=()):
        self.plus, self.minus = tied([self.plus, self.minus], [self.sent, *after])
        self.left = (self.plus, self.left[1])
        self.right = (self.right[0], self.minus)
        self.opposite = (around(self.plus, 1), around(self.minus, -1))


def tied_kernel(with_mark, *refs):
    if with_mark:
        refs[-1][...] = jnp.zeros_like(refs[-1])


def tied(arrays, after, with_mark=False):
    anywhere = pl.BlockSpec(memory_space=pl.ANY)
    marks = int(with_mark)
    return pl.pallas_call(
        functools.partial(tied_kernel, with_mark),
        in_specs=[anywhere] * (len(arrays) + len(after)),
        out_specs=[anywhere] * len(arrays) + [pl.BlockSpec(memory_space=pltpu.VMEM)] * marks,
        out_shape=[jax.ShapeDtypeStruct(x.shape, x.dtype) for x in arrays]
        + [jax.ShapeDtypeStruct((8, LANES), F32)] * marks,
        input_output_aliases={n: n for n in range(len(arrays))},
        compiler_params=params(),
    )(*arrays, *after)


def moved_kernel(n, n_after, plan, *refs):
    sources, outs = refs[:n], refs[n + n_after :]
    for out, parts in zip(outs, plan):
        at = 0
        for source, first, count in parts:
            count = count or sources[source].shape[0] - first
            out[at : at + count] = sources[source][first : first + count]
            at += count


def moved(arrays, plan, after):
    shapes = [sum(c or arrays[n].shape[0] - f for n, f, c in parts) for parts in plan]
    anywhere, vmem = (pl.BlockSpec(memory_space=m) for m in (pl.ANY, pltpu.VMEM))
    return pl.pallas_call(
        functools.partial(moved_kernel, len(arrays), len(after), plan),
        in_specs=[vmem] * len(arrays) + [anywhere] * len(after),
        out_specs=[vmem] * len(plan),
        out_shape=[
            jax.ShapeDtypeStruct((n, arrays[0].shape[1]), arrays[0].dtype) for n in shapes
        ],
        compiler_params=params(32),
        cost_estimate=cost(0, 4 * sum(shapes) * arrays[0].shape[1]),
    )(*arrays, *after)


def flat_kernel(n, w_ref, *refs):
    refs[-2][...] = w_ref[...].reshape(refs[-2].shape)
    refs[-1][...] = jnp.zeros_like(refs[-1])


def flat(w, first, steps, before=None):
    rows, heads, size = w.shape
    block = rows // 8
    args = [w] if before is None else [w, before]
    return pl.pallas_call(
        functools.partial(flat_kernel, len(args)),
        grid=(steps,),
        in_specs=[
            pl.BlockSpec((block, heads, size), lambda j: (j + first, 0, 0)),
            pl.BlockSpec(memory_space=pl.ANY),
        ][: len(args)],
        out_specs=[
            pl.BlockSpec((block, heads * size), lambda j: (j + first, 0)),
            pl.BlockSpec((8, LANES), lambda j: (0, 0)),
        ],
        out_shape=[
            jax.ShapeDtypeStruct((rows, heads * size), w.dtype),
            jax.ShapeDtypeStruct((8, LANES), F32),
        ],
        input_output_aliases={} if before is None else {1: 0},
        compiler_params=params(),
        cost_estimate=cost(0, 2 * w.size * steps // 8),
    )(*args)


class Copies:
    def __init__(self, sems):
        self.sems = sems
        self.used = 0

    def start(self, source, target):
        copy = pltpu.make_async_copy(source, target, self.sems.at[self.used])
        self.used += 1
        copy.start()
        return copy


class Loads:
    def __init__(self, ahead):
        self.ahead = ahead
        self.waiting = []
        self.started = []

    def add(self, start):
        self.waiting.append(start)

    def begin(self):
        while self.waiting and len(self.started) <= self.ahead:
            self.started.append(self.waiting.pop(0)())

    def next(self):
        self.begin()
        for copy in self.started.pop(0):
            copy.wait()


def put_rows(pieces, buffer):
    n = buffer.shape[0] // len(pieces)
    for at, piece in enumerate(pieces):
        buffer[at * n : (at + 1) * n] = piece[:n]


def fetch_weight(copies, w, chunk, columns, target):
    n = target.shape[0]
    return [copies.start(w.at[pl.ds(pl.multiple_of(chunk * n, n), n), columns], target)]


def product_kernel(counts, tasks, n_after, scalars, *refs):
    refs = list(refs)
    take = lambda n: [refs.pop(0) for _ in range(n)]
    ngroups, nweights = len(counts), 1 + max(n for n, *_ in tasks)
    groups = [take(n) for n in counts]
    weights = take(nweights)
    take(n_after)
    outs = take(nweights)
    x, ws, sems = refs
    copies = Copies(sems)
    chunk = x.shape[1] // ngroups
    part = lambda g: x.at[:, pl.ds(g * chunk, chunk)]

    def load(g, n, at, columns):
        target = ws.at[g, :, pl.ds(at, columns.size)]
        return fetch_weight(copies, weights[n], scalars[g], columns, target)

    loads = Loads(AHEAD)
    for task in tasks:
        for g in range(ngroups):
            loads.add(functools.partial(load, g, *task))
    loads.begin()
    for g in range(ngroups):
        put_rows(groups[g], part(g))
    for n, at, columns in tasks:
        total = None
        for g in range(ngroups):
            loads.next()
            w = ws[g, :, at : at + columns.size]
            term = jnp.dot(part(g)[...], w, preferred_element_type=F32)
            total = term if total is None else total + term
        outs[n][:, columns] = total.astype(outs[n].dtype)


def product(rows, groups, index, weights, dtypes, after=()):
    chunk = groups[0][0].shape[1]
    widths = [w.shape[1] for w in weights]
    tasks, held = [], 0
    for n, width in enumerate(widths):
        for at in range(0, width, BLOCK):
            tasks.append((n, held, pl.ds(at, BLOCK)))
            held += BLOCK
    anywhere, vmem = (pl.BlockSpec(memory_space=m) for m in (pl.ANY, pltpu.VMEM))
    pieces = [x for g in groups for x in g]
    cols = sum(widths)
    return pl.pallas_call(
        functools.partial(product_kernel, [len(g) for g in groups], tasks, len(after)),
        in_specs=[pl.BlockSpec(memory_space=pltpu.SMEM)]
        + [vmem] * len(pieces)
        + [anywhere] * (len(weights) + len(after)),
        out_specs=[vmem] * len(weights),
        out_shape=[jax.ShapeDtypeStruct((rows, n), d) for n, d in zip(widths, dtypes)],
        scratch_shapes=[
            pltpu.VMEM((rows, len(groups) * chunk), BF16),
            pltpu.VMEM((len(groups), chunk, held), BF16),
            pltpu.SemaphoreType.DMA((len(tasks) * len(groups),)),
        ],
        compiler_params=params(),
        cost_estimate=cost(
            2 * rows * chunk * len(groups) * cols,
            2 * chunk * len(groups) * (cols + rows) + 4 * rows * cols,
        ),
    )(jnp.stack(list(index)), *pieces, *weights, *after)


def cut_kernel(n_after, scalars, w_ref, *refs):
    outs, mark, sems = refs[n_after:-2], refs[-2], refs[-1]
    copies = Copies(sems)
    cols = outs[0].shape[1]
    n = w_ref.shape[1] // (2 * cols)
    started = []
    for to, out in enumerate(outs):
        at = 2 * lax.rem(scalars[0] + 1 + to, n) + scalars[1]
        started.append(
            copies.start(w_ref.at[:, pl.ds(pl.multiple_of(at * cols, cols), cols)], out)
        )
    mark[...] = jnp.zeros_like(mark)
    for copy in started:
        copy.wait()


def cut_by_device(w, me, core, nval, after):
    rows, cols = w.shape[0], w.shape[1] // (2 * nval)
    anywhere, vmem = (pl.BlockSpec(memory_space=m) for m in (pl.ANY, pltpu.VMEM))
    return pl.pallas_call(
        functools.partial(cut_kernel, len(after)),
        in_specs=[pl.BlockSpec(memory_space=pltpu.SMEM)] + [anywhere] * (1 + len(after)),
        out_specs=[vmem] * nval,
        out_shape=[jax.ShapeDtypeStruct((rows, cols), w.dtype)] * (nval - 1)
        + [jax.ShapeDtypeStruct((8, LANES), F32)],
        scratch_shapes=[pltpu.SemaphoreType.DMA((nval - 1,))],
        compiler_params=params(),
        cost_estimate=cost(0, 4 * rows * cols * (nval - 1)),
    )(jnp.stack([me, core]), w, *after)


def out_kernel(counts, with_total, scalars, *refs):
    refs = list(refs)
    take = lambda n: [refs.pop(0) for _ in range(n)]
    ngroups = len(counts)
    groups = [take(n) for n in counts]
    (local,) = take(1)
    halves = [take(3), take(3)]
    total_ref = take(1)[0] if with_total else None
    out, x, ws, held, sems, out_sems = refs
    copies, out_copies = Copies(sems), Copies(out_sems)
    sources = [scalars[ngroups + n] for n in range(4)]
    core = scalars[ngroups + 4]
    chunk = x.shape[1] // ngroups
    cols, vlocal = ws.shape[2], chunk // 8
    row = lambda n: pl.ds(pl.multiple_of(n * vlocal, vlocal), vlocal)

    sides = (core, 1 - core)

    def load(t):
        at = (2 * sources[0] + sides[t]) * cols
        mine = local.at[:, pl.ds(pl.multiple_of(at, cols), cols)]
        started = []
        for g in range(ngroups):
            for n, w in enumerate([mine, *halves[t]]):
                for h in range(2):
                    to = row(g * 8 + h * 4 + sources[n])
                    source = w.at[row(scalars[g] * 2 + h), :]
                    started.append(copies.start(source, ws.at[t, to, :]))
        return started

    started = [load(t) for t in range(2)]
    for g in range(ngroups):
        put_rows(groups[g], x.at[:, pl.ds(g * chunk, chunk)])
    last = []
    for t, side in enumerate(sides):
        columns = pl.ds(pl.multiple_of(side * cols, cols), cols)
        for copy in started[t]:
            copy.wait()
        total = jnp.dot(x[...], ws[t], preferred_element_type=F32)
        if with_total:
            total = total + total_ref[:, columns]
        held[t] = total.astype(held.dtype)
        last.append(out_copies.start(held.at[t], out.at[:, columns]))
    for copy in last:
        copy.wait()


def out_product(rows, groups, index, sources, core, local, mine, others, total, dtype):
    chunk = groups[0][0].shape[1]
    cols = mine[0].shape[1]
    anywhere, vmem = (pl.BlockSpec(memory_space=m) for m in (pl.ANY, pltpu.VMEM))
    pieces = [x for g in groups for x in g]
    totals = [] if total is None else [total]
    args = [*pieces, local, *mine, *others, *totals]
    n = len(groups)
    return pl.pallas_call(
        functools.partial(out_kernel, [len(g) for g in groups], total is not None),
        in_specs=[pl.BlockSpec(memory_space=pltpu.SMEM)]
        + [vmem] * len(pieces)
        + [anywhere] * 7
        + [vmem] * len(totals),
        out_specs=anywhere,
        out_shape=jax.ShapeDtypeStruct((rows, 2 * cols), dtype),
        scratch_shapes=[
            pltpu.VMEM((rows, n * chunk), BF16),
            pltpu.VMEM((2, n * chunk, cols), BF16),
            pltpu.VMEM((2, rows, cols), dtype),
            pltpu.SemaphoreType.DMA((16 * n,)),
            pltpu.SemaphoreType.DMA((2,)),
        ],
        compiler_params=params(56),
        cost_estimate=cost(4 * rows * chunk * n * cols, 4 * chunk * n * cols + 8 * rows * cols),
    )(jnp.stack(list(index) + list(sources) + [core]), *args)


def values_kernel(scalars, upper, lower, w_ref, acc_ref, gain_ref, after, *refs):
    n = len(refs) - 3
    outs, (x, w, sems) = refs[:n], refs[n:]
    own, more, vlocal = outs[0].shape
    rows, block = acc_ref.shape[0], own * vlocal
    copies = Copies(sems)
    loads = Loads(AHEAD)
    order = [1, n - 1, *range(2, n - 1), 0]

    def spot(k):
        to = lax.rem(scalars[1] + k, n)
        return to, pl.ds(pl.multiple_of(to * block, block), block)

    for k in order:
        loads.add(lambda k=k: fetch_weight(copies, w_ref, scalars[0], spot(k)[1], w.at[k]))
    loads.begin()
    put_rows((upper, lower), x)
    line = lax.broadcasted_iota(jnp.int32, (more - rows, vlocal), 0)
    for k in order:
        to, columns = spot(k)
        loads.next()
        total = acc_ref[:, columns] + jnp.dot(x[...], w[k], preferred_element_type=F32)
        total = total.astype(BF16)
        for h in range(own):
            outs[k][h, :rows] = total[:, h * vlocal : (h + 1) * vlocal]
            tail = jnp.zeros((more - rows, vlocal), F32)
            for m, part in enumerate(parts_of(gain_ref[pl.ds(to * own + h, 1), :])):
                tail = jnp.where(line == m, part, tail)
            outs[k][h, rows:] = tail.astype(BF16)


def values_by_device(halves, index, me, w, acc, gain, own, after):
    rows, cols = acc.shape
    chunk = halves[0].shape[1]
    vlocal = gain.shape[1]
    block = own * vlocal
    steps = cols // block
    shape = (own, rows + 16, vlocal)
    vmem = pl.BlockSpec(memory_space=pltpu.VMEM)
    return pl.pallas_call(
        values_kernel,
        in_specs=[
            pl.BlockSpec(memory_space=pltpu.SMEM),
            vmem,
            vmem,
            pl.BlockSpec(memory_space=pl.ANY),
            vmem,
            vmem,
            pl.BlockSpec(memory_space=pl.ANY),
        ],
        out_specs=[vmem] * steps,
        out_shape=[jax.ShapeDtypeStruct(shape, BF16)] * steps,
        scratch_shapes=[
            pltpu.VMEM((rows, chunk), BF16),
            pltpu.VMEM((steps, chunk, block), BF16),
            pltpu.SemaphoreType.DMA((steps,)),
        ],
        compiler_params=params(),
        cost_estimate=cost(2 * rows * chunk * cols, 2 * chunk * (cols + rows) + 6 * rows * cols),
    )(jnp.stack([index, me]), *halves, w, acc, gain, after)


def exchanged(pieces):
    return [pieces[0], around(pieces[1], 1), around(pieces[3], -1), around(pieces[2], 2)]


def within_kernel(counts, scalars, bias_ref, *refs):
    pieces = iter(refs[: sum(counts)])
    wg_ref, q_ref, k_ref, kwt_ref, p_ref, stat_ref, mark_ref, g_ref = refs[sum(counts) :]
    own, rows, _ = p_ref.shape
    qsize = q_ref.shape[1] // own
    chunk = refs[0].shape[1]
    heads = bias_ref.shape[1]
    gates = None
    for n, count in enumerate(counts):
        w = wg_ref[:, pl.ds(pl.multiple_of(scalars[n] * chunk, chunk), chunk)]
        x = [next(pieces)[: rows // count] for _ in range(count)]
        x = x[0] if count == 1 else jnp.concatenate(x, axis=0)
        term = lax.dot_general(w, x, (((1,), (1,)), ((), ())), preferred_element_type=F32)
        gates = term if gates is None else gates + term
    g_ref[...] = gates
    late = lax.broadcasted_iota(jnp.int32, (rows, rows), 0)
    early = lax.broadcasted_iota(jnp.int32, (rows, rows), 1)
    causal = late >= early
    line = lax.broadcasted_iota(jnp.int32, (8, rows), 0)
    igate, forget = jnp.zeros((8, rows), F32), jnp.zeros((8, rows), F32)
    for h in range(own):
        head = scalars[0] * own + h
        igate = jnp.where(line == h, g_ref[pl.ds(head, 1), :] + bias_ref[0, head], igate)
        row = g_ref[pl.ds(heads + head, 1), :] + bias_ref[1, head]
        forget = jnp.where(line == h, row, forget)
    logf = jnp.minimum(forget, 0.0) - jnp.log1p(jnp.exp(-jnp.abs(forget)))
    cumb = jnp.dot(
        logf,
        (early >= late).astype(F32),
        precision=lax.Precision.HIGHEST,
        preferred_element_type=F32,
    )
    gap_rows = igate - cumb
    both = jnp.concatenate([gap_rows, cumb, jnp.zeros((LANES - 16, rows), F32)], axis=0).T
    gap = both
    most = jnp.max(gap, axis=0, keepdims=True)
    total = pltpu.roll(both[rows - 8 : rows], LANES - 8, axis=1)[7:8]
    mark_ref[...] = jnp.concatenate([total + most, total, jnp.zeros((6, LANES), F32)], axis=0)
    lane = lax.broadcasted_iota(jnp.int32, (rows, LANES), 1)
    stat = jnp.zeros((rows, LANES), F32)
    for h in range(own):
        q = q_ref[:, h * qsize : (h + 1) * qsize]
        k = k_ref[:, h * qsize : (h + 1) * qsize]
        seen = jnp.where(causal, gap_rows[h : h + 1, :], F32(NEVER))
        high = jnp.max(seen, axis=1, keepdims=True)
        score = lax.dot_general(q, k, (((1,), (1,)), ((), ())), preferred_element_type=F32)
        wts = jnp.exp(seen - high) * (score * qsize ** (-0.5))
        wts = jnp.where(causal, wts, 0.0).astype(BF16)
        p_ref[h] = wts
        denom = jnp.sum(wts.astype(F32), axis=1, keepdims=True)
        stat = jnp.where(lane == h, high, jnp.where(lane == own + h, denom, stat))
        fall = jnp.exp(gap[:, h : h + 1] - most[:, h : h + 1])
        kw = (k.astype(F32) * fall).astype(BF16)
        kwt_ref[h * qsize : (h + 1) * qsize] = kw.astype(F32).T.astype(BF16)
    stat_ref[...] = stat


def within(groups, index, wg, bias, q, k, own):
    rows, width = q.shape
    pieces = [x for g in groups for x in g]
    vmem = pl.BlockSpec(memory_space=pltpu.VMEM)
    return pl.pallas_call(
        functools.partial(within_kernel, [len(g) for g in groups]),
        in_specs=[pl.BlockSpec(memory_space=pltpu.SMEM)] * 2 + [vmem] * (len(pieces) + 3),
        out_specs=[vmem] * 4,
        out_shape=[
            jax.ShapeDtypeStruct((width, rows), BF16),
            jax.ShapeDtypeStruct((own, rows, rows), BF16),
            jax.ShapeDtypeStruct((rows, LANES), F32),
            jax.ShapeDtypeStruct((8, LANES), F32),
        ],
        scratch_shapes=[pltpu.VMEM((wg.shape[0], rows), F32)],
        compiler_params=params(),
        cost_estimate=cost(4 * rows * rows * width, 8 * rows * width, own * rows * rows),
    )(jnp.stack(list(index)), bias, *pieces, wg, q, k)


def parts_of(x):
    hi = x.astype(BF16).astype(F32)
    mid = (x - hi).astype(BF16).astype(F32)
    return [hi, mid, x - hi - mid]


def of_head(head, rows):
    return jnp.where(head == 0, rows[:, 0:1], rows[:, 1:2])


def marked(extra, top, total):
    lane = lax.broadcasted_iota(jnp.int32, extra.shape, 1)
    for n, x in enumerate(parts_of(top) + ([] if total is None else parts_of(total))):
        extra = jnp.where(lane == 1 + n, x, extra)
    return extra


def marks_of(extra):
    top = extra[:, 1:2] + extra[:, 2:3] + extra[:, 3:4]
    total = extra[:, 4:5] + extra[:, 5:6] + extra[:, 6:7]
    return top, total


def summary_kernel(scalars, kwt_ref, mark_ref, v0, v1, v2, v3, mine, other, v_ref, gain_ref):
    vlocal = v0.shape[2]
    own, rows, vsize = v_ref.shape
    gain_ref[...] = jnp.zeros_like(gain_ref)
    qsize = kwt_ref.shape[0] // own
    for n, ref in enumerate((v0, v1, v2, v3)):
        at = pl.multiple_of(scalars[n] * vlocal, vlocal)
        for h in range(own):
            v_ref[h, :, pl.ds(at, vlocal)] = ref[h, :rows]
            tail = ref[h, rows:].astype(F32)
            gain_ref[h : h + 1, pl.ds(at, vlocal)] = tail[0:1] + tail[1:2] + tail[2:3]
    lane = lax.broadcasted_iota(jnp.int32, (qsize, LANES), 1)
    core = scalars[4]
    for h, out in ((core, mine), (1 - core, other)):
        kwt = kwt_ref[pl.ds(pl.multiple_of(h * qsize, qsize), qsize), :]
        out[:, :vsize] = jnp.dot(kwt, v_ref[h], preferred_element_type=F32).astype(BF16)
        extra = jnp.where(lane == 0, jnp.sum(kwt.astype(F32), axis=1, keepdims=True), 0.0)
        top, total = of_head(h, mark_ref[0:1, :]), of_head(h, mark_ref[1:2, :])
        out[:, vsize:] = marked(extra, top, total).astype(BF16)


def summary(index, core, kwt, mark, pieces):
    own, _, vlocal = pieces[0].shape
    rows = kwt.shape[1]
    vsize = vlocal * len(pieces)
    whole = lambda shape: pl.BlockSpec(shape, lambda j, s: (0,) * len(shape))
    shapes = [((kwt.shape[0] // own, vsize + LANES), BF16)] * 2
    shapes += [((own, rows, vsize), BF16), ((8, vsize), F32)]
    return pl.pallas_call(
        summary_kernel,
        grid_spec=pltpu.PrefetchScalarGridSpec(
            num_scalar_prefetch=1,
            grid=(1,),
            in_specs=[whole(kwt.shape), whole(mark.shape)] + [whole(x.shape) for x in pieces],
            out_specs=[whole(shape) for shape, _ in shapes],
        ),
        out_shape=[jax.ShapeDtypeStruct(shape, dtype) for shape, dtype in shapes],
        compiler_params=params(32),
        cost_estimate=cost(2 * kwt.size * vsize, 3 * own * rows * vsize * 2),
    )(jnp.stack(list(index) + [core]), kwt, mark, *pieces)


def pair_kernel(scalars, mine, got, out):
    first = scalars[0] == 0
    body = mine.shape[1] - LANES
    a, b = mine[:, body:].astype(F32), got[:, body:].astype(F32)
    early, late = jnp.where(first, a, b), jnp.where(first, b, a)
    (etop, etotal), (ltop, ltotal) = marks_of(early), marks_of(late)
    top = jnp.maximum(etop + ltotal, ltop)
    fe, fl = jnp.exp(etop + ltotal - top), jnp.exp(ltop - top)
    fa, fb = jnp.where(first, fe, fl), jnp.where(first, fl, fe)
    state = fa * mine[:, :body].astype(F32) + fb * got[:, :body].astype(F32)
    out[:, :body] = state.astype(BF16)
    out[:, body:] = marked(fa * a + fb * b, top, etotal + ltotal).astype(BF16)


def pair(core, mine, got):
    vmem = pl.BlockSpec(memory_space=pltpu.VMEM)
    return pl.pallas_call(
        pair_kernel,
        in_specs=[pl.BlockSpec(memory_space=pltpu.SMEM), vmem, vmem],
        out_specs=vmem,
        out_shape=jax.ShapeDtypeStruct(mine.shape, BF16),
        compiler_params=params(32),
        cost_estimate=cost(4 * mine.size, 6 * mine.size),
    )(jnp.stack([core]), mine, got)


def unpair_kernel(scalars, prefix, mine, got, keep, send):
    first = scalars[0] == 0
    body = mine.shape[1] - LANES
    p = prefix[:, body:].astype(F32)
    s = jnp.where(first, mine[:, body:].astype(F32), got[:, body:].astype(F32))
    ptop, _ = marks_of(p)
    stop, stotal = marks_of(s)
    top = jnp.maximum(ptop + stotal, stop)
    fp, fs = jnp.exp(ptop + stotal - top), jnp.exp(stop - top)
    state = jnp.where(first, mine[:, :body], got[:, :body]).astype(F32)
    state = (fp * prefix[:, :body].astype(F32) + fs * state).astype(BF16)
    extra = marked(fp * p + fs * s, top, None).astype(BF16)
    keep[:, :body] = jnp.where(first, prefix[:, :body], state)
    send[:, :body] = jnp.where(first, state, prefix[:, :body])
    keep[:, body:] = jnp.where(first, prefix[:, body:], extra)
    send[:, body:] = jnp.where(first, extra, prefix[:, body:])


def unpair(core, prefix, mine, got):
    vmem = pl.BlockSpec(memory_space=pltpu.VMEM)
    return pl.pallas_call(
        unpair_kernel,
        in_specs=[pl.BlockSpec(memory_space=pltpu.SMEM)] + [vmem] * 3,
        out_specs=[vmem] * 2,
        out_shape=[jax.ShapeDtypeStruct(mine.shape, BF16)] * 2,
        compiler_params=params(32),
        cost_estimate=cost(4 * mine.size, 10 * mine.size),
    )(jnp.stack([core]), prefix, mine, got)


def inside_kernel(p_ref, v_ref, out_ref):
    for h in range(p_ref.shape[0]):
        out_ref[h] = jnp.dot(p_ref[h], v_ref[h], preferred_element_type=F32)


def inside(p, v):
    return pl.pallas_call(
        inside_kernel,
        out_shape=jax.ShapeDtypeStruct(v.shape, F32),
        compiler_params=params(32),
        cost_estimate=cost(2 * p.size * v.shape[2], 6 * v.size),
    )(p, v)


def prefix_kernel(got_ref, out_ref):
    blocks, cut, width = got_ref.shape
    body = width - LANES
    lane = lax.broadcasted_iota(jnp.int32, (cut, LANES), 1)
    source = lax.broadcasted_iota(jnp.int32, (LANES, 2 * LANES), 0)
    target = lax.broadcasted_iota(jnp.int32, (LANES, 2 * LANES), 1)
    first = jnp.where(target < LANES, 1, 4)
    spread = ((source >= first) & (source < first + 3)).astype(F32).astype(BF16)
    marks = jnp.dot(
        got_ref[:, :, body:].reshape(blocks * cut, LANES), spread, preferred_element_type=F32
    )
    state = [jnp.zeros((cut, LANES), F32) for _ in range(width // LANES)]
    ptop = jnp.full((cut, LANES), NEVER, F32)
    for b in range(blocks):
        held = state[-1]
        for n, x in enumerate(parts_of(ptop)):
            held = jnp.where(lane == 1 + n, x, held)
        for n, x in enumerate(state[:-1] + [held]):
            out_ref[b, :, n * LANES : (n + 1) * LANES] = x.astype(BF16)
        if b == blocks - 1:
            break
        top = marks[b * cut : (b + 1) * cut, :LANES]
        total = marks[b * cut : (b + 1) * cut, LANES:]
        new = jnp.maximum(ptop + total, top)
        keep = jnp.exp(ptop + total - new)
        add = jnp.exp(top - new)
        state = [
            keep * x + add * got_ref[b, :, n * LANES : (n + 1) * LANES].astype(F32)
            for n, x in enumerate(state)
        ]
        ptop = new


def prefixes(got):
    return pl.pallas_call(
        prefix_kernel,
        out_shape=jax.ShapeDtypeStruct(got.shape, BF16),
        compiler_params=params(32),
        cost_estimate=cost(4 * got.size, 4 * got.size),
    )(got)


def finish_kernel(scalars, q_ref, mine, got, numer_ref, stat_ref, gain_ref, upper, lower):
    own, rows, vsize = numer_ref.shape
    qsize = q_ref.shape[1] // own
    core = scalars[0]
    for h, prefix_ref in ((core, mine), (1 - core, got)):
        q = q_ref[:, pl.ds(pl.multiple_of(h * qsize, qsize), qsize)]
        inter = jnp.dot(q, prefix_ref[...], preferred_element_type=F32)
        ptop, _ = marks_of(prefix_ref[0:16, vsize:].astype(F32)[0:1])
        high = of_head(h, stat_ref[...])
        top = jnp.maximum(high, ptop)
        fade = jnp.exp(high - top)
        decay = jnp.exp(ptop - top) * qsize ** (-0.5)
        denom = of_head(h, stat_ref[:, own : 2 * own])
        denom = denom * fade + inter[:, vsize : vsize + 1] * decay
        share = 1.0 / jnp.maximum(jnp.abs(denom), 1.0)
        hidden = numer_ref[h] * (fade * share) + inter[:, :vsize] * (decay * share)
        mean = jnp.mean(hidden, axis=1, keepdims=True)
        msq = jnp.mean(hidden * hidden, axis=1, keepdims=True)
        gain = gain_ref[pl.ds(h, 1), :]
        normed = (hidden - mean) * lax.rsqrt(msq - mean * mean + 1e-06) * gain
        normed = normed.astype(BF16)
        columns = pl.ds(pl.multiple_of(h * vsize, vsize), vsize)
        upper[:, columns] = normed[: rows // 2]
        lower[:, columns] = normed[rows // 2 :]


def finish(core, q, mine, got, numer, stat, gain):
    own, rows, vsize = numer.shape
    vmem = pl.BlockSpec(memory_space=pltpu.VMEM)
    return pl.pallas_call(
        finish_kernel,
        in_specs=[pl.BlockSpec(memory_space=pltpu.SMEM)] + [vmem] * 6,
        out_specs=[vmem] * 2,
        out_shape=[jax.ShapeDtypeStruct((rows // 2, own * vsize), BF16)] * 2,
        compiler_params=params(32),
        cost_estimate=cost(2 * q.size * vsize, 8 * numer.size),
    )(jnp.stack([core]), q, mine, got, numer, stat, gain)


def per_device(tokens, w_query, w_key, w_value, w_gate, gate_bias, norm_gain, w_out):
    me = lax.axis_index("val")
    nval = lax.axis_size("val")
    place = lax.axis_index("seq")
    blocks = lax.axis_size("seq")
    rows, chunk = tokens.shape
    width = w_query.shape[0]
    heads, vlocal = w_value.shape[1:]
    own = heads // nval
    qsize = w_query.shape[1] // own
    vsize = vlocal * nval
    index = [(me + d) % nval for d in (0, nval - 1, 1, 2)]

    half = rows // 2
    upper, lower = moved([tokens], [[(0, 0, half)], [(0, half, half)]], [])
    ring = Ring(upper, lower, [upper, lower])
    wg = w_gate.transpose(1, 2, 0).reshape(2 * heads, width)
    wv, early = flat(w_value, 0, 2)
    ring.second([early])
    wv, late = flat(w_value, 2, 2, wv)
    ring.forward([late])
    wv, _ = flat(w_value, 4, 4, wv)
    groups = [(tokens,), ring.left, ring.right]
    acc = product(rows, groups, index[:3], [wv], [F32])[0]
    core = place % 2
    cores = [(i, i ^ 1) for i in range(blocks)]
    local = w_out.reshape(heads * vlocal, -1)
    *pieces, mark = cut_by_device(local, me, core, nval, [acc])
    values = values_by_device(ring.opposite, index[3], me, wv, acc, norm_gain, own, mark)
    pieces = tied(pieces, values[:1])
    halves = exchanged([None, *pieces])[1:]
    groups.append(ring.opposite)
    q, k = product(rows, groups, index, [w_query, w_key], [BF16] * 2, values[:1])

    values = exchanged(values)
    kwt, p, stat, mark = within(groups, index, wg, gate_bias, q, k, own)
    mine, other, v, gain = summary(index, core, kwt, mark, values)
    got = lax.ppermute(other, "seq", cores)
    chips = [list(range(n, blocks, 2)) for n in range(2)]
    sliced = (blocks // 2, -1, vsize + LANES)
    both = pair(core, mine, got).reshape(sliced)
    both = lax.all_to_all(both, "seq", 0, 0, axis_index_groups=chips)
    numer = inside(p, v)
    prefix = lax.all_to_all(prefixes(both), "seq", 0, 0, axis_index_groups=chips)
    keep, send = unpair(core, prefix.reshape(mine.shape), mine, got)
    came = lax.ppermute(send, "seq", cores)
    upper, lower = finish(core, q, keep, came, numer, stat, gain)

    ring = Ring(upper, lower, [upper, lower])
    halves = tied(halves, [upper])
    others = [lax.ppermute(x, "seq", cores) for x in halves]
    *others, there = tied(others, [], with_mark=True)
    ring.second([there])
    ring.forward()
    groups = [ring.own, ring.left, ring.right]
    weights = (index, core, local, halves, others)
    acc = out_product(rows, groups, index[:3], *weights, None, F32)
    return out_product(rows, [ring.opposite], index[3:], *weights, acc, BF16)


def solution(mesh):
    placed = (
        P("seq", "val"),
        P(None, "val"),
        P(None, "val"),
        P(None, None, "val"),
        P(),
        P(),
        P(None, "val"),
        P(None, "val", None),
    )
    return jax.shard_map(
        per_device, mesh=mesh, in_specs=placed, out_specs=P("seq", "val"), check_vma=False
    )
```
